32 devices in a mesh: dp: 8 (over z, y), tensor: 4 (over x, core).
Axes of the slice: x: 2, y: 2, z: 4, core: 2. Of those that a mesh axis runs over, the one named last changes fastest.
Arguments:
- tokens: bfloat16 [1024, 768], P(('dp', 'tensor')), may hold values from -6 to 6
- cotangent: bfloat16 [1024, 768], P(('dp', 'tensor')), may hold values from -6 to 6
- segments: int32 [1024], replicated, may hold values from 0 to 4, never falling along the last dimension, each value on 1 to 384 neighbouring positions
- w_qkv: bfloat16 [2, 768, 3, 768], P(None, None, None, 'tensor'), may hold values from -0.21875 to 0.21875
- qv_bias: float32 [2, 2, 768], P(None, None, 'tensor'), may hold values from -3 to 3
- w_out: bfloat16 [2, 768, 768], P(None, 'tensor'), may hold values from -0.875 to 0.875
- w_up: bfloat16 [2, 768, 3072], P(None, None, 'tensor'), may hold values from -0.21875 to 0.21875
- w_down: bfloat16 [2, 3072, 768], P(None, 'tensor'), may hold values from -0.109375 to 0.109375
- ff_bias: float32 [2, 3072], P(None, 'tensor'), may hold values from -3 to 3
- gains: float32 [2, 2, 768], replicated, may hold values from 0.25 to 1.75
- biases: float32 [2, 4, 768], replicated, may hold values from -2 to 2
Outputs:
- result: bfloat16 [1024, 768], P(('dp', 'tensor'))
- input_grad: bfloat16 [1024, 768], P(('dp', 'tensor'))
- w_qkv_grad: float32 [2, 768, 3, 768], P(None, 'dp', None, 'tensor')
- w_out_grad: float32 [2, 768, 768], P(None, 'tensor', 'dp')
- w_up_grad: float32 [2, 768, 3072], P(None, 'dp', 'tensor')
- w_down_grad: float32 [2, 3072, 768], P(None, 'tensor', 'dp')
- gains_grad: float32 [2, 2, 768], replicated
- biases_grad: float32 [2, 4, 768], replicated
- qv_bias_grad: float32 [2, 2, 768], replicated
- ff_bias_grad: float32 [2, 3072], replicated
The draws below stay inside these ranges and needn't reach their ends.
Inputs may be any that keep to these rules, and one draw needn't show every extreme that they name: `segments`: the document numbers never fall along the stream; each document has 1 to 384 tokens and some document has exactly 384.
All inputs are finite; a program needn't handle non-finite values.
Results may differ from the reference program's by a relative error of at most 0.025.
Values may be sent and summed in bfloat16 or wider, within the bound.
No kernel may reach another device: no remote copies, remote signals or barrier semaphores. Data moves between devices by JAX's collectives and lax.ppermute only.
A program may use at most 128 MiB of HBM per device.

```python
import math
import jax
import jax.numpy as jnp
import numpy as np
from jax import lax

D = 768
HEADS = 12
HD = 64
FF = 3072
TOK_DEV = 128
LAYERS = 2
SPAN = 4
MOST = 384
TOKENS = 1024
SEG_COUNT = 5


def level_of(rng, extent, cuts, smallest, largest):
    def one(position, parts):
        heights = jax.random.uniform(jax.random.fold_in(jax.random.fold_in(rng, 6), position), (parts,), jnp.float32, smallest / len(cuts), largest / len(cuts))
        return jnp.repeat(jnp.exp(heights), extent[position] // parts).reshape((-1,) + (1,) * (len(extent) - position - 1))

    level = one(*cuts[0])
    for cut in cuts[1:]:
        level = level * one(*cut)
    return level


def length_profile(amount, total, most, skew):
    portions = [(1 << 20) // math.isqrt(standing ** skew) + 1 for standing in range(2, amount + 1)]
    surplus, counts = total - most - (amount - 1), [1] * (amount - 1)
    while surplus > 0:
        free = [i for i in range(amount - 1) if counts[i] < most]
        mass, remaining = sum([portions[i] for i in free]), surplus
        for i in free:
            extra = min(most - counts[i], max(1, remaining * portions[i] // mass), surplus)
            counts[i] = counts[i] + extra
            surplus = surplus - extra
    return np.array([most] + counts)


def uneven_parts(key, amount, total, limit, skew):
    if amount == 2:
        one = jax.random.randint(key, (), max(1, total - limit), min(limit, total - 1) + 1)
        return jnp.stack([one, total - one])
    tallies = jnp.asarray(length_profile(amount, total, limit, skew), jnp.int32)
    couples = (amount - 1) // 2
    donor, taker = tallies[1:1 + 2 * couples:2], tallies[2:2 + 2 * couples:2]
    slack = jnp.minimum(donor - 1, limit - taker)
    passed = jax.random.randint(jax.random.fold_in(key, 1), (couples,), 0, 1 << 20) % (slack + 1)
    tallies = tallies.at[1:1 + 2 * couples:2].set(donor - passed).at[2:2 + 2 * couples:2].set(taker + passed)
    return tallies[jax.random.permutation(jax.random.fold_in(key, 2), amount)]


def normal_values(key, extent, spread, reach, split=(), kind=jnp.bfloat16):
    values = spread * jax.random.normal(key, extent, jnp.float32)
    if split:
        values = values * level_of(key, extent, split, -0.22, 0.18)
    return jnp.clip(values, -reach, reach).astype(kind)


def setup_inputs(seed: int = 0) -> dict:
    keys = jax.random.split(jax.random.key(seed), 12)
    return {
        "tokens": normal_values(keys[0], (TOKENS, D), 1.0, 6.0, ((0, 32),)),
        "cotangent": normal_values(keys[1], (TOKENS, D), 1.0, 6.0, ((0, 32),)),
        "segments": jnp.searchsorted(jnp.cumsum(uneven_parts(keys[2], SEG_COUNT, TOKENS, MOST, 0)), jnp.arange(TOKENS), side="right").astype(jnp.int32),
        "w_qkv": normal_values(keys[3], (LAYERS, D, 3, D), D ** -0.5, 0.21875, ((3, 4),)),
        "qv_bias": normal_values(keys[4], (LAYERS, 2, D), 0.5, 3.0, ((2, 4),), jnp.float32),
        "w_out": normal_values(keys[5], (LAYERS, D, D), (max(D // 16, 1)) ** -0.5, 0.875, ((1, 4),)),
        "w_up": normal_values(keys[6], (LAYERS, D, FF), D ** -0.5, 0.21875, ((2, 4),)),
        "w_down": normal_values(keys[7], (LAYERS, FF, D), FF ** -0.5, 0.109375, ((1, 4),)),
        "ff_bias": normal_values(keys[8], (LAYERS, FF), 0.5, 3.0, ((1, 4),), jnp.float32),
        "gains": jnp.clip(1.0 + 0.15 * jax.random.normal(keys[9], (LAYERS, 2, D), jnp.float32), 0.25, 1.75),
        "biases": normal_values(keys[10], (LAYERS, 4, D), 0.3, 2.0, (), jnp.float32),
    }


epsilon = 1e-05
gelu_c = 0.7978845608028654

def norm_fwd(values_in, gain, shift_bias):
    mean_v = lax.optimization_barrier(jnp.mean(values_in, axis=-1, keepdims=True))
    centred = values_in - mean_v
    var_v = lax.optimization_barrier(jnp.mean(centred * centred, axis=-1, keepdims=True))
    rstd = lax.rsqrt(var_v + epsilon)
    normed = centred * rstd
    return (normed * gain + shift_bias, normed, rstd)

def norm_bwd(grad_in, normed, rstd, gain):
    scaled = grad_in * gain
    inner = lax.optimization_barrier(jnp.mean(scaled, axis=-1, keepdims=True))
    along = lax.optimization_barrier(jnp.mean(scaled * normed, axis=-1, keepdims=True))
    return rstd * (scaled - inner - normed * along)

def gelu_pair(pre_act):
    inner = gelu_c * (pre_act + 0.044715 * pre_act * pre_act * pre_act)
    tanh_v = jnp.tanh(inner)
    value_out = 0.5 * pre_act * (1.0 + tanh_v)
    slope = 0.5 * (1.0 + tanh_v) + 0.5 * pre_act * (1.0 - tanh_v * tanh_v) * gelu_c * (1.0 + 3.0 * 0.044715 * pre_act * pre_act)
    return (value_out, slope)

def head_scores(queries, keys_all, allowed):
    scaled = jnp.einsum('qhd,khd->hqk', queries.astype(jnp.float32), keys_all.astype(jnp.float32)) * HD ** (-0.5)
    return jnp.where(allowed[None], scaled, -1e+30)

def attend_forward(queries, keys_all, values_all, allowed):
    scores = head_scores(queries, keys_all, allowed)
    row_max = lax.optimization_barrier(jnp.max(scores, axis=-1, keepdims=True))
    row_total = lax.optimization_barrier(jnp.sum(jnp.exp(scores - row_max), axis=-1, keepdims=True))
    log_total = row_max + jnp.log(row_total)
    weights_b = jnp.exp(scores - log_total).astype(jnp.bfloat16)
    mixed = jnp.einsum('hqk,khd->qhd', weights_b.astype(jnp.float32), values_all.astype(jnp.float32))
    return (mixed.astype(jnp.bfloat16), log_total)

def attend_backward(queries, keys_all, values_all, attended, d_att, log_total, allowed):
    scores = head_scores(queries, keys_all, allowed)
    probs = jnp.exp(scores - log_total)
    d_att32 = d_att.astype(jnp.float32)
    delta = lax.optimization_barrier(jnp.sum(d_att32 * attended.astype(jnp.float32), axis=-1)).T[:, :, None]
    d_prob = jnp.einsum('qhd,khd->hqk', d_att32, values_all.astype(jnp.float32))
    d_score = (probs * (d_prob - delta) * HD ** (-0.5)).astype(jnp.bfloat16).astype(jnp.float32)
    d_query = jnp.einsum('hqk,khd->qhd', d_score, keys_all.astype(jnp.float32))
    d_keys = jnp.einsum('hqk,qhd->khd', d_score, queries.astype(jnp.float32))
    probs_b = probs.astype(jnp.bfloat16).astype(jnp.float32)
    d_values = jnp.einsum('hqk,qhd->khd', probs_b, d_att32)
    return (d_query, d_keys, d_values)

def reference(tokens, cotangent, segments, w_qkv, qv_bias, w_out, w_up, w_down, ff_bias, gains, biases):
    f32 = jnp.float32
    bf16 = jnp.bfloat16
    token_count = tokens.shape[0]
    model_width = tokens.shape[1]
    pad_rows = (SPAN - 1) * TOK_DEV
    window = SPAN * TOK_DEV
    block_count = token_count // TOK_DEV
    block_ids = jnp.arange(block_count, dtype=jnp.int32)
    seg_padded = jnp.concatenate([jnp.full((pad_rows,), -1, dtype=jnp.int32), segments.astype(jnp.int32)])
    local_rows = jnp.arange(TOK_DEV, dtype=jnp.int32)
    window_rows = jnp.arange(window, dtype=jnp.int32)

    def mask_of(block_no):
        first = (block_no * TOK_DEV).astype(jnp.int32)
        query_pos = first + local_rows
        key_pos = first - pad_rows + window_rows
        query_seg = lax.dynamic_slice_in_dim(seg_padded, first + pad_rows, TOK_DEV)
        key_seg = lax.dynamic_slice_in_dim(seg_padded, first, window)
        return (key_pos[None, :] <= query_pos[:, None]) & (key_seg[None, :] == query_seg[:, None])

    def pad_heads(matrix):
        padded = jnp.concatenate([jnp.zeros((pad_rows, model_width), dtype=matrix.dtype), matrix])
        return padded.reshape(-1, HEADS, HD)

    def block_heads(matrix):
        return matrix.reshape(block_count, TOK_DEV, HEADS, HD)
    hidden = tokens.astype(f32)
    caches = []
    for layer_no in range(LAYERS):
        normed1, hat1, rstd1 = norm_fwd(hidden, gains[layer_no, 0], biases[layer_no, 0])
        act1 = normed1.astype(bf16)
        projected = jnp.dot(act1, w_qkv[layer_no].reshape(model_width, 3 * model_width), preferred_element_type=f32).reshape(token_count, 3, model_width)
        queries = (projected[:, 0] + qv_bias[layer_no, 0]).astype(bf16)
        keys_own = projected[:, 1].astype(bf16)
        values_own = (projected[:, 2] + qv_bias[layer_no, 1]).astype(bf16)
        query_blocks = block_heads(queries)
        keys_pad = pad_heads(keys_own)
        values_pad = pad_heads(values_own)

        def forward_one(block_no):
            first = (block_no * TOK_DEV).astype(jnp.int32)
            key_win = lax.dynamic_slice_in_dim(keys_pad, first, window)
            value_win = lax.dynamic_slice_in_dim(values_pad, first, window)
            return attend_forward(query_blocks[block_no], key_win, value_win, mask_of(block_no))
        attended, log_total = lax.map(forward_one, block_ids)
        attended = attended.reshape(token_count, model_width)
        mid = hidden + jnp.dot(attended, w_out[layer_no], preferred_element_type=f32) + biases[layer_no, 1]
        normed2, hat2, rstd2 = norm_fwd(mid, gains[layer_no, 1], biases[layer_no, 2])
        act2 = normed2.astype(bf16)
        pre_act = jnp.dot(act2, w_up[layer_no], preferred_element_type=f32) + ff_bias[layer_no]
        gelu_v, slope = gelu_pair(pre_act)
        act3 = gelu_v.astype(bf16)
        caches.append((hat1, rstd1, act1, queries, keys_own, values_own, attended, log_total, hat2, rstd2, act2, slope, act3))
        hidden = mid + jnp.dot(act3, w_down[layer_no], preferred_element_type=f32) + biases[layer_no, 3]
    result = hidden.astype(bf16)
    grad_now = cotangent.astype(f32)
    qkv_list, out_list, up_list, down_list, gain_list, bias_list, qvb_list, ffb_list = ([], [], [], [], [], [], [], [])
    for layer_no in range(LAYERS - 1, -1, -1):
        hat1, rstd1, act1, queries, keys_own, values_own, attended, log_total, hat2, rstd2, act2, slope, act3 = caches[layer_no]
        g_bdown = lax.optimization_barrier(jnp.sum(grad_now, axis=0))
        out_b = grad_now.astype(bf16)
        g_wdown = jnp.dot(act3.T, out_b, preferred_element_type=f32)
        d_pre = jnp.dot(out_b, w_down[layer_no].T, preferred_element_type=f32) * slope
        g_ffb = lax.optimization_barrier(jnp.sum(d_pre, axis=0))
        pre_b = d_pre.astype(bf16)
        g_wup = jnp.dot(act2.T, pre_b, preferred_element_type=f32)
        d_norm2 = jnp.dot(pre_b, w_up[layer_no].T, preferred_element_type=f32)
        g_gain2 = lax.optimization_barrier(jnp.sum(d_norm2 * hat2, axis=0))
        g_bias2 = lax.optimization_barrier(jnp.sum(d_norm2, axis=0))
        grad_mid = grad_now + norm_bwd(d_norm2, hat2, rstd2, gains[layer_no, 1])
        g_bout = lax.optimization_barrier(jnp.sum(grad_mid, axis=0))
        mid_b = grad_mid.astype(bf16)
        g_wout = jnp.dot(attended.T, mid_b, preferred_element_type=f32)
        d_att = jnp.dot(mid_b, w_out[layer_no].T, preferred_element_type=f32).astype(bf16)
        query_blocks = block_heads(queries)
        att_blocks = block_heads(attended)
        datt_blocks = block_heads(d_att)
        keys_pad = pad_heads(keys_own)
        values_pad = pad_heads(values_own)

        def backward_one(carry, block_no):
            keys_acc, values_acc = carry
            first = (block_no * TOK_DEV).astype(jnp.int32)
            key_win = lax.dynamic_slice_in_dim(keys_pad, first, window)
            value_win = lax.dynamic_slice_in_dim(values_pad, first, window)
            d_q, d_k, d_v = attend_backward(query_blocks[block_no], key_win, value_win, att_blocks[block_no], datt_blocks[block_no], log_total[block_no], mask_of(block_no))
            keys_acc = lax.dynamic_update_slice_in_dim(keys_acc, lax.dynamic_slice_in_dim(keys_acc, first, window) + d_k, first, 0)
            values_acc = lax.dynamic_update_slice_in_dim(values_acc, lax.dynamic_slice_in_dim(values_acc, first, window) + d_v, first, 0)
            return ((keys_acc, values_acc), d_q)
        zero_acc = jnp.zeros((pad_rows + token_count, HEADS, HD), dtype=f32)
        (keys_acc, values_acc), d_query = lax.scan(backward_one, (zero_acc, zero_acc), block_ids)
        d_query = d_query.reshape(token_count, model_width)
        d_keys = keys_acc[pad_rows:].reshape(token_count, model_width)
        d_values = values_acc[pad_rows:].reshape(token_count, model_width)
        g_qb = lax.optimization_barrier(jnp.sum(d_query, axis=0))
        g_vb = lax.optimization_barrier(jnp.sum(d_values, axis=0))
        d_proj = jnp.stack([d_query, d_keys, d_values], axis=1).astype(bf16).reshape(token_count, 3 * model_width)
        g_wqkv = jnp.dot(act1.T, d_proj, preferred_element_type=f32).reshape(model_width, 3, model_width)
        d_norm1 = jnp.dot(d_proj, w_qkv[layer_no].reshape(model_width, 3 * model_width).T, preferred_element_type=f32)
        g_gain1 = lax.optimization_barrier(jnp.sum(d_norm1 * hat1, axis=0))
        g_bias1 = lax.optimization_barrier(jnp.sum(d_norm1, axis=0))
        grad_now = grad_mid + norm_bwd(d_norm1, hat1, rstd1, gains[layer_no, 0])
        qkv_list.insert(0, g_wqkv)
        out_list.insert(0, g_wout)
        up_list.insert(0, g_wup)
        down_list.insert(0, g_wdown)
        gain_list.insert(0, jnp.stack([g_gain1, g_gain2]))
        bias_list.insert(0, jnp.stack([g_bias1, g_bout, g_bias2, g_bdown]))
        qvb_list.insert(0, jnp.stack([g_qb, g_vb]))
        ffb_list.insert(0, g_ffb)
    return (result, grad_now.astype(bf16), jnp.stack(qkv_list), jnp.stack(out_list), jnp.stack(up_list), jnp.stack(down_list), jnp.stack(gain_list), jnp.stack(bias_list), jnp.stack(qvb_list), jnp.stack(ffb_list))
```

```python
import jax
import jax.numpy as jnp
from jax import lax
from jax.sharding import PartitionSpec as P

D = 768
HD = 64
FF = 3072
LAYERS = 2
SPAN = 4


epsilon = 1e-05
gelu_c = 0.7978845608028654
f32 = jnp.float32
bf16 = jnp.bfloat16


def shifted(array, axis, by):
    length = lax.axis_size(axis)
    pairs = [(i, i + by) for i in range(length) if 0 <= i + by < length]
    return lax.ppermute(array, axis, pairs)


def swapped(array, axis, bit):
    length = lax.axis_size(axis)
    return lax.ppermute(array, axis, [(i, i ^ bit) for i in range(length)])


def bits_of(axis):
    length = lax.axis_size(axis)
    found, bit = [], 1
    while bit < length:
        found.append(bit)
        bit *= 2
    assert bit == length
    return found


def norm_fwd(values_in, gain, shift_bias):
    mean_v = jnp.mean(values_in, axis=-1, keepdims=True)
    centred = values_in - mean_v
    var_v = jnp.mean(centred * centred, axis=-1, keepdims=True)
    rstd = lax.rsqrt(var_v + epsilon)
    normed = centred * rstd
    return (normed * gain + shift_bias, normed, rstd)


def norm_bwd(grad_in, normed, rstd, gain):
    scaled = grad_in * gain
    inner = jnp.mean(scaled, axis=-1, keepdims=True)
    along = jnp.mean(scaled * normed, axis=-1, keepdims=True)
    return rstd * (scaled - inner - normed * along)


def gelu_pair(pre_act):
    inner = gelu_c * (pre_act + 0.044715 * pre_act * pre_act * pre_act)
    tanh_v = jnp.tanh(inner)
    value_out = 0.5 * pre_act * (1.0 + tanh_v)
    slope = 0.5 * (1.0 + tanh_v) + 0.5 * pre_act * (1.0 - tanh_v * tanh_v) * gelu_c * (
        1.0 + 3.0 * 0.044715 * pre_act * pre_act
    )
    return (value_out, slope)


def build_mask(segments, tok_rows):
    dev_index = lax.axis_index("dp")
    row_ids = jnp.arange(tok_rows, dtype=jnp.int32)
    query_pos = dev_index * tok_rows + row_ids
    query_seg = lax.dynamic_slice_in_dim(segments, dev_index * tok_rows, tok_rows)
    key_pos = []
    key_seg = []
    for offset in range(SPAN):
        key_start = (dev_index - (SPAN - 1 - offset)) * tok_rows
        key_pos.append(key_start + row_ids)
        key_seg.append(lax.dynamic_slice_in_dim(segments, jnp.maximum(key_start, 0), tok_rows))
    key_pos = jnp.concatenate(key_pos)
    key_seg = jnp.concatenate(key_seg)
    return (
        (key_pos[None, :] <= query_pos[:, None])
        & (key_pos[None, :] >= 0)
        & (key_seg[None, :] == query_seg[:, None])
    )


def gather_rows(rows):
    bits = bits_of("tensor")
    mine = lax.axis_index("tensor")
    for place, bit in enumerate(bits[::-1]):
        other = swapped(rows, "tensor", bit)
        high = (mine & bit) != 0
        pair = [jnp.where(high, other, rows), jnp.where(high, rows, other)]
        rows = jnp.stack(pair, axis=place)
    return rows.reshape(-1, rows.shape[-1])


def tensor_sum(part):
    bits = bits_of("tensor")
    high = (lax.axis_index("tensor") & 1) != 0
    half = part.shape[0] // 2
    low_half, high_half = part[:half], part[half:]
    keep = jnp.where(high, high_half, low_half)
    give = jnp.where(high, low_half, high_half).astype(bf16)
    total = keep + swapped(give, "tensor", 1).astype(f32)
    for bit in bits[1:]:
        rounded = total.astype(bf16)
        total = rounded.astype(f32) + swapped(rounded, "tensor", bit).astype(f32)
    rounded = total.astype(bf16)
    other = swapped(rounded, "tensor", 1)
    return jnp.concatenate(
        [jnp.where(high, other, rounded), jnp.where(high, rounded, other)]
    ).astype(f32)


def dp_halving(pairs):
    bits = bits_of("dp")
    mine = lax.axis_index("dp")
    count = lax.axis_size("dp")

    def pick(array, axis, bit, own):
        at = jnp.where(((mine & bit) != 0) == own, 1, 0)
        return lax.dynamic_index_in_dim(array, at, axis, keepdims=False)

    def products(own):
        parts = []
        for left, right in pairs:
            rows, width = left.shape
            split = left.reshape(rows, count // 2, 2, width // count)
            chosen = pick(split, 2, 1, own).reshape(rows, width // 2)
            parts.append(
                lax.dot_general(
                    chosen, right, (((0,), (0,)), ((), ())), preferred_element_type=f32
                )
            )
        return jnp.concatenate(parts, axis=1)

    incoming = swapped(products(False).astype(bf16), "dp", bits[0])
    total = products(True) + incoming.astype(f32)
    wide = total.shape[1]
    block = total.shape[0] // (count // 2)
    blocks = count // 2
    for bit in bits[1:]:
        split = total.reshape(blocks // 2, 2, block, wide)
        incoming = swapped(pick(split, 1, bit, False).astype(bf16), "dp", bit)
        total = pick(split, 1, bit, True) + incoming.astype(f32)
        blocks //= 2
    return total.reshape(block, wide)


def fetch_keys(packed):
    pieces = []
    for distance in range(1, SPAN):
        pieces.append(shifted(packed, "dp", distance))
    ordered = pieces[::-1] + [packed]
    return jnp.concatenate(ordered, axis=0)


def return_keys(grads_all, tok_rows):
    blocks = [grads_all[offset * tok_rows : (offset + 1) * tok_rows] for offset in range(SPAN)]
    summed = blocks[SPAN - 1]
    for distance in range(1, SPAN):
        given = blocks[SPAN - 1 - distance].astype(bf16)
        summed = summed + shifted(given, "dp", -distance).astype(f32)
    return summed


def score_block(queries, keys_all, key_mask):
    scaled = jnp.einsum(
        "qhd,khd->hqk", queries, keys_all, preferred_element_type=f32
    ) * HD ** (-0.5)
    return jnp.where(key_mask[None], scaled, -1e30)


def layer_forward(hidden, layer_no, params, key_mask):
    w_qkv, qv_bias, w_out, w_up, w_down, ff_bias, gains, biases = params
    local_width = w_out.shape[1]
    head_count = local_width // HD
    normed1, hat1, rstd1 = norm_fwd(hidden, gains[layer_no, 0], biases[layer_no, 0])
    act1 = normed1.astype(bf16)
    tok_rows = act1.shape[0]

    def project(member):
        return jnp.dot(act1, w_qkv[layer_no, :, member], preferred_element_type=f32)

    keys_own = project(1).astype(bf16)
    values_own = (project(2) + qv_bias[layer_no, 1]).astype(bf16)
    key_values = fetch_keys(jnp.concatenate([keys_own, values_own], axis=1))
    queries = (project(0) + qv_bias[layer_no, 0]).astype(bf16)
    queries = queries.reshape(tok_rows, head_count, HD)
    keys_all = key_values[:, :local_width].reshape(-1, head_count, HD)
    values_all = key_values[:, local_width:].reshape(-1, head_count, HD)
    scores = score_block(queries, keys_all, key_mask)
    row_max = jnp.max(scores, axis=-1, keepdims=True)
    row_total = jnp.sum(jnp.exp(scores - row_max), axis=-1, keepdims=True)
    log_total = row_max + jnp.log(row_total)
    weights_b = jnp.exp(scores - log_total).astype(bf16)
    attended = (
        jnp.einsum("hqk,khd->qhd", weights_b, values_all, preferred_element_type=f32)
        .astype(bf16)
        .reshape(tok_rows, local_width)
    )
    branch_sum = tensor_sum(jnp.dot(attended, w_out[layer_no], preferred_element_type=f32))
    mid = hidden + branch_sum + biases[layer_no, 1]
    normed2, hat2, rstd2 = norm_fwd(mid, gains[layer_no, 1], biases[layer_no, 2])
    act2 = normed2.astype(bf16)
    pre_act = jnp.dot(act2, w_up[layer_no], preferred_element_type=f32) + ff_bias[layer_no]
    gelu_v, slope = gelu_pair(pre_act)
    act3 = gelu_v.astype(bf16)
    ffn_total = tensor_sum(jnp.dot(act3, w_down[layer_no], preferred_element_type=f32))
    final = mid + ffn_total + biases[layer_no, 3]
    cache = (
        hat1,
        rstd1,
        act1,
        queries,
        keys_all,
        values_all,
        attended,
        log_total,
        hat2,
        rstd2,
        act2,
        slope,
        act3,
    )
    return (final, cache)


def layer_backward(grad_now, layer_no, params, cache, key_mask):
    w_qkv, qv_bias, w_out, w_up, w_down, ff_bias, gains, biases = params
    (
        hat1,
        rstd1,
        act1,
        queries,
        keys_all,
        values_all,
        attended,
        log_total,
        hat2,
        rstd2,
        act2,
        slope,
        act3,
    ) = cache
    tok_rows = act1.shape[0]
    local_width = w_out.shape[1]
    head_count = local_width // HD
    g_bdown = jnp.sum(grad_now, axis=0)
    out_b = grad_now.astype(bf16)
    d_pre = jnp.dot(out_b, w_down[layer_no].T, preferred_element_type=f32) * slope
    g_ffb = jnp.sum(d_pre, axis=0)
    pre_b = d_pre.astype(bf16)
    d_norm2 = tensor_sum(jnp.dot(pre_b, w_up[layer_no].T, preferred_element_type=f32))
    mlp_grads = dp_halving([(act2, pre_b), (out_b, act3)])
    g_gain2 = jnp.sum(d_norm2 * hat2, axis=0)
    g_bias2 = jnp.sum(d_norm2, axis=0)
    grad_mid = grad_now + norm_bwd(d_norm2, hat2, rstd2, gains[layer_no, 1])
    g_bout = jnp.sum(grad_mid, axis=0)
    mid_b = grad_mid.astype(bf16)
    d_att = (
        jnp.dot(mid_b, w_out[layer_no].T, preferred_element_type=f32)
        .astype(bf16)
        .reshape(tok_rows, head_count, HD)
    )
    att_heads = attended.reshape(tok_rows, head_count, HD)
    delta = jnp.sum(d_att.astype(f32) * att_heads.astype(f32), axis=-1).T[:, :, None]
    scores = score_block(queries, keys_all, key_mask)
    probs = jnp.exp(scores - log_total)
    d_prob = jnp.einsum("qhd,khd->hqk", d_att, values_all, preferred_element_type=f32)
    d_score = (probs * (d_prob - delta) * HD ** (-0.5)).astype(bf16)
    d_keys = jnp.einsum("hqk,qhd->khd", d_score, queries, preferred_element_type=f32).reshape(
        -1, local_width
    )
    d_values = jnp.einsum(
        "hqk,qhd->khd", probs.astype(bf16), d_att, preferred_element_type=f32
    ).reshape(-1, local_width)
    kv_grads = return_keys(jnp.concatenate([d_keys, d_values], axis=1), tok_rows)
    d_query = jnp.einsum("hqk,khd->qhd", d_score, keys_all, preferred_element_type=f32).reshape(
        tok_rows, local_width
    )
    g_qb = jnp.sum(d_query, axis=0)
    g_vb = jnp.sum(kv_grads[:, local_width:], axis=0)
    d_proj = jnp.concatenate([d_query, kv_grads], axis=1).astype(bf16)
    d_norm1 = tensor_sum(
        sum(
            lax.dot_general(
                d_proj[:, member * local_width : (member + 1) * local_width],
                w_qkv[layer_no, :, member],
                (((1,), (1,)), ((), ())),
                preferred_element_type=f32,
            )
            for member in range(3)
        )
    )
    att_grads = dp_halving([(act1, d_proj), (mid_b, attended)])
    g_gain1 = jnp.sum(d_norm1 * hat1, axis=0)
    g_bias1 = jnp.sum(d_norm1, axis=0)
    grad_in = grad_mid + norm_bwd(d_norm1, hat1, rstd1, gains[layer_no, 0])
    small = (
        jnp.stack([g_gain1, g_gain2]),
        jnp.stack([g_bias1, g_bout, g_bias2, g_bdown]),
        jnp.stack([g_qb, g_vb]),
        g_ffb,
    )
    return (grad_in, mlp_grads, att_grads, small)


def shards(
    tokens, cotangent, segments, w_qkv, qv_bias, w_out, w_up, w_down, ff_bias, gains, biases
):
    params = (w_qkv, qv_bias, w_out, w_up, w_down, ff_bias, gains, biases)
    tensor_count = lax.axis_size("tensor")
    tensor_index = lax.axis_index("tensor")
    own_rows = tokens.shape[0]
    tok_rows = own_rows * tensor_count
    local_width = w_out.shape[1]
    local_ff = w_up.shape[2]
    key_mask = build_mask(segments, tok_rows)
    hidden = gather_rows(tokens).astype(f32)
    grad_now = gather_rows(cotangent).astype(f32)
    caches = []
    for layer_no in range(LAYERS):
        hidden, cache = layer_forward(hidden, layer_no, params, key_mask)
        caches.append(cache)

    def own(rows):
        return lax.dynamic_slice_in_dim(rows, tensor_index * own_rows, own_rows).astype(bf16)

    result = own(hidden)
    mlp_parts = [None] * LAYERS
    att_parts = [None] * LAYERS
    small_parts = [None] * LAYERS
    for layer_no in range(LAYERS - 1, -1, -1):
        grad_now, mlp_parts[layer_no], att_parts[layer_no], small_parts[layer_no] = layer_backward(
            grad_now, layer_no, params, caches[layer_no], key_mask
        )
    block = mlp_parts[0].shape[0]
    g_wqkv = jnp.stack([a[:, : 3 * local_width].reshape(block, 3, local_width) for a in att_parts])
    g_wout = jnp.stack([a[:, 3 * local_width :].T for a in att_parts])
    g_wup = jnp.stack([m[:, :local_ff] for m in mlp_parts])
    g_wdown = jnp.stack([m[:, local_ff:].T for m in mlp_parts])

    def widened(array):
        wide = jnp.zeros(array.shape[:-1] + (array.shape[-1] * tensor_count,), f32)
        start = tensor_index * array.shape[-1]
        return lax.dynamic_update_slice_in_dim(wide, array, start, array.ndim - 1)

    share = 1.0 / tensor_count
    small = [
        jnp.stack([s[0] for s in small_parts]) * share,
        jnp.stack([s[1] for s in small_parts]) * share,
        widened(jnp.stack([s[2] for s in small_parts])),
        widened(jnp.stack([s[3] for s in small_parts])),
    ]
    flat = jnp.concatenate([s.reshape(-1, D) for s in small])
    for axis in ("tensor", "dp"):
        for bit in bits_of(axis):
            flat = flat + swapped(flat, axis, bit)
    outs = []
    start = 0
    for s in small:
        rows = s.size // D
        outs.append(flat[start : start + rows].reshape(s.shape))
        start += rows
    return (result, own(grad_now), g_wqkv, g_wout, g_wup, g_wdown, *outs)


def solution(mesh):
    return jax.shard_map(
        shards,
        mesh=mesh,
        in_specs=(
            P(("dp", "tensor"), None),
            P(("dp", "tensor"), None),
            P(),
            P(None, None, None, "tensor"),
            P(None, None, "tensor"),
            P(None, "tensor", None),
            P(None, None, "tensor"),
            P(None, "tensor", None),
            P(None, "tensor"),
            P(),
            P(),
        ),
        out_specs=(
            P(("dp", "tensor"), None),
            P(("dp", "tensor"), None),
            P(None, "dp", None, "tensor"),
            P(None, "tensor", "dp"),
            P(None, "dp", "tensor"),
            P(None, "tensor", "dp"),
            P(),
            P(),
            P(),
            P(),
        ),
        check_vma=False,
    )
```

```python
import jax
import jax.numpy as jnp
from jax import lax
from jax.experimental import pallas as pl
from jax.experimental.pallas import tpu as pltpu
from jax.sharding import PartitionSpec as P

D = 768
HD = 64
FF = 3072
LAYERS = 2
SPAN = 4

epsilon = 1e-05
gelu_c = 0.7978845608028654
f32 = jnp.float32
bf16 = jnp.bfloat16
VMEM_LIMIT = 28 * 1024 * 1024


def shifted(array, axis, by):
    length = lax.axis_size(axis)
    pairs = [(i, i + by) for i in range(length) if 0 <= i + by < length]
    return lax.ppermute(array, axis, pairs)


def swapped(array, axis, bit):
    length = lax.axis_size(axis)
    return lax.ppermute(array, axis, [(i, i ^ bit) for i in range(length)])


def bits_of(axis):
    length = lax.axis_size(axis)
    found, bit = [], 1
    while bit < length:
        found.append(bit)
        bit *= 2
    assert bit == length
    return found


def call(kernel, outs, args, flops=1e8):
    spec = pl.BlockSpec(memory_space=pltpu.VMEM)
    shapes = [jax.ShapeDtypeStruct(shape, dtype) for shape, dtype in outs]
    moved = sum(a.size * a.dtype.itemsize for a in args)
    moved += sum(s.size * s.dtype.itemsize for s in shapes)
    return pl.pallas_call(
        kernel,
        out_shape=shapes,
        in_specs=[spec] * len(args),
        out_specs=[spec] * len(outs),
        compiler_params=pltpu.CompilerParams(vmem_limit_bytes=VMEM_LIMIT),
        cost_estimate=pl.CostEstimate(
            flops=int(flops), bytes_accessed=int(moved), transcendentals=0
        ),
    )(*args)


def mm(left, right, contract=((1,), (0,))):
    return lax.dot_general(left, right, (contract, ((), ())), preferred_element_type=f32)


NT = ((1,), (1,))
TN = ((0,), (0,))


def normalize(values_in):
    mean_v = jnp.mean(values_in, axis=-1, keepdims=True)
    centred = values_in - mean_v
    var_v = jnp.mean(centred * centred, axis=-1, keepdims=True)
    rstd = lax.rsqrt(var_v + epsilon)
    return (centred * rstd, rstd)


def norm_bwd(grad_in, normed, rstd, gain):
    scaled = grad_in * gain
    inner = jnp.mean(scaled, axis=-1, keepdims=True)
    along = jnp.mean(scaled * normed, axis=-1, keepdims=True)
    return rstd * (scaled - inner - normed * along)


def column_sum(values_in):
    return jnp.sum(values_in, axis=0, keepdims=True)


def gelu_pair(pre_act):
    inner = gelu_c * (pre_act + 0.044715 * pre_act * pre_act * pre_act)
    tanh_v = jnp.tanh(inner)
    value_out = 0.5 * pre_act * (1.0 + tanh_v)
    slope = 0.5 * (1.0 + tanh_v) + 0.5 * pre_act * (1.0 - tanh_v * tanh_v) * gelu_c * (
        1.0 + 3.0 * 0.044715 * pre_act * pre_act
    )
    return (value_out, slope)


def joined(own_ref, other_ref):
    return own_ref[...].astype(f32) + other_ref[...].astype(f32)


def place_pieces(pieces, out_ref):
    mine = lax.axis_index("tensor")
    rows = pieces[0].shape[0]
    for number, piece in enumerate(pieces):
        start = pl.multiple_of((mine ^ number) * rows, rows)
        out_ref[pl.ds(start, rows), :] = piece[...].astype(out_ref.dtype)


def gathered(piece):
    pieces = {0: piece}
    for bit in bits_of("tensor")[::-1]:
        for number in list(pieces):
            pieces[number ^ bit] = swapped(pieces[number], "tensor", bit)
    return [pieces[number] for number in range(len(pieces))]


def exchanged(part):
    bits = bits_of("tensor")
    for bit in bits[:-1]:
        other = swapped(part, "tensor", bit)
        part = (part.astype(f32) + other.astype(f32)).astype(bf16)
    return [part, swapped(part, "tensor", bits[-1])]


def project_rows(hidden, layer, refs, outs):
    gains, biases, w_qkv, qv_bias, pick = refs
    h_ref, picked_ref, q_ref, kv_ref = outs
    width = q_ref.shape[1]
    hat, _ = normalize(hidden)
    act = (hat * gains[layer, 0:1] + biases[layer, 0:1]).astype(bf16)
    kv = mm(act, w_qkv[layer, width:], NT)
    values = kv[:, width:] + qv_bias[layer, 1:2]
    kv_ref[...] = jnp.concatenate([kv[:, :width], values], axis=1).astype(bf16)
    query = mm(act, w_qkv[layer, :width], NT)
    q_ref[...] = (query + qv_bias[layer, 0:1]).astype(bf16)
    picked_ref[...] = mm(act, pick[...]).astype(bf16)


def project_first(pieces, params, pick):
    count = len(pieces)
    rows = count * pieces[0].shape[0]
    width = params["w_out"].shape[1]

    def kernel(*refs):
        ins, outs = refs[: count + 5], refs[count + 5 :]
        place_pieces(ins[:count], outs[0])
        project_rows(outs[0][...], 0, ins[count:], outs)

    return call(
        kernel,
        [((rows, D), f32), ((rows, D), bf16), ((rows, width), bf16), ((rows, 2 * width), bf16)],
        [*pieces, *[params[k] for k in ("gains", "biases", "w_qkv", "qv_bias")], pick],
    )


def project_next(mid, pair, layer, params, pick):
    rows = mid.shape[0]
    width = params["w_out"].shape[1]

    def kernel(mid_ref, own_ref, other_ref, *refs):
        ins, outs = refs[:5], refs[5:]
        hidden = mid_ref[...] + joined(own_ref, other_ref) + ins[1][layer - 1, 3:4]
        outs[0][...] = hidden
        project_rows(hidden, layer, ins, outs)

    return call(
        kernel,
        [((rows, D), f32), ((rows, D), bf16), ((rows, width), bf16), ((rows, 2 * width), bf16)],
        [mid, *pair, *[params[k] for k in ("gains", "biases", "w_qkv", "qv_bias")], pick],
    )


def head_lanes(shape, head):
    lane = lax.broadcasted_iota(jnp.int32, shape, 1)
    return (lane >= head * HD) & (lane < (head + 1) * HD)


def allowed_of(seg_q, seg_k, rows):
    shape = (rows, SPAN * rows)
    query = lax.broadcasted_iota(jnp.int32, shape, 0)
    key = lax.broadcasted_iota(jnp.int32, shape, 1)
    return (key <= query + (SPAN - 1) * rows) & (seg_q[...] == seg_k[...])


def attend(q, kv_parts, segs, layer, params):
    rows, width = q.shape
    heads = width // HD

    def kernel(q_ref, *refs):
        kv_refs, (seg_q, seg_k, w_out, att_ref, lse_ref, part_ref) = refs[:SPAN], refs[SPAN:]
        allowed = allowed_of(seg_q, seg_k, rows)
        kv_all = jnp.concatenate([r[...] for r in kv_refs], axis=0)
        keys, values = kv_all[:, :width], kv_all[:, width:]
        query = q_ref[...]
        mixed = jnp.zeros((rows, width), f32)
        logs = jnp.zeros((rows, 128), f32)
        lane = lax.broadcasted_iota(jnp.int32, (rows, 128), 1)
        for head in range(heads):
            inside = head_lanes((rows, width), head)
            scores = mm(jnp.where(inside, query, 0), keys, NT) * HD ** (-0.5)
            scores = jnp.where(allowed, scores, -1e30)
            top = jnp.max(scores, axis=-1, keepdims=True)
            log_total = top + jnp.log(jnp.sum(jnp.exp(scores - top), axis=-1, keepdims=True))
            weights = jnp.exp(scores - log_total).astype(bf16)
            mixed = jnp.where(inside, mm(weights, values), mixed)
            logs = jnp.where(lane == head, log_total, logs)
        att = mixed.astype(bf16)
        att_ref[...] = att
        lse_ref[...] = logs
        part_ref[...] = mm(att, w_out[layer]).astype(bf16)

    return call(
        kernel,
        [((rows, width), bf16), ((rows, 128), f32), ((rows, D), bf16)],
        [q, *kv_parts, *segs, params["w_out"]],
    )


def feed_forward(hidden, pair, picked1, att, layer, params, pick):
    rows, width = att.shape
    half = D // 2
    inner = params["w_up"].shape[2]
    pad = -(2 * half + inner + width) % 128

    def kernel(h_ref, own_ref, other_ref, p1_ref, att_ref, gains, biases, up, down, ffb, pick_ref,
               mid_ref, slope_ref, sent_ref, kept_ref, part_ref):
        mid = h_ref[...] + joined(own_ref, other_ref) + biases[layer, 1:2]
        mid_ref[...] = mid
        hat, _ = normalize(mid)
        act2 = (hat * gains[layer, 1:2] + biases[layer, 2:3]).astype(bf16)
        pre = mm(act2, up[layer]) + ffb[layer : layer + 1]
        value, slope = gelu_pair(pre)
        act3 = value.astype(bf16)
        part_ref[...] = mm(act3, down[layer]).astype(bf16)
        slope_ref[...] = slope
        picked2 = mm(act2, pick_ref[...]).astype(bf16)
        kept_ref[:, :half] = p1_ref[:, :half]
        kept_ref[:, half:] = picked2[:, :half]
        sent_ref[:, :half] = p1_ref[:, half:]
        sent_ref[:, half : 2 * half] = picked2[:, half:]
        sent_ref[:, 2 * half : 2 * half + inner] = act3
        sent_ref[:, 2 * half + inner : 2 * half + inner + width] = att_ref[...]
        if pad:
            sent_ref[:, 2 * half + inner + width :] = jnp.zeros((rows, pad), bf16)

    return call(
        kernel,
        [
            ((rows, D), f32),
            ((rows, inner), f32),
            ((rows, 2 * half + inner + width + pad), bf16),
            ((rows, D), bf16),
            ((rows, D), bf16),
        ],
        [hidden, *pair, picked1, att]
        + [params[k] for k in ("gains", "biases", "w_up", "w_down", "ff_bias")]
        + [pick],
    )


def last_rows(mid, pair, params, own_rows):
    def kernel(mid_ref, own_ref, other_ref, biases, out_ref):
        start = pl.multiple_of(lax.axis_index("tensor") * own_rows, own_rows)
        here = pl.ds(start, own_rows)
        total = mid_ref[here, :] + own_ref[here, :].astype(f32) + other_ref[here, :].astype(f32)
        out_ref[...] = (total + biases[LAYERS - 1, 3:4]).astype(bf16)

    return call(kernel, [((own_rows, D), bf16)], [mid, *pair, params["biases"]])[0]


def norm1_grad(gmid_ref, own_ref, other_ref, h_ref, gains, layer):
    d_norm = joined(own_ref, other_ref)
    hat, rstd = normalize(h_ref[...])
    grad = gmid_ref[...] + norm_bwd(d_norm, hat, rstd, gains[layer, 0:1])
    return grad, column_sum(d_norm * hat), column_sum(d_norm)


def mlp_grad(grad, layer, refs, outs):
    slope_ref, up, down, pick_ref = refs
    sent_ref, part_ref, small_ref, kept_ref = outs
    half = D // 2
    grad_b = grad.astype(bf16)
    d_pre = mm(grad_b, down[layer], NT) * slope_ref[...]
    pre_b = d_pre.astype(bf16)
    part_ref[...] = mm(pre_b, up[layer], NT).astype(bf16)
    picked = mm(grad_b, pick_ref[...]).astype(bf16)
    kept_ref[...] = picked[:, :half]
    sent_ref[:, :half] = picked[:, half:]
    sent_ref[:, half:] = pre_b
    small_ref[0:1, :] = column_sum(d_pre)
    small_ref[1:2, :] = column_sum(grad)


def mlp_outs(rows, inner):
    assert inner == D
    return [
        ((rows, D), f32),
        ((rows, D // 2 + inner), bf16),
        ((rows, D), bf16),
        ((8, D), f32),
        ((rows, D // 2), bf16),
    ]


def mlp_grad_last(pieces, slope, params, pick):
    count = len(pieces)
    rows, inner = slope.shape

    def kernel(*refs):
        ins, outs = refs[: count + 4], refs[count + 4 :]
        place_pieces(ins[:count], outs[0])
        outs[3][...] = jnp.zeros((8, D), f32)
        mlp_grad(outs[0][...], LAYERS - 1, ins[count:], outs[1:])

    return call(
        kernel,
        mlp_outs(rows, inner),
        [*pieces, slope, params["w_up"], params["w_down"], pick],
    )


def mlp_grad_next(gmid, pair, hidden, slope, layer, params, pick):
    rows, inner = slope.shape

    def kernel(gmid_ref, own_ref, other_ref, h_ref, gains, *refs):
        ins, outs = refs[:4], refs[4:]
        grad, g_gain, g_bias = norm1_grad(gmid_ref, own_ref, other_ref, h_ref, gains, layer + 1)
        outs[0][...] = grad
        outs[3][...] = jnp.zeros((8, D), f32)
        mlp_grad(grad, layer, ins, outs[1:])
        outs[3][2:3, :] = g_gain
        outs[3][3:4, :] = g_bias

    return call(
        kernel,
        mlp_outs(rows, inner),
        [gmid, *pair, hidden, params["gains"], slope, params["w_up"], params["w_down"], pick],
    )


def attend_grad(grad, pair, mid, q, kv_parts, segs, att, lse, layer, params, pick):
    rows, width = q.shape
    heads = width // HD
    back = SPAN - 1

    def kernel(g_ref, own_ref, other_ref, mid_ref, q_ref, *refs):
        kv_refs, refs = refs[:SPAN], refs[SPAN:]
        seg_q, seg_k, att_ref, lse_ref, gains, w_out, pick_ref = refs[:7]
        gmid_ref, picked_ref, dq_ref, dkv_ref, small_ref = refs[7:12]
        away_refs = refs[12:]
        d_norm = joined(own_ref, other_ref)
        hat, rstd = normalize(mid_ref[...])
        gmid = g_ref[...] + norm_bwd(d_norm, hat, rstd, gains[layer, 1:2])
        gmid_ref[...] = gmid
        mid_b = gmid.astype(bf16)
        d_att = mm(mid_b, w_out[layer], NT).astype(bf16)
        allowed = allowed_of(seg_q, seg_k, rows)
        kv_all = jnp.concatenate([r[...] for r in kv_refs], axis=0)
        keys, values = kv_all[:, :width], kv_all[:, width:]
        query, logs = q_ref[...], lse_ref[...]
        weighed = d_att.astype(f32) * att_ref[...].astype(f32)
        d_query = jnp.zeros((rows, width), f32)
        d_keys = jnp.zeros((SPAN * rows, width), f32)
        d_values = jnp.zeros((SPAN * rows, width), f32)
        for head in range(heads):
            inside = head_lanes((rows, width), head)
            query_h = jnp.where(inside, query, 0)
            d_att_h = jnp.where(inside, d_att, 0)
            scores = mm(query_h, keys, NT) * HD ** (-0.5)
            scores = jnp.where(allowed, scores, -1e30)
            probs = jnp.exp(scores - logs[:, head : head + 1])
            delta = jnp.sum(jnp.where(inside, weighed, 0.0), axis=-1, keepdims=True)
            d_prob = mm(d_att_h, values, NT)
            d_score = (probs * (d_prob - delta) * HD ** (-0.5)).astype(bf16)
            d_query = jnp.where(inside, mm(d_score, keys), d_query)
            d_keys = d_keys + mm(d_score, query_h, TN)
            d_values = d_values + mm(probs.astype(bf16), d_att_h, TN)
        d_kv = jnp.concatenate([d_keys, d_values], axis=1)
        dq_ref[...] = d_query
        dkv_ref[...] = d_kv[back * rows :]
        for distance in range(1, SPAN):
            block = back - distance
            away_refs[distance - 1][...] = d_kv[block * rows : (block + 1) * rows].astype(bf16)
        picked_ref[...] = mm(mid_b, pick_ref[...]).astype(bf16)
        small_ref[...] = jnp.zeros((8, D), f32)
        small_ref[0:1, :] = column_sum(d_norm * hat)
        small_ref[1:2, :] = column_sum(d_norm)
        small_ref[2:3, :] = column_sum(gmid)

    return call(
        kernel,
        [
            ((rows, D), f32),
            ((rows, D), bf16),
            ((rows, width), f32),
            ((rows, 2 * width), f32),
            ((8, D), f32),
        ]
        + [((rows, 2 * width), bf16)] * back,
        [grad, *pair, mid, q, *kv_parts, *segs, att, lse]
        + [params["gains"], params["w_out"], pick],
    )


def project_grad(dq, dkv, arrived, picked, layer, params):
    rows, width = dq.shape
    half = D // 2
    pad = -(half + 3 * width) % 128

    def kernel(dq_ref, dkv_ref, *refs):
        near, (picked_ref, w_qkv, sent_ref, part_ref, small_ref) = refs[: SPAN - 1], refs[SPAN - 1 :]
        d_kv = dkv_ref[...]
        for ref in near:
            d_kv = d_kv + ref[...].astype(f32)
        d_query = dq_ref[...]
        query_b, kv_b = d_query.astype(bf16), d_kv.astype(bf16)
        part = mm(kv_b, w_qkv[layer, width:]) + mm(query_b, w_qkv[layer, :width])
        part_ref[...] = part.astype(bf16)
        sent_ref[:, :half] = picked_ref[:, half:]
        sent_ref[:, half : half + 2 * width] = kv_b
        sent_ref[:, half + 2 * width : half + 3 * width] = query_b
        if pad:
            sent_ref[:, half + 3 * width :] = jnp.zeros((rows, pad), bf16)
        small_ref[...] = jnp.zeros((8, D), f32)
        small_ref[0:1, :width] = column_sum(d_query)
        small_ref[1:2, :width] = column_sum(d_kv)[:, width:]

    return call(
        kernel,
        [((rows, half + 3 * width + pad), bf16), ((rows, D), bf16), ((8, D), f32)],
        [dq, dkv, *arrived, picked, params["w_qkv"]],
    )


def own_small(mlp_small, qv_small):
    def kernel(*refs):
        mlp, qv, out = refs[:LAYERS], refs[LAYERS : 2 * LAYERS], refs[-1]
        out[...] = jnp.zeros((8, D), f32)
        for layer in range(LAYERS):
            out[layer : layer + 1, :] = mlp[layer][0:1, :]
            at = LAYERS + 2 * layer
            out[at : at + 2, :] = qv[layer][0:2, :]

    return call(kernel, [((8, D), f32)], [*mlp_small, *qv_small], 1e5)[0]


def small_rows(count):
    return 6 * LAYERS + 2 * LAYERS + LAYERS * count


def first_grad(gmid, pair, hidden, params, mlp_small, att_small, own_pieces, own_rows):
    count = len(own_pieces)
    width = params["w_out"].shape[1]
    rows_all = small_rows(count)
    padded = rows_all + -rows_all % 8

    def kernel(gmid_ref, own_ref, other_ref, h_ref, gains, *refs):
        mlp, att = refs[:LAYERS], refs[LAYERS : 2 * LAYERS]
        pieces = refs[2 * LAYERS : 2 * LAYERS + count]
        in_ref, all_ref, g_ref = refs[2 * LAYERS + count :]
        mine = lax.axis_index("tensor")
        grad, g_gain, g_bias = norm1_grad(gmid_ref, own_ref, other_ref, h_ref, gains, 0)
        g_ref[...] = grad
        start = pl.multiple_of(mine * own_rows, own_rows)
        in_ref[...] = g_ref[pl.ds(start, own_rows), :].astype(bf16)
        all_ref[...] = jnp.zeros((padded, D), f32)
        for layer in range(LAYERS):
            gain1 = g_gain if layer == 0 else mlp[layer - 1][2:3, :]
            bias1 = g_bias if layer == 0 else mlp[layer - 1][3:4, :]
            at = 2 * layer
            all_ref[at : at + 1, :] = gain1
            all_ref[at + 1 : at + 2, :] = att[layer][0:1, :]
            at = 2 * LAYERS + 4 * layer
            all_ref[at : at + 1, :] = bias1
            all_ref[at + 1 : at + 2, :] = att[layer][2:3, :]
            all_ref[at + 2 : at + 3, :] = att[layer][1:2, :]
            all_ref[at + 3 : at + 4, :] = mlp[layer][1:2, :]
        for target in range(count):
            chosen = pieces[0][...]
            for number in range(1, count):
                chosen = jnp.where((mine ^ number) == target, pieces[number][...], chosen)
            for layer in range(LAYERS):
                at = 6 * LAYERS + 2 * layer
                source = LAYERS + 2 * layer
                lanes = slice(target * width, (target + 1) * width)
                all_ref[at : at + 2, lanes] = chosen[source : source + 2, :width]
                at = 8 * LAYERS + layer * count + target
                all_ref[at : at + 1, :] = chosen[layer : layer + 1, :]

    rows = gmid.shape[0]
    got = call(
        kernel,
        [((own_rows, D), bf16), ((padded, D), f32), ((rows, D), f32)],
        [gmid, *pair, hidden, params["gains"], *mlp_small, *att_small, *own_pieces],
    )
    return got[0], got[1]


def small_outs(total, other, count):
    def kernel(total_ref, other_ref, gains, biases, qv, ffb):
        both = total_ref[...] + other_ref[...]
        for layer in range(LAYERS):
            gains[layer] = both[2 * layer : 2 * layer + 2]
            at = 2 * LAYERS + 4 * layer
            biases[layer] = both[at : at + 4]
            at = 6 * LAYERS + 2 * layer
            qv[layer] = both[at : at + 2]
            for target in range(count):
                at = 8 * LAYERS + layer * count + target
                ffb[layer : layer + 1, target * D : (target + 1) * D] = both[at : at + 1]

    return call(
        kernel,
        [
            ((LAYERS, 2, D), f32),
            ((LAYERS, 4, D), f32),
            ((LAYERS, 2, D), f32),
            ((LAYERS, count * D), f32),
        ],
        [total, other],
        1e5,
    )


def split_rows(total, bit, block, send_ref, keep_ref):
    mine = lax.axis_index("dp")
    high = jnp.where((mine & bit) != 0, 1, 0)
    pairs = total.shape[0] // (2 * block)
    for pair in range(pairs):
        for which in range(2):
            rows = total[(2 * pair + which) * block : (2 * pair + which + 1) * block]
            out = slice(pair * block, (pair + 1) * block)

            @pl.when(high == which)
            def _():
                keep_ref[out, :] = rows

            @pl.when(high != which)
            def _():
                send_ref[out, :] = rows.astype(bf16)


def split_plain(total, bit, block):
    pairs = total.shape[0] // (2 * block)
    split = total.reshape(pairs, 2, block, total.shape[1])
    high = jnp.where((lax.axis_index("dp") & bit) != 0, 1, 0)
    send = lax.dynamic_index_in_dim(split, 1 - high, 1, keepdims=False)
    keep = lax.dynamic_index_in_dim(split, high, 1, keepdims=False)
    return send.reshape(-1, total.shape[1]).astype(bf16), keep.reshape(-1, total.shape[1])


def halved(send, keep, bits, block):
    for place, bit in enumerate(bits):
        arrived = swapped(send, "dp", bit)
        if place == len(bits) - 1:
            return keep, arrived
        shape = (keep.shape[0] // 2, keep.shape[1])
        if block % 16:
            send, keep = split_plain(keep + arrived.astype(f32), bits[place + 1], block)
        else:

            def kernel(keep_ref, arrived_ref, send_ref, kept_ref, following=bits[place + 1]):
                total = keep_ref[...] + arrived_ref[...].astype(f32)
                split_rows(total, following, block, send_ref, kept_ref)

            send, keep = call(kernel, [(shape, bf16), (shape, f32)], [keep, arrived], 1e6)


def weight_parts(first, second, products, wide):
    half = D // 2
    count = lax.axis_size("dp")
    block = D // count
    bits = bits_of("dp")
    flat = []
    for sent, kept in (first, second):
        flat += [sent, swapped(sent, "dp", bits[0]), kept]
    shape = (half // 2, wide)

    def products_of(refs):
        done = []
        for (la, kept_at, sent_at), (ra, r0, r1) in products:
            kept = refs[3 * la + 2][:, kept_at : kept_at + half]
            given = refs[3 * la + 1][:, sent_at : sent_at + half]
            left = jnp.concatenate([kept, given], axis=0)
            right = jnp.concatenate([refs[3 * ra][:, r0:r1], refs[3 * ra + 1][:, r0:r1]], axis=0)
            done.append(mm(left, right, TN))
        return jnp.concatenate(done, axis=1)

    if block % 16:

        def kernel(*refs):
            refs[6][...] = products_of(refs)

        total = call(kernel, [((half, wide), f32)], flat, 3e8)[0]
        send, keep = split_plain(total, bits[1], block)
    else:

        def kernel(*refs):
            split_rows(products_of(refs), bits[1], block, refs[6], refs[7])

        send, keep = call(kernel, [(shape, bf16), (shape, f32)], flat, 3e8)
    return halved(send, keep, bits[1:], block)


def mlp_outputs(parts, block, inner):
    def kernel(*refs):
        up, down = refs[-2:]
        for layer in range(LAYERS):
            total = joined(refs[2 * layer], refs[2 * layer + 1])
            up[layer] = total[:, :inner]
            down[layer] = total[:, inner:]

    args = [a for pair in parts for a in pair]
    return call(kernel, [((LAYERS, block, inner), f32)] * 2, args, 1e6)


def att_outputs(parts, block, width):
    def kernel(*refs):
        qkv, out = refs[-2:]
        for layer in range(LAYERS):
            total = joined(refs[2 * layer], refs[2 * layer + 1])
            qkv[layer, 0] = total[:, 2 * width : 3 * width]
            qkv[layer, 1] = total[:, :width]
            qkv[layer, 2] = total[:, width : 2 * width]
            out[layer] = total[:, 3 * width :]

    args = [a for pair in parts for a in pair]
    return call(
        kernel,
        [((LAYERS, 3, block, width), f32), ((LAYERS, block, width), f32)],
        args,
        1e6,
    )


def shards(
    tokens, cotangent, segments, w_qkv, qv_bias, w_out, w_up, w_down, ff_bias, gains, biases
):
    tensor_count = lax.axis_size("tensor")
    dp_count = lax.axis_size("dp")
    dp_index = lax.axis_index("dp")
    own_rows = tokens.shape[0]
    rows = own_rows * tensor_count
    width = w_out.shape[1]
    inner = w_up.shape[2]
    half = D // 2
    block = D // dp_count
    params = {
        "w_qkv": w_qkv.transpose(0, 2, 3, 1).reshape(LAYERS, 3 * width, D),
        "qv_bias": qv_bias,
        "w_out": w_out,
        "w_up": w_up,
        "w_down": w_down,
        "ff_bias": ff_bias,
        "gains": gains,
        "biases": biases,
    }
    seg_q = lax.dynamic_slice_in_dim(segments, dp_index * rows, rows)[:, None]
    padded = jnp.concatenate([jnp.full(((SPAN - 1) * rows,), -1, jnp.int32), segments])
    seg_k = lax.dynamic_slice_in_dim(padded, dp_index * rows, SPAN * rows)[None, :]
    segs = [seg_q, seg_k]
    column = lax.broadcasted_iota(jnp.int32, (D, D), 1)
    side = (dp_index & 1) ^ (column // half)
    column = column % half
    source = (column // block) * (2 * block) + side * block + column % block
    pick = (lax.broadcasted_iota(jnp.int32, (D, D), 0) == source).astype(bf16)

    token_pieces = gathered(tokens)
    cot_pieces = gathered(cotangent)
    saved = []
    sent_fwd = []
    mid = pair = None
    for layer in range(LAYERS):
        if layer == 0:
            hidden, picked1, q, kv = project_first(token_pieces, params, pick)
        else:
            hidden, picked1, q, kv = project_next(mid, pair, layer, params, pick)
        kv_parts = [shifted(kv, "dp", distance) for distance in range(SPAN - 1, 0, -1)] + [kv]
        att, lse, part = attend(q, kv_parts, segs, layer, params)
        mid, slope, sent, kept, part = feed_forward(
            hidden, exchanged(part), picked1, att, layer, params, pick
        )
        sent_fwd.append((sent, kept))
        pair = exchanged(part)
        saved.append((hidden, q, kv_parts, att, lse, mid, slope))
    result = last_rows(mid, pair, params, own_rows)

    up_at, act3_at, att_at = half, 2 * half, 2 * half + inner
    mlp_products = [
        ((0, up_at, up_at), (1, half, half + inner)),
        ((1, 0, 0), (0, act3_at, act3_at + inner)),
    ]
    att_products = [
        ((0, 0, 0), (1, half, half + 3 * width)),
        ((1, 0, 0), (0, att_at, att_at + width)),
    ]
    mlp_small, att_small, qv_small = ([None] * LAYERS for _ in range(3))
    mlp_parts, att_parts = ([None] * LAYERS for _ in range(2))
    gmid = None
    for layer in range(LAYERS - 1, -1, -1):
        hidden, q, kv_parts, att, lse, mid, slope = saved[layer]
        if layer == LAYERS - 1:
            grad, sent1, part, mlp_small[layer], kept1 = mlp_grad_last(cot_pieces, slope, params, pick)
        else:
            grad, sent1, part, mlp_small[layer], kept1 = mlp_grad_next(
                gmid, pair, saved[layer + 1][0], slope, layer, params, pick
            )
        pair = exchanged(part)
        gmid, picked, dq, dkv, att_small[layer], *away = attend_grad(
            grad, pair, mid, q, kv_parts, segs, att, lse, layer, params, pick
        )
        arrived = [shifted(a, "dp", -(place + 1)) for place, a in enumerate(away)]
        sent2, part, qv_small[layer] = project_grad(dq, dkv, arrived, picked, layer, params)
        pair = exchanged(part)
        mlp_parts[layer] = weight_parts(sent_fwd[layer], (sent1, kept1), mlp_products, 2 * inner)
        att_parts[layer] = weight_parts(sent_fwd[layer], (sent2, picked), att_products, 4 * width)

    own_pieces = gathered(own_small(mlp_small, qv_small))
    input_grad, small = first_grad(
        gmid, pair, saved[0][0], params, mlp_small, att_small, own_pieces, own_rows
    )
    dp_bits = bits_of("dp")
    for bit in dp_bits[:-1]:
        small = small + swapped(small, "dp", bit)
    small_grads = small_outs(small, swapped(small, "dp", dp_bits[-1]), tensor_count)
    g_up, g_down = mlp_outputs(mlp_parts, block, inner)
    g_qkv, g_out = att_outputs(att_parts, block, width)
    return (
        result,
        input_grad,
        g_qkv.transpose(0, 2, 1, 3),
        g_out.transpose(0, 2, 1),
        g_up,
        g_down.transpose(0, 2, 1),
        *small_grads,
    )


def solution(mesh):
    return jax.shard_map(
        shards,
        mesh=mesh,
        in_specs=(
            P(("dp", "tensor"), None),
            P(("dp", "tensor"), None),
            P(),
            P(None, None, None, "tensor"),
            P(None, None, "tensor"),
            P(None, "tensor", None),
            P(None, None, "tensor"),
            P(None, "tensor", None),
            P(None, "tensor"),
            P(),
            P(),
        ),
        out_specs=(
            P(("dp", "tensor"), None),
            P(("dp", "tensor"), None),
            P(None, "dp", None, "tensor"),
            P(None, "tensor", "dp"),
            P(None, "dp", "tensor"),
            P(None, "tensor", "dp"),
            P(),
            P(),
            P(),
            P(),
        ),
        check_vma=False,
    )
```

```python
import jax
import jax.numpy as jnp
from jax import lax
from jax.experimental import pallas as pl
from jax.experimental.pallas import tpu as pltpu
from jax.sharding import PartitionSpec as P

D = 768
HD = 64
FF = 3072
LAYERS = 2
SPAN = 4
PAIR = 2

epsilon = 1e-05
gelu_c = 0.7978845608028654
f32 = jnp.float32
bf16 = jnp.bfloat16
VMEM_LIMIT = 28 * 1024 * 1024


def shifted(array, axis, by):
    length = lax.axis_size(axis)
    pairs = [(i, i + by) for i in range(length) if 0 <= i + by < length]
    return lax.ppermute(array, axis, pairs)


def swapped(array, axis, bit):
    length = lax.axis_size(axis)
    return lax.ppermute(array, axis, [(i, i ^ bit) for i in range(length)])


def bits_of(axis):
    length = lax.axis_size(axis)
    found, bit = [], 1
    while bit < length:
        found.append(bit)
        bit *= 2
    assert bit == length
    return found


def call(kernel, outs, args, flops=1e8):
    spec = pl.BlockSpec(memory_space=pltpu.VMEM)
    shapes = [jax.ShapeDtypeStruct(shape, dtype) for shape, dtype in outs]
    return pl.pallas_call(
        kernel,
        out_shape=shapes,
        in_specs=[spec] * len(args),
        out_specs=[spec] * len(outs),
        compiler_params=pltpu.CompilerParams(vmem_limit_bytes=VMEM_LIMIT),
        cost_estimate=pl.CostEstimate(flops=1, bytes_accessed=1, transcendentals=0),
    )(*args)


def mm(left, right, contract=((1,), (0,))):
    return lax.dot_general(left, right, (contract, ((), ())), preferred_element_type=f32)


NT = ((1,), (1,))
TN = ((0,), (0,))


def normalize(values_in):
    mean_v = jnp.mean(values_in, axis=-1, keepdims=True)
    centred = values_in - mean_v
    var_v = jnp.mean(centred * centred, axis=-1, keepdims=True)
    rstd = lax.rsqrt(var_v + epsilon)
    return (centred * rstd, rstd)


def norm_bwd(grad_in, normed, rstd, gain):
    scaled = grad_in * gain
    inner = jnp.mean(scaled, axis=-1, keepdims=True)
    along = jnp.mean(scaled * normed, axis=-1, keepdims=True)
    return rstd * (scaled - inner - normed * along)


def gain(small, layer, which):
    return small[0][layer, which : which + 1]


def bias(small, layer, which):
    return small[1][layer, which : which + 1]


def ff_bias_row(small, layer):
    return small[2][layer : layer + 1]


def qv_bias(small, layer, which):
    return small[3][layer, which : which + 1]


def column_sum(values_in):
    return jnp.sum(values_in, axis=0, keepdims=True)


def gelu_pair(pre_act):
    inner = gelu_c * (pre_act + 0.044715 * pre_act * pre_act * pre_act)
    tanh_v = jnp.tanh(inner)
    value_out = 0.5 * pre_act * (1.0 + tanh_v)
    slope = 0.5 * (1.0 + tanh_v) + 0.5 * pre_act * (1.0 - tanh_v * tanh_v) * gelu_c * (
        1.0 + 3.0 * 0.044715 * pre_act * pre_act
    )
    return (value_out, slope)


def joined(own_ref, other_ref):
    high = (lax.axis_index("tensor") & 1) == 1
    own, other = own_ref[...].astype(f32), other_ref[...].astype(f32)
    return jnp.concatenate(
        [jnp.where(high, other, own), jnp.where(high, own, other)], axis=0
    )


def split_halves(total, keep_ref, give_ref):
    half = total.shape[0] // 2
    high = (lax.axis_index("tensor") & 1) == 1
    low_rows, high_rows = total[:half], total[half:]
    keep_ref[...] = jnp.where(high, high_rows, low_rows)
    give_ref[...] = jnp.where(high, low_rows, high_rows).astype(bf16)


def place_pieces(pieces, out_ref):
    mine = lax.axis_index("tensor")
    rows = pieces[0].shape[0]
    for number, piece in enumerate(pieces):
        start = pl.multiple_of((mine ^ number) * rows, rows)
        out_ref[pl.ds(start, rows), :] = piece[...].astype(out_ref.dtype)


def gathered(piece):
    pieces = {0: piece}
    for bit in bits_of("tensor")[::-1]:
        for number in list(pieces):
            pieces[number ^ bit] = swapped(pieces[number], "tensor", bit)
    return [pieces[number] for number in range(len(pieces))]


def after(value, *others):
    return lax.optimization_barrier((value, *others))[0]


def exchanged(keep, give, launch=None, due=()):
    bits = bits_of("tensor")
    total = keep + swapped(give, "tensor", bits[0]).astype(f32)
    for bit in bits[1:]:
        rounded = after(total.astype(bf16), *due)
        other = swapped(rounded, "tensor", bit)
        if launch is not None and bit == bits[-1]:
            launch(rounded)
        total = rounded.astype(f32) + other.astype(f32)
    rounded = total.astype(bf16)
    return [rounded, swapped(rounded, "tensor", bits[0])]


def project_rows(hidden, layer, refs, outs):
    small, (w_qkv, pick) = refs[:4], refs[4:]
    h_ref, picked_ref, q_ref, kv_ref = outs
    width = q_ref.shape[1]
    hat, _ = normalize(hidden)
    act = (hat * gain(small, layer, 0) + bias(small, layer, 0)).astype(bf16)
    kv = mm(act, w_qkv[layer, width:], NT)
    values = kv[:, width:] + qv_bias(small, layer, 1)
    kv_ref[...] = jnp.concatenate([kv[:, :width], values], axis=1).astype(bf16)
    query = mm(act, w_qkv[layer, :width], NT)
    q_ref[...] = (query + qv_bias(small, layer, 0)).astype(bf16)
    picked_ref[...] = mm(act, pick[...]).astype(bf16)


def project_first(tokens, pieces, params, pick):
    count = len(pieces)
    own_rows = tokens.shape[0]
    rows = (count + 1) * own_rows
    width = params["w_out"].shape[1]
    gains, biases, _, qv = params["small"]
    far = [tokens, gains, biases, qv, params["w_qkv"]]
    near_shapes = [a.shape for a in far[:4]] + [(1,) + far[4].shape[1:]]
    many = len(far)

    def kernel(*refs):
        ins, far_refs, pick_ref = refs[:count], refs[count : count + many], refs[count + many]
        outs, near, sems = refs[-many - 5 : -many - 1], refs[-many - 1 : -1], refs[-1]
        sources = [*far_refs[:-1], far_refs[-1].at[pl.ds(0, 1)]]
        copies = [pltpu.make_async_copy(sources[k], near[k], sems.at[k]) for k in range(many)]
        for copy in copies:
            copy.start()
        for copy in copies:
            copy.wait()
        place_pieces([near[0], *ins], outs[0])
        small = (near[1], near[2], None, near[3])
        project_rows(outs[0][...], 0, [*small, near[4], pick_ref], outs)

    spec = pl.BlockSpec(memory_space=pltpu.VMEM)
    return pl.pallas_call(
        kernel,
        out_shape=[
            jax.ShapeDtypeStruct((rows, D), f32),
            jax.ShapeDtypeStruct((rows, D), bf16),
            jax.ShapeDtypeStruct((rows, width), bf16),
            jax.ShapeDtypeStruct((rows, 2 * width), bf16),
        ],
        in_specs=[spec] * count + [pl.BlockSpec(memory_space=pltpu.HBM)] * many + [spec],
        out_specs=[spec] * 4,
        scratch_shapes=[
            pltpu.VMEM(shape, a.dtype) for shape, a in zip(near_shapes, far, strict=True)
        ]
        + [pltpu.SemaphoreType.DMA((many,))],
        compiler_params=pltpu.CompilerParams(vmem_limit_bytes=VMEM_LIMIT),
        cost_estimate=pl.CostEstimate(flops=1, bytes_accessed=1, transcendentals=0),
    )(*pieces, *far, pick)


def project_next(mid, pair, layer, params, pick):
    rows = mid.shape[0]
    width = params["w_out"].shape[1]

    def kernel(mid_ref, own_ref, other_ref, *refs):
        ins, outs = refs[:6], refs[6:]
        hidden = mid_ref[...] + joined(own_ref, other_ref) + bias(ins, layer - 1, 3)
        outs[0][...] = hidden
        project_rows(hidden, layer, ins, outs)

    return call(
        kernel,
        [((rows, D), f32), ((rows, D), bf16), ((rows, width), bf16), ((rows, 2 * width), bf16)],
        [mid, *pair, *params["small"], params["w_qkv"], pick],
    )


def head_lanes(shape, head):
    lane = lax.broadcasted_iota(jnp.int32, shape, 1)
    return (lane >= head * HD) & (lane < (head + 1) * HD)


def allowed_of(seg_q, seg_k, rows):
    shape = (rows, SPAN * rows)
    query = lax.broadcasted_iota(jnp.int32, shape, 0)
    key = lax.broadcasted_iota(jnp.int32, shape, 1)
    return (key <= query + (SPAN - 1) * rows) & (seg_q[...] == seg_k[...])


def split_shapes(rows):
    return [((rows // 2, D), f32), ((rows // 2, D), bf16)]


def attend(q, kv_parts, segs, picked1, layer, params):
    rows, width = q.shape
    half = D // 2
    pad = -(half + width) % 128
    heads = width // HD

    def kernel(q_ref, *refs):
        kv_refs, refs = refs[:SPAN], refs[SPAN:]
        seg_q, seg_k, w_out, p1_ref, att_ref, lse_ref, sent_ref, keep_ref, give_ref = refs
        allowed = allowed_of(seg_q, seg_k, rows)
        kv_all = jnp.concatenate([r[...] for r in kv_refs], axis=0)
        keys, values = kv_all[:, :width], kv_all[:, width:]
        query = q_ref[...]
        mixed = jnp.zeros((rows, width), f32)
        logs = jnp.zeros((rows, 128), f32)
        lane = lax.broadcasted_iota(jnp.int32, (rows, 128), 1)
        for head in range(heads):
            inside = head_lanes((rows, width), head)
            scores = mm(jnp.where(inside, query, 0), keys, NT) * HD ** (-0.5)
            scores = jnp.where(allowed, scores, -1e30)
            top = jnp.max(scores, axis=-1, keepdims=True)
            log_total = top + jnp.log(jnp.sum(jnp.exp(scores - top), axis=-1, keepdims=True))
            weights = jnp.exp(scores - log_total).astype(bf16)
            mixed = jnp.where(inside, mm(weights, values), mixed)
            logs = jnp.where(lane == head, log_total, logs)
        att = mixed.astype(bf16)
        att_ref[...] = att
        sent_ref[:, :half] = p1_ref[:, half:]
        sent_ref[:, half : half + width] = att
        if pad:
            sent_ref[:, half + width :] = jnp.zeros((rows, pad), bf16)
        lse_ref[...] = logs
        split_halves(mm(att, w_out[layer]), keep_ref, give_ref)

    return call(
        kernel,
        [((rows, width), bf16), ((rows, 128), f32), ((rows, half + width + pad), bf16)]
        + split_shapes(rows),
        [q, *kv_parts, *segs, params["w_out"], picked1],
    )


def feed_forward(hidden, pair, layer, params, pick):
    rows = hidden.shape[0]
    half = D // 2
    inner = params["w_up"].shape[2]

    def kernel(h_ref, own_ref, other_ref, g_ref, b_ref, f_ref, q_ref, up, down, pick_ref,
               mid_ref, slope_ref, sent_ref, kept_ref, keep_ref, give_ref):
        small = (g_ref, b_ref, f_ref, q_ref)
        mid = h_ref[...] + joined(own_ref, other_ref) + bias(small, layer, 1)
        mid_ref[...] = mid
        hat, _ = normalize(mid)
        act2 = (hat * gain(small, layer, 1) + bias(small, layer, 2)).astype(bf16)
        pre = mm(act2, up[layer]) + ff_bias_row(small, layer)
        value, slope = gelu_pair(pre)
        act3 = value.astype(bf16)
        split_halves(mm(act3, down[layer]), keep_ref, give_ref)
        slope_ref[...] = slope
        picked2 = mm(act2, pick_ref[...]).astype(bf16)
        kept_ref[...] = picked2[:, :half]
        sent_ref[:, :half] = picked2[:, half:]
        sent_ref[:, half:] = act3

    return call(
        kernel,
        [
            ((rows, D), f32),
            ((rows, inner), f32),
            ((rows, half + inner), bf16),
            ((rows, half), bf16),
        ]
        + split_shapes(rows),
        [hidden, *pair]
        + [*params["small"], params["w_up"], params["w_down"]]
        + [pick],
    )


def last_rows(mid, pair, params, own_rows):
    def kernel(mid_ref, own_ref, other_ref, biases, out_ref, all_ref):
        total = mid_ref[...] + joined(own_ref, other_ref)
        all_ref[...] = total + biases[LAYERS - 1, 3:4]
        start = pl.multiple_of(lax.axis_index("tensor") * own_rows, own_rows)
        out_ref[...] = all_ref[pl.ds(start, own_rows), :].astype(bf16)

    args = [mid, *pair, params["small"][1]]
    return call(kernel, [((own_rows, D), bf16), (mid.shape, f32)], args)[0]


def norm1_grad(gmid_ref, own_ref, other_ref, h_ref, gains, layer):
    d_norm = joined(own_ref, other_ref)
    hat, rstd = normalize(h_ref[...])
    grad = gmid_ref[...] + norm_bwd(d_norm, hat, rstd, gains[layer, 0:1])
    return grad, column_sum(d_norm * hat), column_sum(d_norm)


def mlp_grad(grad, layer, refs, outs):
    slope_ref, up, down, pick_ref = refs
    sent_ref, small_ref, kept_ref, keep_ref, give_ref = outs
    half = D // 2
    grad_b = grad.astype(bf16)
    d_pre = mm(grad_b, down[layer], NT) * slope_ref[...]
    pre_b = d_pre.astype(bf16)
    split_halves(mm(pre_b, up[layer], NT), keep_ref, give_ref)
    picked = mm(grad_b, pick_ref[...]).astype(bf16)
    kept_ref[...] = picked[:, :half]
    sent_ref[:, :half] = picked[:, half:]
    sent_ref[:, half:] = pre_b
    small_ref[0:1, :] = column_sum(d_pre)
    small_ref[1:2, :] = column_sum(grad)


def mlp_outs(rows, inner):
    assert inner == D
    return [
        ((rows, D), f32),
        ((rows, D // 2 + inner), bf16),
        ((8, D), f32),
        ((rows, D // 2), bf16),
    ] + split_shapes(rows)


def mlp_grad_last(pieces, slope, params, pick):
    count = len(pieces)
    rows, inner = slope.shape

    def kernel(*refs):
        ins, outs = refs[: count + 4], refs[count + 4 :]
        place_pieces(ins[:count], outs[0])
        outs[2][...] = jnp.zeros((8, D), f32)
        mlp_grad(outs[0][...], LAYERS - 1, ins[count:], outs[1:])

    return call(
        kernel,
        mlp_outs(rows, inner),
        [*pieces, slope, params["w_up"], params["w_down"], pick],
    )


def mlp_grad_next(gmid, pair, hidden, slope, layer, params, pick):
    rows, inner = slope.shape

    def kernel(gmid_ref, own_ref, other_ref, h_ref, gains, *refs):
        ins, outs = refs[:4], refs[4:]
        grad, g_gain, g_bias = norm1_grad(gmid_ref, own_ref, other_ref, h_ref, gains, layer + 1)
        outs[0][...] = grad
        outs[2][...] = jnp.zeros((8, D), f32)
        mlp_grad(grad, layer, ins, outs[1:])
        outs[2][2:3, :] = g_gain
        outs[2][3:4, :] = g_bias

    return call(
        kernel,
        mlp_outs(rows, inner),
        [gmid, *pair, hidden, params["small"][0], slope, params["w_up"], params["w_down"], pick],
    )


def attend_grad(grad, pair, mid, q, kv_parts, segs, att, lse, layer, params, pick):
    rows, width = q.shape
    heads = width // HD
    back = SPAN - 1

    def kernel(g_ref, own_ref, other_ref, mid_ref, q_ref, *refs):
        kv_refs, refs = refs[:SPAN], refs[SPAN:]
        seg_q, seg_k, att_ref, lse_ref, gains, w_out, pick_ref = refs[:7]
        gmid_ref, picked_ref, dq_ref, dkv_ref, small_ref = refs[7:12]
        away_refs = refs[12:]
        d_norm = joined(own_ref, other_ref)
        hat, rstd = normalize(mid_ref[...])
        gmid = g_ref[...] + norm_bwd(d_norm, hat, rstd, gains[layer, 1:2])
        gmid_ref[...] = gmid
        mid_b = gmid.astype(bf16)
        d_att = mm(mid_b, w_out[layer], NT).astype(bf16)
        allowed = allowed_of(seg_q, seg_k, rows)
        kv_all = jnp.concatenate([r[...] for r in kv_refs], axis=0)
        keys, values = kv_all[:, :width], kv_all[:, width:]
        query, logs = q_ref[...], lse_ref[...]
        weighed = d_att.astype(f32) * att_ref[...].astype(f32)
        d_query = jnp.zeros((rows, width), f32)
        d_keys = jnp.zeros((SPAN * rows, width), f32)
        d_values = jnp.zeros((SPAN * rows, width), f32)
        for head in range(heads):
            inside = head_lanes((rows, width), head)
            query_h = jnp.where(inside, query, 0)
            d_att_h = jnp.where(inside, d_att, 0)
            scores = mm(query_h, keys, NT) * HD ** (-0.5)
            scores = jnp.where(allowed, scores, -1e30)
            probs = jnp.exp(scores - logs[:, head : head + 1])
            delta = jnp.sum(jnp.where(inside, weighed, 0.0), axis=-1, keepdims=True)
            d_prob = mm(d_att_h, values, NT)
            d_score = (probs * (d_prob - delta) * HD ** (-0.5)).astype(bf16)
            d_query = jnp.where(inside, mm(d_score, keys), d_query)
            d_keys = d_keys + mm(d_score, query_h, TN)
            d_values = d_values + mm(probs.astype(bf16), d_att_h, TN)
        d_kv = jnp.concatenate([d_keys, d_values], axis=1)
        dq_ref[...] = d_query
        dkv_ref[...] = d_kv[back * rows :]
        for distance in range(1, SPAN):
            block = back - distance
            away_refs[distance - 1][...] = d_kv[block * rows : (block + 1) * rows].astype(bf16)
        picked_ref[...] = mm(mid_b, pick_ref[...]).astype(bf16)
        small_ref[...] = jnp.zeros((8, D), f32)
        small_ref[0:1, :] = column_sum(d_norm * hat)
        small_ref[1:2, :] = column_sum(d_norm)
        small_ref[2:3, :] = column_sum(gmid)

    return call(
        kernel,
        [
            ((rows, D), f32),
            ((rows, D), bf16),
            ((rows, width), f32),
            ((rows, 2 * width), f32),
            ((8, D), f32),
        ]
        + [((rows, 2 * width), bf16)] * back,
        [grad, *pair, mid, q, *kv_parts, *segs, att, lse]
        + [params["small"][0], params["w_out"], pick],
    )


def project_grad(dq, dkv, arrived, picked, layer, params):
    rows, width = dq.shape
    half = D // 2
    pad = -(half + 3 * width) % 128

    def kernel(dq_ref, dkv_ref, *refs):
        near, refs = refs[: SPAN - 1], refs[SPAN - 1 :]
        picked_ref, w_qkv, sent_ref, small_ref, keep_ref, give_ref = refs
        d_kv = dkv_ref[...]
        for ref in near:
            d_kv = d_kv + ref[...].astype(f32)
        d_query = dq_ref[...]
        query_b, kv_b = d_query.astype(bf16), d_kv.astype(bf16)
        part = mm(kv_b, w_qkv[layer, width:]) + mm(query_b, w_qkv[layer, :width])
        split_halves(part, keep_ref, give_ref)
        sent_ref[:, :half] = picked_ref[:, half:]
        sent_ref[:, half : half + 2 * width] = kv_b
        sent_ref[:, half + 2 * width : half + 3 * width] = query_b
        if pad:
            sent_ref[:, half + 3 * width :] = jnp.zeros((rows, pad), bf16)
        small_ref[...] = jnp.zeros((8, D), f32)
        small_ref[0:1, :width] = column_sum(d_query)
        small_ref[1:2, :width] = column_sum(d_kv)[:, width:]

    return call(
        kernel,
        [((rows, half + 3 * width + pad), bf16), ((8, D), f32)] + split_shapes(rows),
        [dq, dkv, *arrived, picked, params["w_qkv"]],
    )


def small_rows(count):
    rows = 8 * LAYERS + LAYERS * count
    return rows + -rows % 8


def local_small(keep, give, hidden, mlp_small, att_small, qv_small, count, width):
    share = 1.0 / count

    def kernel(keep_ref, give_ref, h_ref, *refs):
        mlp, att, qv, out = refs[:LAYERS], refs[LAYERS : 2 * LAYERS], refs[2 * LAYERS : -1], refs[-1]
        mine = lax.axis_index("tensor")
        part = joined(keep_ref, give_ref)
        hat, _ = normalize(h_ref[...])
        out[...] = jnp.zeros(out.shape, f32)
        for layer in range(LAYERS):
            gain1 = column_sum(part * hat) if layer == 0 else mlp[layer - 1][2:3, :] * share
            bias1 = column_sum(part) if layer == 0 else mlp[layer - 1][3:4, :] * share
            at = 2 * layer
            out[at : at + 1, :] = gain1
            out[at + 1 : at + 2, :] = att[layer][0:1, :] * share
            at = 2 * LAYERS + 4 * layer
            out[at : at + 1, :] = bias1
            out[at + 1 : at + 2, :] = att[layer][2:3, :] * share
            out[at + 2 : at + 3, :] = att[layer][1:2, :] * share
            out[at + 3 : at + 4, :] = mlp[layer][1:2, :] * share
            for target in range(count):
                here = mine == target
                at = 6 * LAYERS + 2 * layer
                lanes = slice(target * width, (target + 1) * width)
                out[at : at + 2, lanes] = jnp.where(here, qv[layer][0:2, :width], 0.0)
                at = 8 * LAYERS + layer * count + target
                out[at : at + 1, :] = jnp.where(here, mlp[layer][0:1, :], 0.0)

    args = [keep, give, hidden, *mlp_small, *att_small, *qv_small]
    return call(kernel, [((small_rows(count), D), f32)], args, 1e6)[0]


def first_grad(gmid, pair, hidden, params, own_rows):
    def kernel(gmid_ref, own_ref, other_ref, h_ref, gains, in_ref, g_ref):
        g_ref[...] = norm1_grad(gmid_ref, own_ref, other_ref, h_ref, gains, 0)[0]
        start = pl.multiple_of(lax.axis_index("tensor") * own_rows, own_rows)
        in_ref[...] = g_ref[pl.ds(start, own_rows), :].astype(bf16)

    args = [gmid, *pair, hidden, params["small"][0]]
    return call(kernel, [((own_rows, D), bf16), (gmid.shape, f32)], args)[0]


def small_outs(total, other, count):
    def kernel(total_ref, other_ref, gains, biases, qv, ffb):
        both = total_ref[...] + other_ref[...]
        for layer in range(LAYERS):
            gains[layer] = both[2 * layer : 2 * layer + 2]
            at = 2 * LAYERS + 4 * layer
            biases[layer] = both[at : at + 4]
            at = 6 * LAYERS + 2 * layer
            qv[layer] = both[at : at + 2]
            for target in range(count):
                at = 8 * LAYERS + layer * count + target
                ffb[layer : layer + 1, target * D : (target + 1) * D] = both[at : at + 1]

    return call(
        kernel,
        [
            ((LAYERS, 2, D), f32),
            ((LAYERS, 4, D), f32),
            ((LAYERS, 2, D), f32),
            ((LAYERS, count * D), f32),
        ],
        [total, other],
        1e5,
    )


def split_rows(total, bit, block, send_ref, keep_ref):
    mine = lax.axis_index("dp")
    high = jnp.where((mine & bit) != 0, 1, 0)
    pairs = total.shape[0] // (2 * block)
    for pair in range(pairs):
        for which in range(2):
            rows = total[(2 * pair + which) * block : (2 * pair + which + 1) * block]
            out = slice(pair * block, (pair + 1) * block)

            @pl.when(high == which)
            def _():
                keep_ref[out, :] = rows

            @pl.when(high != which)
            def _():
                send_ref[out, :] = rows.astype(bf16)


def split_plain(total, bit, block):
    pairs = total.shape[0] // (2 * block)
    split = total.reshape(pairs, 2, block, total.shape[1])
    high = jnp.where((lax.axis_index("dp") & bit) != 0, 1, 0)
    send = lax.dynamic_index_in_dim(split, 1 - high, 1, keepdims=False)
    keep = lax.dynamic_index_in_dim(split, high, 1, keepdims=False)
    return send.reshape(-1, total.shape[1]).astype(bf16), keep.reshape(-1, total.shape[1])


class Halving:
    def __init__(self, products, wide):
        self.products, self.wide = products, wide
        self.bits = [bit for bit in bits_of("dp") if bit != PAIR]
        self.block = D // lax.axis_size("dp")
        self.place = 0

    def begin(self, sources):
        half = D // 2
        flat = [array for source in sources for array in source]
        shape = (half // 2, self.wide)
        spots = self.products

        def products_of(refs):
            done = []
            for (la, kept_at, sent_at), (ra, r0, r1) in spots:
                kept = refs[3 * la + 2][:, kept_at : kept_at + half]
                given = refs[3 * la + 1][:, sent_at : sent_at + half]
                left = jnp.concatenate([kept, given], axis=0)
                right = [refs[3 * ra][:, r0:r1], refs[3 * ra + 1][:, r0:r1]]
                done.append(mm(left, jnp.concatenate(right, axis=0), TN))
            return jnp.concatenate(done, axis=1)

        bit, block, count = self.bits[0], self.block, len(flat)
        if block % 16:

            def kernel(*refs):
                refs[count][...] = products_of(refs)

            total = call(kernel, [((half, self.wide), f32)], flat, 3e8)[0]
            self.send, self.keep = split_plain(total, bit, block)
        else:

            def kernel(*refs):
                split_rows(products_of(refs), bit, block, refs[count], refs[count + 1])

            self.send, self.keep = call(kernel, [(shape, bf16), (shape, f32)], flat, 3e8)

    def launch(self, *gates):
        send = after(self.send, *gates) if gates else self.send
        self.arrived = swapped(send, "dp", self.bits[self.place])

    def absorb(self):
        self.place += 1
        bit, block = self.bits[self.place], self.block
        if block % 16:
            total = self.keep + self.arrived.astype(f32)
            self.send, self.keep = split_plain(total, bit, block)
            return

        def kernel(keep_ref, arrived_ref, send_ref, kept_ref):
            total = keep_ref[...] + arrived_ref[...].astype(f32)
            split_rows(total, bit, block, send_ref, kept_ref)

        shape = (self.keep.shape[0] // 2, self.wide)
        args = [self.keep, self.arrived]
        self.send, self.keep = call(kernel, [(shape, bf16), (shape, f32)], args, 1e6)

    def finish(self):
        while self.place < len(self.bits) - 1:
            self.absorb()
            self.launch()
        return [self.keep, self.arrived]


def mlp_outputs(parts, block, inner):
    def kernel(*refs):
        up, down = refs[-2:]
        for layer in range(LAYERS):
            total = refs[2 * layer][...] + refs[2 * layer + 1][...].astype(f32)
            up[layer] = total[:, :inner]
            down[layer] = total[:, inner:]

    args = [a for pair in parts for a in pair]
    return call(kernel, [((LAYERS, block, inner), f32)] * 2, args, 1e6)


def att_outputs(parts, block, width):
    def kernel(*refs):
        qkv, out = refs[-2:]
        for layer in range(LAYERS):
            total = refs[2 * layer][...] + refs[2 * layer + 1][...].astype(f32)
            qkv[layer, 0] = total[:, 2 * width : 3 * width]
            qkv[layer, 1] = total[:, :width]
            qkv[layer, 2] = total[:, width : 2 * width]
            out[layer] = total[:, 3 * width :]

    args = [a for pair in parts for a in pair]
    return call(
        kernel,
        [((LAYERS, 3, block, width), f32), ((LAYERS, block, width), f32)],
        args,
        1e6,
    )


def shards(
    tokens, cotangent, segments, w_qkv, qv_bias, w_out, w_up, w_down, ff_bias, gains, biases
):
    tensor_count = lax.axis_size("tensor")
    dp_count = lax.axis_size("dp")
    dp_index = lax.axis_index("dp")
    own_rows = tokens.shape[0]
    rows = own_rows * tensor_count
    width = w_out.shape[1]
    inner = w_up.shape[2]
    half = D // 2
    block = D // dp_count
    joint = w_qkv.transpose(0, 2, 3, 1).reshape(LAYERS, 3 * width, D)
    params = {
        "small": [gains, biases, ff_bias, qv_bias],
        "w_qkv": joint,
        "w_out": w_out,
        "w_up": w_up,
        "w_down": w_down,
    }
    seg_q = lax.dynamic_slice_in_dim(segments, dp_index * rows, rows)[:, None]
    padded = jnp.concatenate([jnp.full(((SPAN - 1) * rows,), -1, jnp.int32), segments])
    seg_k = lax.dynamic_slice_in_dim(padded, dp_index * rows, SPAN * rows)[None, :]
    segs = [seg_q, seg_k]
    column = lax.broadcasted_iota(jnp.int32, (D, D), 1)
    side = ((dp_index >> 1) & 1) ^ (column // half)
    column = column % half
    piece = column // block
    source = ((piece // 2) * 4 + side * 2 + piece % 2) * block + column % block
    pick = (lax.broadcasted_iota(jnp.int32, (D, D), 0) == source).astype(bf16)

    def paired(sent, kept, gate):
        return [sent, swapped(after(sent, gate), "dp", PAIR), kept]

    mlp_work = [
        Halving([((0, 0, 0), (1, half, half + inner)), ((1, 0, 0), (0, half, half + inner))], 2 * inner)
        for _ in range(LAYERS)
    ]
    att_work = [
        Halving([((0, 0, 0), (1, half, half + 3 * width)), ((1, 0, 0), (0, half, half + width))], 4 * width)
        for _ in range(LAYERS)
    ]
    token_pieces = gathered(tokens)
    saved, rows_a, rows_b = [], [None] * LAYERS, [None] * LAYERS
    cot_pieces = None
    mid = pair = None
    for layer in range(LAYERS):
        if layer == 0:
            hidden, picked1, q, kv = project_first(tokens, token_pieces[1:], params, pick)
        else:
            hidden, picked1, q, kv = project_next(mid, pair, layer, params, pick)
        kv_parts = [shifted(kv, "dp", distance) for distance in range(SPAN - 1, 0, -1)] + [kv]
        if layer:
            q = after(q, rows_a[layer - 1][1], rows_b[layer - 1][1])
        att, lse, sent_a, keep, give = attend(q, kv_parts, segs, picked1, layer, params)

        def launch_a(gate):
            nonlocal cot_pieces
            rows_a[layer] = paired(sent_a, picked1, gate)
            if layer == 0:
                cot_pieces = gathered(after(cotangent, gate))

        pair = exchanged(keep, give, launch_a)
        mid, slope, sent_b, kept_b, keep, give = feed_forward(hidden, pair, layer, params, pick)
        saved.append((hidden, q, kv_parts, att, lse, mid, slope))
        if layer < LAYERS - 1:

            def launch_b(gate):
                rows_b[layer] = paired(sent_b, kept_b, gate)

            pair = exchanged(keep, give, launch_b)
            pair[0] = after(pair[0], cot_pieces[-1])
    last_total, last_give = keep, give

    mlp_small, att_small, qv_small = ([None] * LAYERS for _ in range(3))
    gmid = last_pair = None
    for layer in range(LAYERS - 1, -1, -1):
        last = layer == LAYERS - 1
        hidden, q, kv_parts, att, lse, mid, slope = saved[layer]
        if last:
            grad, sent1, mlp_small[layer], kept1, keep, give = mlp_grad_last(
                cot_pieces, slope, params, pick
            )
        else:
            grad, sent1, mlp_small[layer], kept1, keep, give = mlp_grad_next(
                gmid, pair, saved[layer + 1][0], slope, layer, params, pick
            )
        rows_1 = None

        def launch_1(gate):
            nonlocal rows_1
            if last:
                rows_b[layer] = paired(sent_b, kept_b, gate)
            rows_1 = paired(sent1, kept1, gate)

        if last:
            pair = exchanged(keep, give, launch_1)
            pair[0] = after(pair[0], rows_a[layer][1])
        else:
            later = layer + 1
            mlp_work[later].absorb()
            pair = exchanged(keep, give, launch_1, [mlp_work[later].send, att_work[later].send])
            mlp_work[later].launch()
            att_work[later].launch()
            pair[0] = after(pair[0], last_pair[1])
        gmid, picked, dq, dkv, att_small[layer], *away = attend_grad(
            grad, pair, mid, q, kv_parts, segs, att, lse, layer, params, pick
        )
        arrived = [shifted(a, "dp", -(place + 1)) for place, a in enumerate(away)]
        mlp_work[layer].begin([rows_b[layer], rows_1])
        mlp_work[layer].launch()
        due = [mlp_work[layer].send]
        if last:
            other = swapped(after(last_give, gmid), "tensor", 1)
            last_total = last_total + other.astype(f32)
            due.append(last_total)
        else:
            att_work[later].absorb()
            due += [mlp_work[later].arrived, att_work[later].send]
        sent2, qv_small[layer], keep, give = project_grad(
            dq, after(dkv, *due), arrived, picked, layer, params
        )
        rows_2 = None

        def launch_2(gate):
            nonlocal rows_2
            rows_2 = paired(sent2, picked, gate)
            if last:
                nonlocal last_total, last_pair
                for bit in bits_of("tensor")[1:]:
                    rounded = after(last_total.astype(bf16), gate)
                    other = swapped(rounded, "tensor", bit)
                    last_total = rounded.astype(f32) + other.astype(f32)
                rounded = last_total.astype(bf16)
                last_pair = [rounded, swapped(rounded, "tensor", 1)]

        if last:
            pair = exchanged(keep, give, launch_2)
        else:
            small = local_small(
                keep, give, saved[0][0], mlp_small, att_small, qv_small, tensor_count, width
            )
            att_work[later].launch()
            mlp_work[layer].absorb()
            pair = exchanged(keep, give, launch_2)
            mlp_work[layer].launch()
            pair[0] = after(pair[0], rows_2[1], mlp_work[layer].send)
        att_work[layer].begin([rows_a[layer], rows_2])
        att_work[layer].launch()
    input_grad = first_grad(gmid, pair, saved[0][0], params, own_rows)
    result = last_rows(saved[-1][5], last_pair, params, own_rows)
    for bit in bits_of("tensor"):
        small = small + swapped(small, "tensor", bit)
    gates = [mlp_work[0].send, att_work[0].send]
    att_work[0].absorb()
    att_work[0].launch()
    gates.append(att_work[0].send)
    dp_bits = bits_of("dp")
    for place, bit in enumerate(dp_bits):
        if place < len(gates):
            small = after(small, gates[place])
        arriving = swapped(small, "dp", bit)
        if bit != dp_bits[-1]:
            small = small + arriving
    small_grads = small_outs(small, arriving, tensor_count)
    mlp_parts = [work.finish() for work in mlp_work]
    att_parts = [work.finish() for work in att_work]
    g_up, g_down = mlp_outputs(mlp_parts, block, inner)
    g_qkv, g_out = att_outputs(att_parts, block, width)
    return (
        result,
        input_grad,
        g_qkv.transpose(0, 2, 1, 3),
        g_out.transpose(0, 2, 1),
        g_up,
        g_down.transpose(0, 2, 1),
        *small_grads,
    )


def solution(mesh):
    return jax.shard_map(
        shards,
        mesh=mesh,
        in_specs=(
            P(("dp", "tensor"), None),
            P(("dp", "tensor"), None),
            P(),
            P(None, None, None, "tensor"),
            P(None, None, "tensor"),
            P(None, "tensor", None),
            P(None, None, "tensor"),
            P(None, "tensor", None),
            P(None, "tensor"),
            P(),
            P(),
        ),
        out_specs=(
            P(("dp", "tensor"), None),
            P(("dp", "tensor"), None),
            P(None, "dp", None, "tensor"),
            P(None, "tensor", "dp"),
            P(None, "dp", "tensor"),
            P(None, "tensor", "dp"),
            P(),
            P(),
            P(),
            P(),
        ),
        check_vma=False,
    )
```

```python
import jax
import jax.numpy as jnp
from jax import lax
from jax.experimental import pallas as pl
from jax.experimental.pallas import tpu as pltpu
from jax.sharding import PartitionSpec as P

D = 768
HD = 64
FF = 3072
LAYERS = 2
SPAN = 4

epsilon = 1e-05
gelu_c = 0.7978845608028654
f32 = jnp.float32
bf16 = jnp.bfloat16
VMEM_LIMIT = 28 * 1024 * 1024


def shifted(array, axis, by):
    length = lax.axis_size(axis)
    pairs = [(i, i + by) for i in range(length) if 0 <= i + by < length]
    return lax.ppermute(array, axis, pairs)


def swapped(array, axis, bit):
    length = lax.axis_size(axis)
    return lax.ppermute(array, axis, [(i, i ^ bit) for i in range(length)])


def bits_of(axis):
    length = lax.axis_size(axis)
    found, bit = [], 1
    while bit < length:
        found.append(bit)
        bit *= 2
    assert bit == length
    return found


def call(kernel, outs, args, flops=1, moved=1):
    spec = pl.BlockSpec(memory_space=pltpu.VMEM)
    shapes = [jax.ShapeDtypeStruct(shape, dtype) for shape, dtype in outs]
    return pl.pallas_call(
        kernel,
        out_shape=shapes,
        in_specs=[spec] * len(args),
        out_specs=[spec] * len(outs),
        compiler_params=pltpu.CompilerParams(vmem_limit_bytes=VMEM_LIMIT),
        cost_estimate=pl.CostEstimate(
            flops=int(flops), bytes_accessed=int(moved), transcendentals=0
        ),
    )(*args)


def picked_halves(rows):
    wide = rows.shape[1] // 4
    high = (lax.axis_index("dp") // (lax.axis_size("dp") // 4)) % 2 == 1
    quarters = [rows[:, k * wide : (k + 1) * wide] for k in range(4)]
    return tuple(
        jnp.concatenate(
            [jnp.where(high, quarters[k + one], quarters[k + zero]) for k in (0, 2)], axis=1
        )
        for zero, one in ((0, 1), (1, 0))
    )


def mm(left, right, contract=((1,), (0,))):
    return lax.dot_general(left, right, (contract, ((), ())), preferred_element_type=f32)


NT = ((1,), (1,))
TN = ((0,), (0,))


def normalize(values_in):
    mean_v = jnp.mean(values_in, axis=-1, keepdims=True)
    centred = values_in - mean_v
    var_v = jnp.mean(centred * centred, axis=-1, keepdims=True)
    rstd = lax.rsqrt(var_v + epsilon)
    return (centred * rstd, rstd)


def norm_bwd(grad_in, normed, rstd, gain):
    scaled = grad_in * gain
    inner = jnp.mean(scaled, axis=-1, keepdims=True)
    along = jnp.mean(scaled * normed, axis=-1, keepdims=True)
    return rstd * (scaled - inner - normed * along)


def gain(small, layer, which):
    return small[0][layer, which : which + 1]


def bias(small, layer, which):
    return small[1][layer, which : which + 1]


def ff_bias_row(small, layer):
    return small[2][layer : layer + 1]


def qv_bias(small, layer, which):
    return small[3][layer, which : which + 1]


def column_sum(values_in):
    return jnp.sum(values_in, axis=0, keepdims=True)


def gelu_pair(pre_act):
    inner = gelu_c * (pre_act + 0.044715 * pre_act * pre_act * pre_act)
    tanh_v = jnp.tanh(inner)
    value_out = 0.5 * pre_act * (1.0 + tanh_v)
    slope = 0.5 * (1.0 + tanh_v) + 0.5 * pre_act * (1.0 - tanh_v * tanh_v) * gelu_c * (
        1.0 + 3.0 * 0.044715 * pre_act * pre_act
    )
    return (value_out, slope)


def joined(own_ref, other_ref):
    high = (lax.axis_index("tensor") & 1) == 1
    own, other = own_ref[...].astype(f32), other_ref[...].astype(f32)
    return jnp.concatenate(
        [jnp.where(high, other, own), jnp.where(high, own, other)], axis=0
    )


def split_halves(total, keep_ref, give_ref):
    half = total.shape[0] // 2
    high = (lax.axis_index("tensor") & 1) == 1
    low_rows, high_rows = total[:half], total[half:]
    keep_ref[...] = jnp.where(high, high_rows, low_rows)
    give_ref[...] = jnp.where(high, low_rows, high_rows).astype(bf16)


def place_pieces(pieces, out_ref):
    mine = lax.axis_index("tensor")
    rows = pieces[0].shape[0]
    for number, piece in enumerate(pieces):
        start = pl.multiple_of((mine ^ number) * rows, rows)
        out_ref[pl.ds(start, rows), :] = piece[...].astype(out_ref.dtype)


def gathered(piece):
    pieces = {0: piece}
    for bit in bits_of("tensor")[::-1]:
        for number in list(pieces):
            pieces[number ^ bit] = swapped(pieces[number], "tensor", bit)
    return [pieces[number] for number in range(len(pieces))]


def after(value, *others):
    return lax.optimization_barrier((value, *others))[0]


def exchanged(keep, give, launch=None, due=()):
    bits = bits_of("tensor")
    total = keep + swapped(give, "tensor", bits[0]).astype(f32)
    for bit in bits[1:]:
        rounded = after(total.astype(bf16), *due)
        other = swapped(rounded, "tensor", bit)
        if launch is not None and bit == bits[-1]:
            launch(rounded)
        total = rounded.astype(f32) + other.astype(f32)
    rounded = total.astype(bf16)
    return [rounded, swapped(rounded, "tensor", bits[0])]


def project_rows(hidden, layer, refs, outs):
    small, w_qkv = refs[:4], refs[4]
    h_ref, picked_ref, q_ref, kv_ref = outs
    width = q_ref.shape[1]
    hat, _ = normalize(hidden)
    act = (hat * gain(small, layer, 0) + bias(small, layer, 0)).astype(bf16)
    kv = mm(act, w_qkv[layer, width:], NT)
    values = kv[:, width:] + qv_bias(small, layer, 1)
    kv_ref[...] = jnp.concatenate([kv[:, :width], values], axis=1).astype(bf16)
    query = mm(act, w_qkv[layer, :width], NT)
    q_ref[...] = (query + qv_bias(small, layer, 0)).astype(bf16)
    half = act.shape[1] // 2
    picked_ref[:, :half], picked_ref[:, half:] = picked_halves(act)


def project_first(tokens, pieces, params):
    count = len(pieces)
    own_rows = tokens.shape[0]
    rows = (count + 1) * own_rows
    width = params["w_out"].shape[1]
    gains, biases, _, qv = params["small"]
    far = [tokens, gains, biases, qv, params["w_qkv"]]
    many = len(far)

    def kernel(*refs):
        ins, near = refs[:count], refs[count : count + many]
        outs = refs[-4:]
        place_pieces([near[0], *ins], outs[0])
        small = (near[1], near[2], None, near[3])
        project_rows(outs[0][...], 0, [*small, near[4]], outs)

    def whole(array):
        zeros = (0,) * array.ndim
        return pl.BlockSpec(array.shape, lambda step: zeros)

    spec = pl.BlockSpec(memory_space=pltpu.VMEM)
    return pl.pallas_call(
        kernel,
        grid=(1,),
        out_shape=[
            jax.ShapeDtypeStruct((rows, D), f32),
            jax.ShapeDtypeStruct((rows, D), bf16),
            jax.ShapeDtypeStruct((rows, width), bf16),
            jax.ShapeDtypeStruct((rows, 2 * width), bf16),
        ],
        in_specs=[spec] * count
        + [whole(a) for a in far[:-1]]
        + [pl.BlockSpec((1,) + far[-1].shape[1:], lambda step: (0, 0, 0))],
        out_specs=[spec] * 4,
        compiler_params=pltpu.CompilerParams(vmem_limit_bytes=VMEM_LIMIT),
        cost_estimate=pl.CostEstimate(flops=1, bytes_accessed=1, transcendentals=0),
    )(*pieces, *far)


def project_next(mid, pair, layer, params):
    rows = mid.shape[0]
    width = params["w_out"].shape[1]

    def kernel(mid_ref, own_ref, other_ref, *refs):
        ins, outs = refs[:5], refs[5:]
        hidden = mid_ref[...] + joined(own_ref, other_ref) + bias(ins, layer - 1, 3)
        outs[0][...] = hidden
        project_rows(hidden, layer, ins, outs)

    return call(
        kernel,
        [((rows, D), f32), ((rows, D), bf16), ((rows, width), bf16), ((rows, 2 * width), bf16)],
        [mid, *pair, *params["small"], params["w_qkv"]],
    )


def head_lanes(shape, head):
    lane = lax.broadcasted_iota(jnp.int32, shape, 1)
    return (lane >= head * HD) & (lane < (head + 1) * HD)


def allowed_rows(segments, rows):
    def kernel(seg_ref, out_ref):
        mine = lax.axis_index("dp")
        here = seg_ref[:, pl.ds(pl.multiple_of(mine * rows, rows), rows)].astype(f32)
        query_seg = jnp.broadcast_to(here, (rows, rows)).T
        query = lax.broadcasted_iota(jnp.int32, (rows, rows), 0)
        key = lax.broadcasted_iota(jnp.int32, (rows, rows), 1)
        for place in range(SPAN):
            behind = SPAN - 1 - place
            start = jnp.maximum(mine - behind, 0) * rows
            key_seg = seg_ref[:, pl.ds(pl.multiple_of(start, rows), rows)].astype(f32)
            same = (query_seg == key_seg) & (key <= query + behind * rows)
            seen = jnp.where(same, 1.0, 0.0) * jnp.where(mine >= behind, 1.0, 0.0)
            out_ref[:, place * rows : (place + 1) * rows] = seen

    row = segments[None, :]
    return call(kernel, [((rows, SPAN * rows), f32)], [row], 1e10, 1e8)[0]


def split_shapes(rows):
    return [((rows // 2, D), f32), ((rows // 2, D), bf16)]


def attend(q, kv_parts, mask, picked1, layer, params):
    rows, width = q.shape
    half = D // 2
    pad = -(half + width) % 128
    heads = width // HD

    def kernel(q_ref, *refs):
        kv_refs, refs = refs[:SPAN], refs[SPAN:]
        mask_ref, w_out, p1_ref, att_ref, lse_ref, sent_ref, keep_ref, give_ref = refs
        allowed = mask_ref[...] > 0.0
        kv_all = jnp.concatenate([r[...] for r in kv_refs], axis=0)
        keys, values = kv_all[:, :width], kv_all[:, width:]
        query = q_ref[...]
        mixed = jnp.zeros((rows, width), f32)
        logs = jnp.zeros((rows, 128), f32)
        lane = lax.broadcasted_iota(jnp.int32, (rows, 128), 1)
        for head in range(heads):
            inside = head_lanes((rows, width), head)
            scores = mm(jnp.where(inside, query, 0), keys, NT) * HD ** (-0.5)
            scores = jnp.where(allowed, scores, -1e30)
            top = jnp.max(scores, axis=-1, keepdims=True)
            log_total = top + jnp.log(jnp.sum(jnp.exp(scores - top), axis=-1, keepdims=True))
            weights = jnp.exp(scores - log_total).astype(bf16)
            mixed = jnp.where(inside, mm(weights, values), mixed)
            logs = jnp.where(lane == head, log_total, logs)
        att = mixed.astype(bf16)
        att_ref[...] = att
        sent_ref[:, :half] = p1_ref[:, half:]
        sent_ref[:, half : half + width] = att
        if pad:
            sent_ref[:, half + width :] = jnp.zeros((rows, pad), bf16)
        lse_ref[...] = logs
        split_halves(mm(att, w_out[layer]), keep_ref, give_ref)

    return call(
        kernel,
        [((rows, width), bf16), ((rows, 128), f32), ((rows, half + width + pad), bf16)]
        + split_shapes(rows),
        [q, *kv_parts, mask, params["w_out"], picked1],
    )


def feed_forward(hidden, pair, layer, params):
    rows = hidden.shape[0]
    half = D // 2
    inner = params["w_up"].shape[2]

    def kernel(h_ref, own_ref, other_ref, g_ref, b_ref, f_ref, q_ref, up, down,
               mid_ref, slope_ref, sent_ref, kept_ref, keep_ref, give_ref):
        small = (g_ref, b_ref, f_ref, q_ref)
        mid = h_ref[...] + joined(own_ref, other_ref) + bias(small, layer, 1)
        mid_ref[...] = mid
        hat, _ = normalize(mid)
        act2 = (hat * gain(small, layer, 1) + bias(small, layer, 2)).astype(bf16)
        pre = mm(act2, up[layer]) + ff_bias_row(small, layer)
        value, slope = gelu_pair(pre)
        act3 = value.astype(bf16)
        split_halves(mm(act3, down[layer]), keep_ref, give_ref)
        slope_ref[...] = slope
        kept_ref[...], sent_ref[:, :half] = picked_halves(act2)
        sent_ref[:, half:] = act3

    return call(
        kernel,
        [
            ((rows, D), f32),
            ((rows, inner), f32),
            ((rows, half + inner), bf16),
            ((rows, half), bf16),
        ]
        + split_shapes(rows),
        [hidden, *pair]
        + [*params["small"], params["w_up"], params["w_down"]],
    )


def last_rows(mid, pair, params, own_rows):
    def kernel(mid_ref, own_ref, other_ref, biases, out_ref, all_ref):
        own = mid_ref.shape[0] // 2
        total = mid_ref[...] + joined(own_ref.at[own:], other_ref.at[own:])
        all_ref[...] = total + biases[LAYERS - 1, 3:4]
        start = pl.multiple_of(lax.axis_index("tensor") * own_rows, own_rows)
        out_ref[...] = all_ref[pl.ds(start, own_rows), :].astype(bf16)

    args = [mid, *pair, params["small"][1]]
    return call(kernel, [((own_rows, D), bf16), (mid.shape, f32)], args)[0]


def norm1_grad(gmid_ref, own_ref, other_ref, h_ref, gains, layer):
    d_norm = joined(own_ref, other_ref)
    hat, rstd = normalize(h_ref[...])
    grad = gmid_ref[...] + norm_bwd(d_norm, hat, rstd, gains[layer, 0:1])
    return grad, column_sum(d_norm * hat), column_sum(d_norm)


def mlp_grad(grad, layer, refs, outs):
    slope_ref, up, down = refs
    sent_ref, small_ref, kept_ref, keep_ref, give_ref = outs
    half = D // 2
    grad_b = grad.astype(bf16)
    d_pre = mm(grad_b, down[layer], NT) * slope_ref[...]
    pre_b = d_pre.astype(bf16)
    split_halves(mm(pre_b, up[layer], NT), keep_ref, give_ref)
    kept_ref[...], sent_ref[:, :half] = picked_halves(grad_b)
    sent_ref[:, half:] = pre_b
    small_ref[0:1, :] = column_sum(d_pre)
    small_ref[1:2, :] = column_sum(grad)


def mlp_outs(rows, inner):
    assert inner == D
    return [
        ((rows, D), f32),
        ((rows, D // 2 + inner), bf16),
        ((8, D), f32),
        ((rows, D // 2), bf16),
    ] + split_shapes(rows)


def mlp_grad_last(pieces, slope, params):
    count = len(pieces)
    rows, inner = slope.shape

    def kernel(*refs):
        ins, outs = refs[: count + 3], refs[count + 3 :]
        place_pieces(ins[:count], outs[0])
        outs[2][...] = jnp.zeros((8, D), f32)
        mlp_grad(outs[0][...], LAYERS - 1, ins[count:], outs[1:])

    return call(
        kernel,
        mlp_outs(rows, inner),
        [*pieces, slope, params["w_up"], params["w_down"]],
    )


def mlp_grad_next(gmid, pair, hidden, slope, layer, params):
    rows, inner = slope.shape

    def kernel(gmid_ref, own_ref, other_ref, h_ref, gains, *refs):
        ins, outs = refs[:3], refs[3:]
        grad, g_gain, g_bias = norm1_grad(gmid_ref, own_ref, other_ref, h_ref, gains, layer + 1)
        outs[0][...] = grad
        outs[2][...] = jnp.zeros((8, D), f32)
        mlp_grad(grad, layer, ins, outs[1:])
        outs[2][2:3, :] = g_gain
        outs[2][3:4, :] = g_bias

    return call(
        kernel,
        mlp_outs(rows, inner),
        [gmid, *pair, hidden, params["small"][0], slope, params["w_up"], params["w_down"]],
    )


def attend_grad(grad, pair, mid, q, kv_parts, mask, att, lse, layer, params):
    rows, width = q.shape
    heads = width // HD
    back = SPAN - 1

    def kernel(g_ref, own_ref, other_ref, mid_ref, q_ref, *refs):
        kv_refs, refs = refs[:SPAN], refs[SPAN:]
        mask_ref, att_ref, lse_ref, gains, w_out = refs[:5]
        gmid_ref, picked_ref, dq_ref, dkv_ref, small_ref = refs[5:10]
        away_refs = refs[10:]
        d_norm = joined(own_ref, other_ref)
        hat, rstd = normalize(mid_ref[...])
        gmid = g_ref[...] + norm_bwd(d_norm, hat, rstd, gains[layer, 1:2])
        gmid_ref[...] = gmid
        mid_b = gmid.astype(bf16)
        d_att = mm(mid_b, w_out[layer], NT).astype(bf16)
        allowed = mask_ref[...] > 0.0
        kv_all = jnp.concatenate([r[...] for r in kv_refs], axis=0)
        keys, values = kv_all[:, :width], kv_all[:, width:]
        query, logs = q_ref[...], lse_ref[...]
        weighed = d_att.astype(f32) * att_ref[...].astype(f32)
        d_query = jnp.zeros((rows, width), f32)
        d_keys = jnp.zeros((SPAN * rows, width), f32)
        d_values = jnp.zeros((SPAN * rows, width), f32)
        for head in range(heads):
            inside = head_lanes((rows, width), head)
            query_h = jnp.where(inside, query, 0)
            d_att_h = jnp.where(inside, d_att, 0)
            scores = mm(query_h, keys, NT) * HD ** (-0.5)
            scores = jnp.where(allowed, scores, -1e30)
            probs = jnp.exp(scores - logs[:, head : head + 1])
            delta = jnp.sum(jnp.where(inside, weighed, 0.0), axis=-1, keepdims=True)
            d_prob = mm(d_att_h, values, NT)
            d_score = (probs * (d_prob - delta) * HD ** (-0.5)).astype(bf16)
            d_query = jnp.where(inside, mm(d_score, keys), d_query)
            d_keys = d_keys + mm(d_score, query_h, TN)
            d_values = d_values + mm(probs.astype(bf16), d_att_h, TN)
        d_kv = jnp.concatenate([d_keys, d_values], axis=1)
        dq_ref[...] = d_query
        dkv_ref[...] = d_kv[back * rows :]
        for distance in range(1, SPAN):
            block = back - distance
            away_refs[distance - 1][...] = d_kv[block * rows : (block + 1) * rows].astype(bf16)
        half = D // 2
        picked_ref[:, :half], picked_ref[:, half:] = picked_halves(mid_b)
        small_ref[...] = jnp.zeros((8, D), f32)
        small_ref[0:1, :] = column_sum(d_norm * hat)
        small_ref[1:2, :] = column_sum(d_norm)
        small_ref[2:3, :] = column_sum(gmid)

    return call(
        kernel,
        [
            ((rows, D), f32),
            ((rows, D), bf16),
            ((rows, width), f32),
            ((rows, 2 * width), f32),
            ((8, D), f32),
        ]
        + [((rows, 2 * width), bf16)] * back,
        [grad, *pair, mid, q, *kv_parts, mask, att, lse]
        + [params["small"][0], params["w_out"]],
    )


def project_grad(dq, dkv, arrived, picked, layer, params, more=()):
    rows, width = dq.shape
    half = D // 2
    pad = -(half + 3 * width) % 128

    def kernel(dq_ref, dkv_ref, *refs):
        near, refs = refs[: SPAN - 1], refs[SPAN - 1 :]
        picked_ref, w_qkv = refs[:2]
        sent_ref, small_ref, keep_ref, give_ref = refs[-4:]
        d_kv = dkv_ref[...]
        for ref in near:
            d_kv = d_kv + ref[...].astype(f32)
        d_query = dq_ref[...]
        query_b, kv_b = d_query.astype(bf16), d_kv.astype(bf16)
        part = mm(kv_b, w_qkv[layer, width:]) + mm(query_b, w_qkv[layer, :width])
        own = rows // 2
        split_halves(part, keep_ref.at[:own], give_ref.at[:own])
        for ref, source in zip((keep_ref, give_ref), refs[2:-4]):
            ref[own:, :] = source[...]
        sent_ref[:, :half] = picked_ref[:, half:]
        sent_ref[:, half : half + 2 * width] = kv_b
        sent_ref[:, half + 2 * width : half + 3 * width] = query_b
        if pad:
            sent_ref[:, half + 3 * width :] = jnp.zeros((rows, pad), bf16)
        small_ref[...] = jnp.zeros((8, D), f32)
        small_ref[0:1, :width] = column_sum(d_query)
        small_ref[1:2, :width] = column_sum(d_kv)[:, width:]

    return call(
        kernel,
        [((rows, half + 3 * width + pad), bf16), ((8, D), f32)]
        + split_shapes(rows * (2 if more else 1)),
        [dq, dkv, *arrived, picked, params["w_qkv"], *more],
    )


def small_rows(count):
    rows = 8 * LAYERS + LAYERS * count
    return rows + -rows % 8


def local_small(keep, give, hidden, mlp_small, att_small, qv_small, count, width):
    share = 1.0 / count

    def kernel(keep_ref, give_ref, h_ref, *refs):
        mlp, att, qv, out = refs[:LAYERS], refs[LAYERS : 2 * LAYERS], refs[2 * LAYERS : -1], refs[-1]
        mine = lax.axis_index("tensor")
        own = h_ref.shape[0] // 2
        part = joined(keep_ref.at[:own], give_ref.at[:own])
        hat, _ = normalize(h_ref[...])
        out[...] = jnp.zeros(out.shape, f32)
        for layer in range(LAYERS):
            gain1 = column_sum(part * hat) if layer == 0 else mlp[layer - 1][2:3, :] * share
            bias1 = column_sum(part) if layer == 0 else mlp[layer - 1][3:4, :] * share
            at = 2 * layer
            out[at : at + 1, :] = gain1
            out[at + 1 : at + 2, :] = att[layer][0:1, :] * share
            at = 2 * LAYERS + 4 * layer
            out[at : at + 1, :] = bias1
            out[at + 1 : at + 2, :] = att[layer][2:3, :] * share
            out[at + 2 : at + 3, :] = att[layer][1:2, :] * share
            out[at + 3 : at + 4, :] = mlp[layer][1:2, :] * share
            for target in range(count):
                here = mine == target
                at = 6 * LAYERS + 2 * layer
                lanes = slice(target * width, (target + 1) * width)
                out[at : at + 2, lanes] = jnp.where(here, qv[layer][0:2, :width], 0.0)
                at = 8 * LAYERS + layer * count + target
                out[at : at + 1, :] = jnp.where(here, mlp[layer][0:1, :], 0.0)

    args = [keep, give, hidden, *mlp_small, *att_small, *qv_small]
    return call(kernel, [((small_rows(count), D), f32)], args)[0]


def first_grad(gmid, pair, hidden, params, own_rows):
    def kernel(gmid_ref, own_ref, other_ref, h_ref, gains, in_ref, g_ref):
        own = h_ref.shape[0] // 2
        near, away = own_ref.at[:own], other_ref.at[:own]
        g_ref[...] = norm1_grad(gmid_ref, near, away, h_ref, gains, 0)[0]
        start = pl.multiple_of(lax.axis_index("tensor") * own_rows, own_rows)
        in_ref[...] = g_ref[pl.ds(start, own_rows), :].astype(bf16)

    args = [gmid, *pair, hidden, params["small"][0]]
    return call(kernel, [((own_rows, D), bf16), (gmid.shape, f32)], args)[0]


def small_outs(total, other, count):
    def kernel(total_ref, other_ref, gains, biases, qv, ffb):
        both = total_ref[...] + other_ref[...]
        for layer in range(LAYERS):
            gains[layer] = both[2 * layer : 2 * layer + 2]
            at = 2 * LAYERS + 4 * layer
            biases[layer] = both[at : at + 4]
            at = 6 * LAYERS + 2 * layer
            qv[layer] = both[at : at + 2]
            for target in range(count):
                at = 8 * LAYERS + layer * count + target
                ffb[layer : layer + 1, target * D : (target + 1) * D] = both[at : at + 1]

    return call(
        kernel,
        [
            ((LAYERS, 2, D), f32),
            ((LAYERS, 4, D), f32),
            ((LAYERS, 2, D), f32),
            ((LAYERS, count * D), f32),
        ],
        [total, other],
    )


def split_rows(total, bit, block, send_ref, keep_ref):
    mine = lax.axis_index("dp")
    high = jnp.where((mine & bit) != 0, 1, 0)
    pairs = total.shape[0] // (2 * block)
    for pair in range(pairs):
        for which in range(2):
            rows = total[(2 * pair + which) * block : (2 * pair + which + 1) * block]
            out = slice(pair * block, (pair + 1) * block)

            @pl.when(high == which)
            def _():
                keep_ref[out, :] = rows

            @pl.when(high != which)
            def _():
                send_ref[out, :] = rows.astype(bf16)


def split_plain(total, bit, block):
    pairs = total.shape[0] // (2 * block)
    split = total.reshape(pairs, 2, block, total.shape[1])
    high = jnp.where((lax.axis_index("dp") & bit) != 0, 1, 0)
    send = lax.dynamic_index_in_dim(split, 1 - high, 1, keepdims=False)
    keep = lax.dynamic_index_in_dim(split, high, 1, keepdims=False)
    return send.reshape(-1, total.shape[1]).astype(bf16), keep.reshape(-1, total.shape[1])


class Halving:
    def __init__(self, products, wide):
        self.products, self.wide = products, wide
        self.bits = [bit for bit in bits_of("dp") if bit != lax.axis_size("dp") // 4]
        self.block = D // lax.axis_size("dp")
        self.place = 0

    def begin(self, sources):
        half = D // 2
        flat = [array for source in sources for array in source]
        shape = (half // 2, self.wide)
        spots = self.products

        def products_of(refs):
            done = []
            for (la, kept_at, sent_at), (ra, r0, r1) in spots:
                kept = refs[3 * la + 2][:, kept_at : kept_at + half]
                given = refs[3 * la + 1][:, sent_at : sent_at + half]
                left = jnp.concatenate([kept, given], axis=0)
                right = [refs[3 * ra][:, r0:r1], refs[3 * ra + 1][:, r0:r1]]
                done.append(mm(left, jnp.concatenate(right, axis=0), TN))
            return jnp.concatenate(done, axis=1)

        bit, block, count = self.bits[0], self.block, len(flat)
        if block % 16:

            def kernel(*refs):
                refs[count][...] = products_of(refs)

            total = call(kernel, [((half, self.wide), f32)], flat)[0]
            self.send, self.keep = split_plain(total, bit, block)
        else:

            def kernel(*refs):
                split_rows(products_of(refs), bit, block, refs[count], refs[count + 1])

            self.send, self.keep = call(kernel, [(shape, bf16), (shape, f32)], flat)

    def launch(self, *gates):
        send = after(self.send, *gates) if gates else self.send
        self.arrived = swapped(send, "dp", self.bits[self.place])

    def absorb(self):
        self.place += 1
        bit, block = self.bits[self.place], self.block
        if block % 16:
            total = self.keep + self.arrived.astype(f32)
            self.send, self.keep = split_plain(total, bit, block)
            return

        def kernel(keep_ref, arrived_ref, send_ref, kept_ref):
            total = keep_ref[...] + arrived_ref[...].astype(f32)
            split_rows(total, bit, block, send_ref, kept_ref)

        shape = (self.keep.shape[0] // 2, self.wide)
        args = [self.keep, self.arrived]
        self.send, self.keep = call(kernel, [(shape, bf16), (shape, f32)], args)

    def finish(self):
        while self.place < len(self.bits) - 1:
            self.absorb()
            self.launch()
        return [self.keep, self.arrived]


def mlp_outputs(parts, block, inner):
    def kernel(*refs):
        up, down = refs[-2:]
        for layer in range(LAYERS):
            total = refs[2 * layer][...] + refs[2 * layer + 1][...].astype(f32)
            up[layer] = total[:, :inner]
            down[layer] = total[:, inner:]

    args = [a for pair in parts for a in pair]
    return call(kernel, [((LAYERS, block, inner), f32)] * 2, args)


def att_outputs(parts, block, width):
    def kernel(*refs):
        qkv, out = refs[-2:]
        for layer in range(LAYERS):
            total = refs[2 * layer][...] + refs[2 * layer + 1][...].astype(f32)
            qkv[layer, 0] = total[:, 2 * width : 3 * width]
            qkv[layer, 1] = total[:, :width]
            qkv[layer, 2] = total[:, width : 2 * width]
            out[layer] = total[:, 3 * width :].T

    args = [a for pair in parts for a in pair]
    return call(
        kernel,
        [((LAYERS, 3, block, width), f32), ((LAYERS, width, block), f32)],
        args,
    )


def shards(
    tokens, cotangent, segments, w_qkv, qv_bias, w_out, w_up, w_down, ff_bias, gains, biases
):
    tensor_count = lax.axis_size("tensor")
    dp_count = lax.axis_size("dp")
    own_rows = tokens.shape[0]
    rows = own_rows * tensor_count
    width = w_out.shape[1]
    inner = w_up.shape[2]
    half = D // 2
    block = D // dp_count
    joint = w_qkv.transpose(0, 2, 3, 1).reshape(LAYERS, 3 * width, D)
    params = {
        "small": [gains, biases, ff_bias, qv_bias],
        "w_qkv": joint,
        "w_out": w_out,
        "w_up": w_up,
        "w_down": w_down,
    }
    mask = allowed_rows(segments, rows)
    near = dp_count // 4

    def paired(sent, kept, gate):
        return [sent, swapped(after(sent, gate), "dp", near), kept]

    mlp_work = [
        Halving([((0, 0, 0), (1, half, half + inner)), ((1, 0, 0), (0, half, half + inner))], 2 * inner)
        for _ in range(LAYERS)
    ]
    att_work = [
        Halving([((0, 0, 0), (1, half, half + 3 * width)), ((1, 0, 0), (0, half, half + width))], 4 * width)
        for _ in range(LAYERS)
    ]
    token_pieces = gathered(tokens)
    token_pieces[-1] = after(token_pieces[-1], mask)
    saved, rows_a, rows_b = [], [None] * LAYERS, [None] * LAYERS
    cot_pieces = None
    mid = pair = None
    for layer in range(LAYERS):
        if layer == 0:
            hidden, picked1, q, kv = project_first(tokens, token_pieces[1:], params)
        else:
            hidden, picked1, q, kv = project_next(mid, pair, layer, params)
        kv_parts = [shifted(kv, "dp", distance) for distance in range(SPAN - 1, 0, -1)] + [kv]
        if layer:
            q = after(q, rows_a[layer - 1][1], rows_b[layer - 1][1])
        att, lse, sent_a, keep, give = attend(q, kv_parts, mask, picked1, layer, params)

        def launch_a(gate):
            nonlocal cot_pieces
            rows_a[layer] = paired(sent_a, picked1, gate)
            if layer == 0:
                cot_pieces = gathered(after(cotangent, gate))

        pair = exchanged(keep, give, launch_a)
        mid, slope, sent_b, kept_b, keep, give = feed_forward(hidden, pair, layer, params)
        saved.append((hidden, q, kv_parts, att, lse, mid, slope))
        if layer < LAYERS - 1:

            def launch_b(gate):
                rows_b[layer] = paired(sent_b, kept_b, gate)

            pair = exchanged(keep, give, launch_b)
            pair[0] = after(pair[0], cot_pieces[-1])
    last_keep, last_give = keep, give

    mlp_small, att_small, qv_small = ([None] * LAYERS for _ in range(3))
    gmid = last_pair = None
    for layer in range(LAYERS - 1, -1, -1):
        last = layer == LAYERS - 1
        later = layer + 1
        hidden, q, kv_parts, att, lse, mid, slope = saved[layer]
        if last:
            grad, sent1, mlp_small[layer], kept1, keep, give = mlp_grad_last(
                cot_pieces, slope, params
            )
        else:
            grad, sent1, mlp_small[layer], kept1, keep, give = mlp_grad_next(
                gmid, pair, saved[layer + 1][0], slope, layer, params
            )
        rows_1 = None

        def launch_1(gate):
            nonlocal rows_1
            if last:
                rows_b[layer] = paired(sent_b, kept_b, gate)
            rows_1 = paired(sent1, kept1, gate)

        pair = exchanged(keep, give, launch_1)
        if last:
            pair[0] = after(pair[0], rows_a[layer][1])
        gmid, picked, dq, dkv, att_small[layer], *away = attend_grad(
            grad, pair, mid, q, kv_parts, mask, att, lse, layer, params
        )
        arrived = [shifted(a, "dp", -(place + 1)) for place, a in enumerate(away)]
        mlp_work[layer].begin([rows_b[layer], rows_1])
        due = [mlp_work[layer].send]
        if last:
            mlp_work[layer].launch()
        else:
            mlp_work[later].absorb()
            due += [mlp_work[later].send, att_work[later].send]
        sent2, qv_small[layer], keep, give = project_grad(
            dq,
            after(dkv, *due),
            arrived,
            picked,
            layer,
            params,
            () if last else (last_keep, last_give),
        )
        rows_2 = None

        def launch_2(gate):
            nonlocal rows_2
            rows_2 = paired(sent2, picked, gate)

        if last:
            pair = exchanged(keep, give, launch_2)
            att_work[layer].begin([rows_a[layer], rows_2])
    small = local_small(
        keep, give, saved[0][0], mlp_small, att_small, qv_small, tensor_count, width
    )
    rows_2 = [sent2, swapped(sent2, "dp", near), picked]
    mlp_work[1].launch()
    att_work[1].launch()
    mlp_work[0].launch()
    bits = bits_of("tensor")
    dp_bits = bits_of("dp")
    dp_bits = [near] + [bit for bit in dp_bits if bit != near]
    total = keep
    for place, bit in enumerate(bits):
        rounded = give if place == 0 else total.astype(bf16)
        other = swapped(rounded, "tensor", bit)
        total = (total if place == 0 else rounded.astype(f32)) + other.astype(f32)
        small = small + swapped(small, "tensor", bit)
        total, small = lax.optimization_barrier((total, small))
    total = after(total, mlp_work[1].arrived, att_work[1].arrived)
    att_work[1].absorb()
    att_work[1].launch()
    rounded = total.astype(bf16)
    pair = [rounded, swapped(rounded, "tensor", bits[0])]
    small = small + swapped(after(small, total), "dp", dp_bits[0])
    pair[0] = after(pair[0], small)
    input_grad = first_grad(gmid, pair, saved[0][0], params, own_rows)
    result = last_rows(saved[-1][5], pair, params, own_rows)
    rows_2[1] = after(rows_2[1], input_grad, result)
    att_work[0].begin([rows_a[0], rows_2])
    att_work[0].launch()
    mlp_work[0].arrived = after(mlp_work[0].arrived, att_work[0].send, att_work[1].arrived)
    mlp_work[0].absorb()
    mlp_work[0].launch()
    small = after(small, mlp_work[0].send)
    for bit in dp_bits[1:-1]:
        small = small + swapped(small, "dp", bit)
    att_work[0].absorb()
    att_work[0].launch()
    small_grads = small_outs(small, swapped(small, "dp", dp_bits[-1]), tensor_count)
    mlp_parts = [work.finish() for work in mlp_work]
    att_parts = [work.finish() for work in att_work]
    g_up, g_down = mlp_outputs(mlp_parts, block, inner)
    g_qkv, g_out = att_outputs(att_parts, block, width)
    return (
        result,
        input_grad,
        g_qkv.transpose(0, 2, 1, 3),
        g_out,
        g_up,
        g_down.transpose(0, 2, 1),
        *small_grads,
    )


def solution(mesh):
    return jax.shard_map(
        shards,
        mesh=mesh,
        in_specs=(
            P(("dp", "tensor"), None),
            P(("dp", "tensor"), None),
            P(),
            P(None, None, None, "tensor"),
            P(None, None, "tensor"),
            P(None, "tensor", None),
            P(None, None, "tensor"),
            P(None, "tensor", None),
            P(None, "tensor"),
            P(),
            P(),
        ),
        out_specs=(
            P(("dp", "tensor"), None),
            P(("dp", "tensor"), None),
            P(None, "dp", None, "tensor"),
            P(None, "tensor", "dp"),
            P(None, "dp", "tensor"),
            P(None, "tensor", "dp"),
            P(),
            P(),
            P(),
            P(),
        ),
        check_vma=False,
    )
```

```python
import jax
import jax.numpy as jnp
from jax import lax
from jax.experimental import pallas as pl
from jax.experimental.pallas import tpu as pltpu
from jax.sharding import PartitionSpec as P

D = 768
HD = 64
FF = 3072
LAYERS = 2
SPAN = 4

epsilon = 1e-05
gelu_c = 0.7978845608028654
f32 = jnp.float32
bf16 = jnp.bfloat16
VMEM_LIMIT = 28 * 1024 * 1024


def shifted(array, axis, by):
    length = lax.axis_size(axis)
    pairs = [(i, i + by) for i in range(length) if 0 <= i + by < length]
    return lax.ppermute(array, axis, pairs)


def swapped(array, axis, bit):
    length = lax.axis_size(axis)
    return lax.ppermute(array, axis, [(i, i ^ bit) for i in range(length)])


def bits_of(axis):
    length = lax.axis_size(axis)
    found, bit = [], 1
    while bit < length:
        found.append(bit)
        bit *= 2
    assert bit == length
    return found


def call(kernel, outs, args, flops=1, moved=1):
    spec = pl.BlockSpec(memory_space=pltpu.VMEM)
    shapes = [jax.ShapeDtypeStruct(shape, dtype) for shape, dtype in outs]
    return pl.pallas_call(
        kernel,
        out_shape=shapes,
        in_specs=[spec] * len(args),
        out_specs=[spec] * len(outs),
        compiler_params=pltpu.CompilerParams(vmem_limit_bytes=VMEM_LIMIT),
        cost_estimate=pl.CostEstimate(
            flops=int(flops), bytes_accessed=int(moved), transcendentals=0
        ),
    )(*args)


def picked_halves(rows):
    wide = rows.shape[1] // 4
    high = (lax.axis_index("dp") // (lax.axis_size("dp") // 4)) % 2 == 1
    quarters = [rows[:, k * wide : (k + 1) * wide] for k in range(4)]
    return tuple(
        jnp.concatenate(
            [jnp.where(high, quarters[k + one], quarters[k + zero]) for k in (0, 2)], axis=1
        )
        for zero, one in ((0, 1), (1, 0))
    )


def mm(left, right, contract=((1,), (0,))):
    return lax.dot_general(left, right, (contract, ((), ())), preferred_element_type=f32)


NT = ((1,), (1,))
TN = ((0,), (0,))


def normalize(values_in):
    mean_v = jnp.mean(values_in, axis=-1, keepdims=True)
    centred = values_in - mean_v
    var_v = jnp.mean(centred * centred, axis=-1, keepdims=True)
    rstd = lax.rsqrt(var_v + epsilon)
    return (centred * rstd, rstd)


def norm_bwd(grad_in, normed, rstd, gain):
    scaled = grad_in * gain
    inner = jnp.mean(scaled, axis=-1, keepdims=True)
    along = jnp.mean(scaled * normed, axis=-1, keepdims=True)
    return rstd * (scaled - inner - normed * along)


def gain(small, layer, which):
    return small[0][layer, which : which + 1]


def bias(small, layer, which):
    return small[1][layer, which : which + 1]


def ff_bias_row(small, layer):
    return small[2][layer : layer + 1]


def qv_bias(small, layer, which):
    return small[3][layer, which : which + 1]


def column_sum(values_in):
    return jnp.sum(values_in, axis=0, keepdims=True)


def gelu_pair(pre_act):
    inner = gelu_c * (pre_act + 0.044715 * pre_act * pre_act * pre_act)
    tanh_v = jnp.tanh(inner)
    value_out = 0.5 * pre_act * (1.0 + tanh_v)
    slope = 0.5 * (1.0 + tanh_v) + 0.5 * pre_act * (1.0 - tanh_v * tanh_v) * gelu_c * (
        1.0 + 3.0 * 0.044715 * pre_act * pre_act
    )
    return (value_out, slope)


def joined(own_ref, other_ref):
    high = (lax.axis_index("tensor") & 1) == 1
    own, other = own_ref[...].astype(f32), other_ref[...].astype(f32)
    return jnp.concatenate(
        [jnp.where(high, other, own), jnp.where(high, own, other)], axis=0
    )


def split_halves(total, keep_ref, give_ref):
    half = total.shape[0] // 2
    high = (lax.axis_index("tensor") & 1) == 1
    low_rows, high_rows = total[:half], total[half:]
    keep_ref[...] = jnp.where(high, high_rows, low_rows)
    give_ref[...] = jnp.where(high, low_rows, high_rows).astype(bf16)


def place_pieces(pieces, out_ref):
    mine = lax.axis_index("tensor")
    rows = pieces[0].shape[0]
    for number, piece in enumerate(pieces):
        start = pl.multiple_of((mine ^ number) * rows, rows)
        out_ref[pl.ds(start, rows), :] = piece[...].astype(out_ref.dtype)


def gathered(piece):
    pieces = {0: piece}
    for bit in bits_of("tensor")[::-1]:
        for number in list(pieces):
            pieces[number ^ bit] = swapped(pieces[number], "tensor", bit)
    return [pieces[number] for number in range(len(pieces))]


def after(value, *others):
    return lax.optimization_barrier((value, *others))[0]


def exchanged(keep, give, launch=None, due=()):
    bits = bits_of("tensor")
    total = keep + swapped(give, "tensor", bits[0]).astype(f32)
    for bit in bits[1:]:
        rounded = after(total.astype(bf16), *due)
        other = swapped(rounded, "tensor", bit)
        if launch is not None and bit == bits[-1]:
            launch(rounded)
        total = rounded.astype(f32) + other.astype(f32)
    rounded = total.astype(bf16)
    return [rounded, swapped(rounded, "tensor", bits[0])]


def project_rows(hidden, layer, refs, outs):
    small, w_qkv = refs[:4], refs[4]
    h_ref, picked_ref, q_ref, kv_ref = outs
    width = q_ref.shape[1]
    hat, _ = normalize(hidden)
    act = (hat * gain(small, layer, 0) + bias(small, layer, 0)).astype(bf16)
    kv = mm(act, w_qkv[layer, width:], NT)
    values = kv[:, width:] + qv_bias(small, layer, 1)
    kv_ref[...] = jnp.concatenate([kv[:, :width], values], axis=1).astype(bf16)
    query = mm(act, w_qkv[layer, :width], NT)
    q_ref[...] = (query + qv_bias(small, layer, 0)).astype(bf16)
    half = act.shape[1] // 2
    picked_ref[:, :half], picked_ref[:, half:] = picked_halves(act)


def project_first(tokens, pieces, params):
    count = len(pieces)
    own_rows = tokens.shape[0]
    rows = (count + 1) * own_rows
    width = params["w_out"].shape[1]
    gains, biases, _, qv = params["small"]
    far = [tokens, gains, biases, qv, params["w_qkv"]]
    many = len(far)

    def kernel(*refs):
        ins, near = refs[:count], refs[count : count + many]
        outs = refs[-4:]
        place_pieces([near[0], *ins], outs[0])
        small = (near[1], near[2], None, near[3])
        project_rows(outs[0][...], 0, [*small, near[4]], outs)

    def whole(array):
        zeros = (0,) * array.ndim
        return pl.BlockSpec(array.shape, lambda step: zeros)

    spec = pl.BlockSpec(memory_space=pltpu.VMEM)
    return pl.pallas_call(
        kernel,
        grid=(1,),
        out_shape=[
            jax.ShapeDtypeStruct((rows, D), f32),
            jax.ShapeDtypeStruct((rows, D), bf16),
            jax.ShapeDtypeStruct((rows, width), bf16),
            jax.ShapeDtypeStruct((rows, 2 * width), bf16),
        ],
        in_specs=[spec] * count
        + [whole(a) for a in far[:-1]]
        + [pl.BlockSpec((1,) + far[-1].shape[1:], lambda step: (0, 0, 0))],
        out_specs=[spec] * 4,
        compiler_params=pltpu.CompilerParams(vmem_limit_bytes=VMEM_LIMIT),
        cost_estimate=pl.CostEstimate(flops=1, bytes_accessed=1, transcendentals=0),
    )(*pieces, *far)


def project_next(mid, pair, layer, params):
    rows = mid.shape[0]
    width = params["w_out"].shape[1]

    def kernel(mid_ref, own_ref, other_ref, *refs):
        ins, outs = refs[:5], refs[5:]
        hidden = mid_ref[...] + joined(own_ref, other_ref) + bias(ins, layer - 1, 3)
        outs[0][...] = hidden
        project_rows(hidden, layer, ins, outs)

    return call(
        kernel,
        [((rows, D), f32), ((rows, D), bf16), ((rows, width), bf16), ((rows, 2 * width), bf16)],
        [mid, *pair, *params["small"], params["w_qkv"]],
    )


def head_lanes(shape, head):
    lane = lax.broadcasted_iota(jnp.int32, shape, 1)
    return (lane >= head * HD) & (lane < (head + 1) * HD)


def allowed_rows(segments, rows):
    def kernel(seg_ref, out_ref):
        mine = lax.axis_index("dp")
        here = seg_ref[:, pl.ds(pl.multiple_of(mine * rows, rows), rows)].astype(f32)
        query_seg = jnp.broadcast_to(here, (rows, rows)).T
        query = lax.broadcasted_iota(jnp.int32, (rows, rows), 0)
        key = lax.broadcasted_iota(jnp.int32, (rows, rows), 1)
        for place in range(SPAN):
            behind = SPAN - 1 - place
            start = jnp.maximum(mine - behind, 0) * rows
            key_seg = seg_ref[:, pl.ds(pl.multiple_of(start, rows), rows)].astype(f32)
            same = (query_seg == key_seg) & (key <= query + behind * rows)
            seen = jnp.where(same, 1.0, 0.0) * jnp.where(mine >= behind, 1.0, 0.0)
            out_ref[:, place * rows : (place + 1) * rows] = seen

    row = segments[None, :]
    return call(kernel, [((rows, SPAN * rows), f32)], [row], 1e10, 1e8)[0]


def split_shapes(rows):
    return [((rows // 2, D), f32), ((rows // 2, D), bf16)]


def attend(q, kv_parts, mask, picked1, layer, params):
    rows, width = q.shape
    half = D // 2
    pad = -(half + width) % 128
    heads = width // HD

    def kernel(q_ref, *refs):
        kv_refs, refs = refs[:SPAN], refs[SPAN:]
        mask_ref, w_out, p1_ref, att_ref, lse_ref, sent_ref, keep_ref, give_ref = refs
        allowed = mask_ref[...] > 0.0
        kv_all = jnp.concatenate([r[...] for r in kv_refs], axis=0)
        keys, values = kv_all[:, :width], kv_all[:, width:]
        query = q_ref[...]
        mixed = jnp.zeros((rows, width), f32)
        logs = jnp.zeros((rows, 128), f32)
        lane = lax.broadcasted_iota(jnp.int32, (rows, 128), 1)
        for head in range(heads):
            inside = head_lanes((rows, width), head)
            scores = mm(jnp.where(inside, query, 0), keys, NT) * HD ** (-0.5)
            scores = jnp.where(allowed, scores, -1e30)
            top = jnp.max(scores, axis=-1, keepdims=True)
            log_total = top + jnp.log(jnp.sum(jnp.exp(scores - top), axis=-1, keepdims=True))
            weights = jnp.exp(scores - log_total).astype(bf16)
            mixed = jnp.where(inside, mm(weights, values), mixed)
            logs = jnp.where(lane == head, log_total, logs)
        att = mixed.astype(bf16)
        att_ref[...] = att
        sent_ref[:, :half] = p1_ref[:, half:]
        sent_ref[:, half : half + width] = att
        if pad:
            sent_ref[:, half + width :] = jnp.zeros((rows, pad), bf16)
        lse_ref[...] = logs
        split_halves(mm(att, w_out[layer]), keep_ref, give_ref)

    return call(
        kernel,
        [((rows, width), bf16), ((rows, 128), f32), ((rows, half + width + pad), bf16)]
        + split_shapes(rows),
        [q, *kv_parts, mask, params["w_out"], picked1],
    )


def feed_forward(hidden, pair, layer, params):
    rows = hidden.shape[0]
    half = D // 2
    inner = params["w_up"].shape[2]

    def kernel(h_ref, own_ref, other_ref, g_ref, b_ref, f_ref, q_ref, up, down,
               mid_ref, slope_ref, sent_ref, kept_ref, keep_ref, give_ref):
        small = (g_ref, b_ref, f_ref, q_ref)
        mid = h_ref[...] + joined(own_ref, other_ref) + bias(small, layer, 1)
        mid_ref[...] = mid
        hat, _ = normalize(mid)
        act2 = (hat * gain(small, layer, 1) + bias(small, layer, 2)).astype(bf16)
        pre = mm(act2, up[layer]) + ff_bias_row(small, layer)
        value, slope = gelu_pair(pre)
        act3 = value.astype(bf16)
        split_halves(mm(act3, down[layer]), keep_ref, give_ref)
        slope_ref[...] = slope
        kept_ref[...], sent_ref[:, :half] = picked_halves(act2)
        sent_ref[:, half:] = act3

    return call(
        kernel,
        [
            ((rows, D), f32),
            ((rows, inner), f32),
            ((rows, half + inner), bf16),
            ((rows, half), bf16),
        ]
        + split_shapes(rows),
        [hidden, *pair]
        + [*params["small"], params["w_up"], params["w_down"]],
    )


def last_rows(mid, pair, params, own_rows):
    def kernel(mid_ref, own_ref, other_ref, biases, out_ref, all_ref):
        own = mid_ref.shape[0] // 2
        total = mid_ref[...] + joined(own_ref.at[own:], other_ref.at[own:])
        all_ref[...] = total + biases[LAYERS - 1, 3:4]
        start = pl.multiple_of(lax.axis_index("tensor") * own_rows, own_rows)
        out_ref[...] = all_ref[pl.ds(start, own_rows), :].astype(bf16)

    args = [mid, *pair, params["small"][1]]
    return call(kernel, [((own_rows, D), bf16), (mid.shape, f32)], args)[0]


def norm1_grad(gmid_ref, own_ref, other_ref, h_ref, gains, layer):
    d_norm = joined(own_ref, other_ref)
    hat, rstd = normalize(h_ref[...])
    grad = gmid_ref[...] + norm_bwd(d_norm, hat, rstd, gains[layer, 0:1])
    return grad, column_sum(d_norm * hat), column_sum(d_norm)


def mlp_grad(grad, layer, refs, outs):
    slope_ref, up, down = refs
    sent_ref, small_ref, kept_ref, keep_ref, give_ref = outs
    half = D // 2
    grad_b = grad.astype(bf16)
    d_pre = mm(grad_b, down[layer], NT) * slope_ref[...]
    pre_b = d_pre.astype(bf16)
    split_halves(mm(pre_b, up[layer], NT), keep_ref, give_ref)
    kept_ref[...], sent_ref[:, :half] = picked_halves(grad_b)
    sent_ref[:, half:] = pre_b
    small_ref[0:1, :] = column_sum(d_pre)
    small_ref[1:2, :] = column_sum(grad)


def mlp_outs(rows, inner):
    assert inner == D
    return [
        ((rows, D), f32),
        ((rows, D // 2 + inner), bf16),
        ((8, D), f32),
        ((rows, D // 2), bf16),
    ] + split_shapes(rows)


def mlp_grad_last(pieces, slope, params):
    count = len(pieces)
    rows, inner = slope.shape

    def kernel(*refs):
        ins, outs = refs[: count + 3], refs[count + 3 :]
        place_pieces(ins[:count], outs[0])
        outs[2][...] = jnp.zeros((8, D), f32)
        mlp_grad(outs[0][...], LAYERS - 1, ins[count:], outs[1:])

    return call(
        kernel,
        mlp_outs(rows, inner),
        [*pieces, slope, params["w_up"], params["w_down"]],
    )


def mlp_grad_next(gmid, pair, hidden, slope, layer, params):
    rows, inner = slope.shape

    def kernel(gmid_ref, own_ref, other_ref, h_ref, gains, *refs):
        ins, outs = refs[:3], refs[3:]
        grad, g_gain, g_bias = norm1_grad(gmid_ref, own_ref, other_ref, h_ref, gains, layer + 1)
        outs[0][...] = grad
        outs[2][...] = jnp.zeros((8, D), f32)
        mlp_grad(grad, layer, ins, outs[1:])
        outs[2][2:3, :] = g_gain
        outs[2][3:4, :] = g_bias

    return call(
        kernel,
        mlp_outs(rows, inner),
        [gmid, *pair, hidden, params["small"][0], slope, params["w_up"], params["w_down"]],
    )


def attend_grad(grad, pair, mid, q, kv_parts, mask, att, lse, layer, params):
    rows, width = q.shape
    heads = width // HD
    back = SPAN - 1

    def kernel(g_ref, own_ref, other_ref, mid_ref, q_ref, *refs):
        kv_refs, refs = refs[:SPAN], refs[SPAN:]
        mask_ref, att_ref, lse_ref, gains, w_out = refs[:5]
        gmid_ref, picked_ref, dq_ref, dkv_ref, small_ref = refs[5:10]
        away_refs = refs[10:]
        d_norm = joined(own_ref, other_ref)
        hat, rstd = normalize(mid_ref[...])
        gmid = g_ref[...] + norm_bwd(d_norm, hat, rstd, gains[layer, 1:2])
        gmid_ref[...] = gmid
        mid_b = gmid.astype(bf16)
        d_att = mm(mid_b, w_out[layer], NT).astype(bf16)
        allowed = mask_ref[...] > 0.0
        kv_all = jnp.concatenate([r[...] for r in kv_refs], axis=0)
        keys, values = kv_all[:, :width], kv_all[:, width:]
        query, logs = q_ref[...], lse_ref[...]
        weighed = d_att.astype(f32) * att_ref[...].astype(f32)
        d_query = jnp.zeros((rows, width), f32)
        d_keys = jnp.zeros((SPAN * rows, width), f32)
        d_values = jnp.zeros((SPAN * rows, width), f32)
        for head in range(heads):
            inside = head_lanes((rows, width), head)
            query_h = jnp.where(inside, query, 0)
            d_att_h = jnp.where(inside, d_att, 0)
            scores = mm(query_h, keys, NT) * HD ** (-0.5)
            scores = jnp.where(allowed, scores, -1e30)
            probs = jnp.exp(scores - logs[:, head : head + 1])
            delta = jnp.sum(jnp.where(inside, weighed, 0.0), axis=-1, keepdims=True)
            d_prob = mm(d_att_h, values, NT)
            d_score = (probs * (d_prob - delta) * HD ** (-0.5)).astype(bf16)
            d_query = jnp.where(inside, mm(d_score, keys), d_query)
            d_keys = d_keys + mm(d_score, query_h, TN)
            d_values = d_values + mm(probs.astype(bf16), d_att_h, TN)
        d_kv = jnp.concatenate([d_keys, d_values], axis=1)
        dq_ref[...] = d_query
        dkv_ref[...] = d_kv[back * rows :]
        for distance in range(1, SPAN):
            block = back - distance
            away_refs[distance - 1][...] = d_kv[block * rows : (block + 1) * rows].astype(bf16)
        half = D // 2
        picked_ref[:, :half], picked_ref[:, half:] = picked_halves(mid_b)
        small_ref[...] = jnp.zeros((8, D), f32)
        small_ref[0:1, :] = column_sum(d_norm * hat)
        small_ref[1:2, :] = column_sum(d_norm)
        small_ref[2:3, :] = column_sum(gmid)

    return call(
        kernel,
        [
            ((rows, D), f32),
            ((rows, D), bf16),
            ((rows, width), f32),
            ((rows, 2 * width), f32),
            ((8, D), f32),
        ]
        + [((rows, 2 * width), bf16)] * back,
        [grad, *pair, mid, q, *kv_parts, mask, att, lse]
        + [params["small"][0], params["w_out"]],
    )


def project_grad(dq, dkv, arrived, picked, layer, params, more=()):
    rows, width = dq.shape
    half = D // 2
    pad = -(half + 3 * width) % 128

    def kernel(dq_ref, dkv_ref, *refs):
        near, refs = refs[: SPAN - 1], refs[SPAN - 1 :]
        picked_ref, w_qkv = refs[:2]
        sent_ref, small_ref, keep_ref, give_ref = refs[-4:]
        d_kv = dkv_ref[...]
        for ref in near:
            d_kv = d_kv + ref[...].astype(f32)
        d_query = dq_ref[...]
        query_b, kv_b = d_query.astype(bf16), d_kv.astype(bf16)
        part = mm(kv_b, w_qkv[layer, width:]) + mm(query_b, w_qkv[layer, :width])
        own = rows // 2
        split_halves(part, keep_ref.at[:own], give_ref.at[:own])
        for ref, source in zip((keep_ref, give_ref), refs[2:-4]):
            ref[own:, :] = source[...]
        sent_ref[:, :half] = picked_ref[:, half:]
        sent_ref[:, half : half + 2 * width] = kv_b
        sent_ref[:, half + 2 * width : half + 3 * width] = query_b
        if pad:
            sent_ref[:, half + 3 * width :] = jnp.zeros((rows, pad), bf16)
        small_ref[...] = jnp.zeros((8, D), f32)
        small_ref[0:1, :width] = column_sum(d_query)
        small_ref[1:2, :width] = column_sum(d_kv)[:, width:]

    return call(
        kernel,
        [((rows, half + 3 * width + pad), bf16), ((8, D), f32)]
        + split_shapes(rows * (2 if more else 1)),
        [dq, dkv, *arrived, picked, params["w_qkv"], *more],
    )


def small_rows(count):
    rows = 8 * LAYERS + LAYERS * count
    return rows + -rows % 8


def local_small(keep, give, hidden, mlp_small, att_small, qv_small, count, width):
    share = 1.0 / count

    def kernel(keep_ref, give_ref, h_ref, *refs):
        mlp, att, qv, out = refs[:LAYERS], refs[LAYERS : 2 * LAYERS], refs[2 * LAYERS : -1], refs[-1]
        mine = lax.axis_index("tensor")
        own = h_ref.shape[0] // 2
        part = joined(keep_ref.at[:own], give_ref.at[:own])
        hat, _ = normalize(h_ref[...])
        out[...] = jnp.zeros(out.shape, f32)
        for layer in range(LAYERS):
            gain1 = column_sum(part * hat) if layer == 0 else mlp[layer - 1][2:3, :] * share
            bias1 = column_sum(part) if layer == 0 else mlp[layer - 1][3:4, :] * share
            at = 2 * layer
            out[at : at + 1, :] = gain1
            out[at + 1 : at + 2, :] = att[layer][0:1, :] * share
            at = 2 * LAYERS + 4 * layer
            out[at : at + 1, :] = bias1
            out[at + 1 : at + 2, :] = att[layer][2:3, :] * share
            out[at + 2 : at + 3, :] = att[layer][1:2, :] * share
            out[at + 3 : at + 4, :] = mlp[layer][1:2, :] * share
            for target in range(count):
                here = mine == target
                at = 6 * LAYERS + 2 * layer
                lanes = slice(target * width, (target + 1) * width)
                out[at : at + 2, lanes] = jnp.where(here, qv[layer][0:2, :width], 0.0)
                at = 8 * LAYERS + layer * count + target
                out[at : at + 1, :] = jnp.where(here, mlp[layer][0:1, :], 0.0)

    args = [keep, give, hidden, *mlp_small, *att_small, *qv_small]
    return call(kernel, [((small_rows(count), D), f32)], args)[0]


def first_grad(gmid, pair, hidden, params, own_rows):
    def kernel(gmid_ref, own_ref, other_ref, h_ref, gains, in_ref, g_ref):
        own = h_ref.shape[0] // 2
        near, away = own_ref.at[:own], other_ref.at[:own]
        g_ref[...] = norm1_grad(gmid_ref, near, away, h_ref, gains, 0)[0]
        start = pl.multiple_of(lax.axis_index("tensor") * own_rows, own_rows)
        in_ref[...] = g_ref[pl.ds(start, own_rows), :].astype(bf16)

    args = [gmid, *pair, hidden, params["small"][0]]
    return call(kernel, [((own_rows, D), bf16), (gmid.shape, f32)], args)[0]


def small_outs(total, other, count):
    def kernel(total_ref, other_ref, gains, biases, qv, ffb):
        both = total_ref[...] + other_ref[...]
        for layer in range(LAYERS):
            gains[layer] = both[2 * layer : 2 * layer + 2]
            at = 2 * LAYERS + 4 * layer
            biases[layer] = both[at : at + 4]
            at = 6 * LAYERS + 2 * layer
            qv[layer] = both[at : at + 2]
            for target in range(count):
                at = 8 * LAYERS + layer * count + target
                ffb[layer : layer + 1, target * D : (target + 1) * D] = both[at : at + 1]

    return call(
        kernel,
        [
            ((LAYERS, 2, D), f32),
            ((LAYERS, 4, D), f32),
            ((LAYERS, 2, D), f32),
            ((LAYERS, count * D), f32),
        ],
        [total, other],
    )


def split_rows(total, bit, block, send_ref, keep_ref):
    mine = lax.axis_index("dp")
    high = jnp.where((mine & bit) != 0, 1, 0)
    pairs = total.shape[0] // (2 * block)
    for pair in range(pairs):
        for which in range(2):
            rows = total[(2 * pair + which) * block : (2 * pair + which + 1) * block]
            out = slice(pair * block, (pair + 1) * block)

            @pl.when(high == which)
            def _():
                keep_ref[out, :] = rows

            @pl.when(high != which)
            def _():
                send_ref[out, :] = rows.astype(bf16)


def split_plain(total, bit, block):
    pairs = total.shape[0] // (2 * block)
    split = total.reshape(pairs, 2, block, total.shape[1])
    high = jnp.where((lax.axis_index("dp") & bit) != 0, 1, 0)
    send = lax.dynamic_index_in_dim(split, 1 - high, 1, keepdims=False)
    keep = lax.dynamic_index_in_dim(split, high, 1, keepdims=False)
    return send.reshape(-1, total.shape[1]).astype(bf16), keep.reshape(-1, total.shape[1])


class Halving:
    def __init__(self, products, wide):
        self.products, self.wide = products, wide
        self.bits = [bit for bit in bits_of("dp") if bit != lax.axis_size("dp") // 4]
        self.block = D // lax.axis_size("dp")
        self.place = 0

    def begin(self, sources):
        half = D // 2
        flat = [array for source in sources for array in source]
        shape = (half // 2, self.wide)
        spots = self.products

        def products_of(refs):
            done = []
            for (la, kept_at, sent_at), (ra, r0, r1) in spots:
                kept = refs[3 * la + 2][:, kept_at : kept_at + half]
                given = refs[3 * la + 1][:, sent_at : sent_at + half]
                left = jnp.concatenate([kept, given], axis=0)
                right = [refs[3 * ra][:, r0:r1], refs[3 * ra + 1][:, r0:r1]]
                done.append(mm(left, jnp.concatenate(right, axis=0), TN))
            return jnp.concatenate(done, axis=1)

        bit, block, count = self.bits[0], self.block, len(flat)
        if block % 16:

            def kernel(*refs):
                refs[count][...] = products_of(refs)

            total = call(kernel, [((half, self.wide), f32)], flat)[0]
            self.send, self.keep = split_plain(total, bit, block)
        else:

            def kernel(*refs):
                split_rows(products_of(refs), bit, block, refs[count], refs[count + 1])

            self.send, self.keep = call(kernel, [(shape, bf16), (shape, f32)], flat)

    def launch(self, *gates):
        send = after(self.send, *gates) if gates else self.send
        self.arrived = swapped(send, "dp", self.bits[self.place])

    def absorb(self):
        self.place += 1
        bit, block = self.bits[self.place], self.block
        if block % 16:
            total = self.keep + self.arrived.astype(f32)
            self.send, self.keep = split_plain(total, bit, block)
            return

        def kernel(keep_ref, arrived_ref, send_ref, kept_ref):
            total = keep_ref[...] + arrived_ref[...].astype(f32)
            split_rows(total, bit, block, send_ref, kept_ref)

        shape = (self.keep.shape[0] // 2, self.wide)
        args = [self.keep, self.arrived]
        self.send, self.keep = call(kernel, [(shape, bf16), (shape, f32)], args)

    def finish(self):
        while self.place < len(self.bits) - 1:
            self.absorb()
            self.launch()
        return [self.keep, self.arrived]


def mlp_outputs(parts, block, inner):
    def kernel(*refs):
        up, down = refs[-2:]
        for layer in range(LAYERS):
            total = refs[2 * layer][...] + refs[2 * layer + 1][...].astype(f32)
            up[layer] = total[:, :inner]
            down[layer] = total[:, inner:]

    args = [a for pair in parts for a in pair]
    return call(kernel, [((LAYERS, block, inner), f32)] * 2, args)


def att_outputs(parts, block, width):
    def kernel(*refs):
        qkv, out = refs[-2:]
        for layer in range(LAYERS):
            total = refs[2 * layer][...] + refs[2 * layer + 1][...].astype(f32)
            qkv[layer, 0] = total[:, 2 * width : 3 * width]
            qkv[layer, 1] = total[:, :width]
            qkv[layer, 2] = total[:, width : 2 * width]
            out[layer] = total[:, 3 * width :].T

    args = [a for pair in parts for a in pair]
    return call(
        kernel,
        [((LAYERS, 3, block, width), f32), ((LAYERS, width, block), f32)],
        args,
    )


def shards(
    tokens, cotangent, segments, w_qkv, qv_bias, w_out, w_up, w_down, ff_bias, gains, biases
):
    tensor_count = lax.axis_size("tensor")
    dp_count = lax.axis_size("dp")
    own_rows = tokens.shape[0]
    rows = own_rows * tensor_count
    width = w_out.shape[1]
    inner = w_up.shape[2]
    half = D // 2
    block = D // dp_count
    joint = w_qkv.transpose(0, 2, 3, 1).reshape(LAYERS, 3 * width, D)
    params = {
        "small": [gains, biases, ff_bias, qv_bias],
        "w_qkv": joint,
        "w_out": w_out,
        "w_up": w_up,
        "w_down": w_down,
    }
    mask = allowed_rows(segments, rows)
    near = dp_count // 4

    def paired(sent, kept, gate):
        return [sent, swapped(after(sent, gate), "dp", near), kept]

    mlp_work = [
        Halving([((0, 0, 0), (1, half, half + inner)), ((1, 0, 0), (0, half, half + inner))], 2 * inner)
        for _ in range(LAYERS)
    ]
    att_work = [
        Halving([((0, 0, 0), (1, half, half + 3 * width)), ((1, 0, 0), (0, half, half + width))], 4 * width)
        for _ in range(LAYERS)
    ]
    token_pieces = gathered(tokens)
    token_pieces[-1] = after(token_pieces[-1], mask)
    saved, rows_a, rows_b = [], [None] * LAYERS, [None] * LAYERS
    cot_pieces = None
    mid = pair = None
    for layer in range(LAYERS):
        if layer == 0:
            hidden, picked1, q, kv = project_first(tokens, token_pieces[1:], params)
        else:
            hidden, picked1, q, kv = project_next(mid, pair, layer, params)
        kv_parts = [shifted(kv, "dp", distance) for distance in range(SPAN - 1, 0, -1)] + [kv]
        if layer:
            q = after(q, rows_a[layer - 1][1], rows_b[layer - 1][1])
        att, lse, sent_a, keep, give = attend(q, kv_parts, mask, picked1, layer, params)

        def launch_a(gate):
            nonlocal cot_pieces
            rows_a[layer] = paired(sent_a, picked1, gate)
            if layer == 0:
                cot_pieces = gathered(after(cotangent, gate))

        pair = exchanged(keep, give, launch_a)
        if layer == LAYERS - 1:
            pair[0] = after(pair[0], rows_a[layer][1])
        mid, slope, sent_b, kept_b, keep, give = feed_forward(hidden, pair, layer, params)
        saved.append((hidden, q, kv_parts, att, lse, mid, slope))
        if layer < LAYERS - 1:

            def launch_b(gate):
                rows_b[layer] = paired(sent_b, kept_b, gate)

            pair = exchanged(keep, give, launch_b)
            pair[0] = after(pair[0], cot_pieces[-1])
    last_keep, last_give = keep, give

    mlp_small, att_small, qv_small = ([None] * LAYERS for _ in range(3))
    gmid = last_pair = None
    for layer in range(LAYERS - 1, -1, -1):
        last = layer == LAYERS - 1
        later = layer + 1
        hidden, q, kv_parts, att, lse, mid, slope = saved[layer]
        if last:
            grad, sent1, mlp_small[layer], kept1, keep, give = mlp_grad_last(
                cot_pieces, slope, params
            )
        else:
            grad, sent1, mlp_small[layer], kept1, keep, give = mlp_grad_next(
                gmid, pair, saved[layer + 1][0], slope, layer, params
            )
        rows_1 = None

        def launch_1(gate):
            nonlocal rows_1
            if last:
                rows_b[layer] = paired(sent_b, kept_b, gate)
            else:
                rows_1 = paired(sent1, kept1, gate)

        pair = exchanged(keep, give, launch_1)
        gmid, picked, dq, dkv, att_small[layer], *away = attend_grad(
            grad, pair, mid, q, kv_parts, mask, att, lse, layer, params
        )
        arrived = [shifted(a, "dp", -(place + 1)) for place, a in enumerate(away)]
        due = []
        if last:
            due.append(rows_b[layer][1])
        else:
            mlp_work[layer].begin([rows_b[layer], rows_1])
            mlp_work[later].absorb()
            due += [mlp_work[layer].send, mlp_work[later].send, att_work[later].send]
        sent2, qv_small[layer], keep, give = project_grad(
            dq,
            after(dkv, *due),
            arrived,
            picked,
            layer,
            params,
            () if last else (last_keep, last_give),
        )
        rows_2 = None

        def launch_2(gate):
            nonlocal rows_2
            rows_2 = paired(sent2, picked, gate)

        if last:

            def launch_late(gate):
                nonlocal rows_1
                rows_1 = paired(sent1, kept1, gate)
                launch_2(gate)

            pair = exchanged(keep, give, launch_late)
            mlp_work[layer].begin([rows_b[layer], rows_1])
            mlp_work[layer].launch()
            att_work[layer].begin([rows_a[layer], rows_2])
    small = local_small(
        keep, give, saved[0][0], mlp_small, att_small, qv_small, tensor_count, width
    )
    rows_2 = [sent2, swapped(sent2, "dp", near), picked]
    mlp_work[1].launch()
    mlp_work[0].launch()
    bits, dp_bits = bits_of("tensor"), bits_of("dp")
    total = keep
    for place, bit in enumerate(bits):
        rounded = give if place == 0 else total.astype(bf16)
        other = swapped(rounded, "tensor", bit)
        total = (total if place == 0 else rounded.astype(f32)) + other.astype(f32)
        small = small + swapped(small, "tensor", bit)
        total, small = lax.optimization_barrier((total, small))
    att_work[1].launch(total)
    small = small + swapped(small, "dp", dp_bits[-1])
    total = after(total, small, mlp_work[1].arrived, att_work[1].arrived)
    att_work[1].absorb()
    att_work[1].launch()
    rounded = total.astype(bf16)
    pair = [rounded, swapped(rounded, "tensor", bits[0])]
    input_grad = first_grad(gmid, pair, saved[0][0], params, own_rows)
    result = last_rows(saved[-1][5], pair, params, own_rows)
    rows_2[1] = after(rows_2[1], input_grad, result)
    att_work[0].begin([rows_a[0], rows_2])
    att_work[0].launch()
    mlp_work[0].arrived = after(mlp_work[0].arrived, att_work[0].send, att_work[1].arrived)
    mlp_work[0].absorb()
    mlp_work[0].launch()
    small = after(small, mlp_work[0].send)
    hops = dp_bits[:-1]
    for bit in hops[:-1]:
        small = small + swapped(small, "dp", bit)
    att_work[0].arrived = after(att_work[0].arrived, small)
    att_work[0].absorb()
    att_work[0].launch()
    small = after(small, att_work[0].send)
    small_grads = small_outs(small, swapped(small, "dp", hops[-1]), tensor_count)
    mlp_parts = [work.finish() for work in mlp_work]
    att_parts = [work.finish() for work in att_work]
    g_up, g_down = mlp_outputs(mlp_parts, block, inner)
    g_qkv, g_out = att_outputs(att_parts, block, width)
    return (
        result,
        input_grad,
        g_qkv.transpose(0, 2, 1, 3),
        g_out,
        g_up,
        g_down.transpose(0, 2, 1),
        *small_grads,
    )


def solution(mesh):
    return jax.shard_map(
        shards,
        mesh=mesh,
        in_specs=(
            P(("dp", "tensor"), None),
            P(("dp", "tensor"), None),
            P(),
            P(None, None, None, "tensor"),
            P(None, None, "tensor"),
            P(None, "tensor", None),
            P(None, None, "tensor"),
            P(None, "tensor", None),
            P(None, "tensor"),
            P(),
            P(),
        ),
        out_specs=(
            P(("dp", "tensor"), None),
            P(("dp", "tensor"), None),
            P(None, "dp", None, "tensor"),
            P(None, "tensor", "dp"),
            P(None, "dp", "tensor"),
            P(None, "tensor", "dp"),
            P(),
            P(),
            P(),
            P(),
        ),
        check_vma=False,
    )
```

```python
import jax
import jax.numpy as jnp
from jax import lax
from jax.experimental import pallas as pl
from jax.experimental.pallas import tpu as pltpu
from jax.sharding import PartitionSpec as P

D = 768
HD = 64
FF = 3072
LAYERS = 2
SPAN = 4

epsilon = 1e-05
gelu_c = 0.7978845608028654
f32 = jnp.float32
bf16 = jnp.bfloat16
VMEM_LIMIT = 28 * 1024 * 1024


def shifted(array, axis, by):
    length = lax.axis_size(axis)
    pairs = [(i, i + by) for i in range(length) if 0 <= i + by < length]
    return lax.ppermute(array, axis, pairs)


def swapped(array, axis, bit):
    length = lax.axis_size(axis)
    return lax.ppermute(array, axis, [(i, i ^ bit) for i in range(length)])


def bits_of(axis):
    length = lax.axis_size(axis)
    found, bit = [], 1
    while bit < length:
        found.append(bit)
        bit *= 2
    assert bit == length
    return found


def call(kernel, outs, args, flops=1, moved=1):
    spec = pl.BlockSpec(memory_space=pltpu.VMEM)
    shapes = [jax.ShapeDtypeStruct(shape, dtype) for shape, dtype in outs]
    return pl.pallas_call(
        kernel,
        out_shape=shapes,
        in_specs=[spec] * len(args),
        out_specs=[spec] * len(outs),
        compiler_params=pltpu.CompilerParams(vmem_limit_bytes=VMEM_LIMIT),
        cost_estimate=pl.CostEstimate(
            flops=int(flops), bytes_accessed=int(moved), transcendentals=0
        ),
    )(*args)


def picked_halves(rows):
    wide = rows.shape[1] // 4
    high = (lax.axis_index("dp") // (lax.axis_size("dp") // 4)) % 2 == 1
    quarters = [rows[:, k * wide : (k + 1) * wide] for k in range(4)]
    return tuple(
        jnp.concatenate(
            [jnp.where(high, quarters[k + one], quarters[k + zero]) for k in (0, 2)], axis=1
        )
        for zero, one in ((0, 1), (1, 0))
    )


def mm(left, right, contract=((1,), (0,))):
    return lax.dot_general(left, right, (contract, ((), ())), preferred_element_type=f32)


NT = ((1,), (1,))
TN = ((0,), (0,))


def normalize(values_in):
    mean_v = jnp.mean(values_in, axis=-1, keepdims=True)
    centred = values_in - mean_v
    var_v = jnp.mean(centred * centred, axis=-1, keepdims=True)
    rstd = lax.rsqrt(var_v + epsilon)
    return (centred * rstd, rstd)


def norm_bwd(grad_in, normed, rstd, gain):
    scaled = grad_in * gain
    inner = jnp.mean(scaled, axis=-1, keepdims=True)
    along = jnp.mean(scaled * normed, axis=-1, keepdims=True)
    return rstd * (scaled - inner - normed * along)


def gain(small, layer, which):
    return small[0][layer, which : which + 1]


def bias(small, layer, which):
    return small[1][layer, which : which + 1]


def ff_bias_row(small, layer):
    return small[2][layer : layer + 1]


def qv_bias(small, layer, which):
    return small[3][layer, which : which + 1]


def column_sum(values_in):
    return jnp.sum(values_in, axis=0, keepdims=True)


def gelu_pair(pre_act):
    inner = gelu_c * (pre_act + 0.044715 * pre_act * pre_act * pre_act)
    tanh_v = jnp.tanh(inner)
    value_out = 0.5 * pre_act * (1.0 + tanh_v)
    slope = 0.5 * (1.0 + tanh_v) + 0.5 * pre_act * (1.0 - tanh_v * tanh_v) * gelu_c * (
        1.0 + 3.0 * 0.044715 * pre_act * pre_act
    )
    return (value_out, slope)


def joined(own_ref, other_ref):
    high = (lax.axis_index("tensor") & 1) == 1
    own, other = own_ref[...].astype(f32), other_ref[...].astype(f32)
    return jnp.concatenate(
        [jnp.where(high, other, own), jnp.where(high, own, other)], axis=0
    )


def split_halves(total, keep_ref, give_ref):
    half = total.shape[0] // 2
    high = (lax.axis_index("tensor") & 1) == 1
    low_rows, high_rows = total[:half], total[half:]
    keep_ref[...] = jnp.where(high, high_rows, low_rows)
    give_ref[...] = jnp.where(high, low_rows, high_rows).astype(bf16)


def place_pieces(pieces, out_ref):
    mine = lax.axis_index("tensor")
    rows = pieces[0].shape[0]
    for number, piece in enumerate(pieces):
        start = pl.multiple_of((mine ^ number) * rows, rows)
        out_ref[pl.ds(start, rows), :] = piece[...].astype(out_ref.dtype)


def gathered(piece):
    pieces = {0: piece}
    for bit in bits_of("tensor")[::-1]:
        for number in list(pieces):
            pieces[number ^ bit] = swapped(pieces[number], "tensor", bit)
    return [pieces[number] for number in range(len(pieces))]


def after(value, *others):
    return lax.optimization_barrier((value, *others))[0]


def exchanged(keep, give, launch=None, due=()):
    bits = bits_of("tensor")
    total = keep + swapped(give, "tensor", bits[0]).astype(f32)
    for bit in bits[1:]:
        rounded = after(total.astype(bf16), *due)
        other = swapped(rounded, "tensor", bit)
        if launch is not None and bit == bits[-1]:
            launch(rounded)
        total = rounded.astype(f32) + other.astype(f32)
    rounded = total.astype(bf16)
    return [rounded, swapped(rounded, "tensor", bits[0])]


def project_rows(hidden, layer, refs, outs):
    small, w_qkv = refs[:4], refs[4]
    h_ref, picked_ref, q_ref, kv_ref = outs
    width = q_ref.shape[1]
    hat, _ = normalize(hidden)
    act = (hat * gain(small, layer, 0) + bias(small, layer, 0)).astype(bf16)
    kv = mm(act, w_qkv[layer, width:], NT)
    values = kv[:, width:] + qv_bias(small, layer, 1)
    kv_ref[...] = jnp.concatenate([kv[:, :width], values], axis=1).astype(bf16)
    query = mm(act, w_qkv[layer, :width], NT)
    q_ref[...] = (query + qv_bias(small, layer, 0)).astype(bf16)
    half = act.shape[1] // 2
    picked_ref[:, :half], picked_ref[:, half:] = picked_halves(act)


def project_first(tokens, pieces, params):
    count = len(pieces)
    own_rows = tokens.shape[0]
    rows = (count + 1) * own_rows
    width = params["w_out"].shape[1]
    gains, biases, _, qv = params["small"]
    far = [tokens, gains, biases, qv, params["w_qkv"]]
    many = len(far)

    def kernel(*refs):
        ins, near = refs[:count], refs[count : count + many]
        outs = refs[-4:]
        place_pieces([near[0], *ins], outs[0])
        small = (near[1], near[2], None, near[3])
        project_rows(outs[0][...], 0, [*small, near[4]], outs)

    def whole(array):
        zeros = (0,) * array.ndim
        return pl.BlockSpec(array.shape, lambda step: zeros)

    spec = pl.BlockSpec(memory_space=pltpu.VMEM)
    return pl.pallas_call(
        kernel,
        grid=(1,),
        out_shape=[
            jax.ShapeDtypeStruct((rows, D), f32),
            jax.ShapeDtypeStruct((rows, D), bf16),
            jax.ShapeDtypeStruct((rows, width), bf16),
            jax.ShapeDtypeStruct((rows, 2 * width), bf16),
        ],
        in_specs=[spec] * count
        + [whole(a) for a in far[:-1]]
        + [pl.BlockSpec((1,) + far[-1].shape[1:], lambda step: (0, 0, 0))],
        out_specs=[spec] * 4,
        compiler_params=pltpu.CompilerParams(vmem_limit_bytes=VMEM_LIMIT),
        cost_estimate=pl.CostEstimate(flops=1, bytes_accessed=1, transcendentals=0),
    )(*pieces, *far)


def project_next(mid, pair, layer, params):
    rows = mid.shape[0]
    width = params["w_out"].shape[1]

    def kernel(mid_ref, own_ref, other_ref, *refs):
        ins, outs = refs[:5], refs[5:]
        hidden = mid_ref[...] + joined(own_ref, other_ref) + bias(ins, layer - 1, 3)
        outs[0][...] = hidden
        project_rows(hidden, layer, ins, outs)

    return call(
        kernel,
        [((rows, D), f32), ((rows, D), bf16), ((rows, width), bf16), ((rows, 2 * width), bf16)],
        [mid, *pair, *params["small"], params["w_qkv"]],
    )


def head_lanes(shape, head):
    lane = lax.broadcasted_iota(jnp.int32, shape, 1)
    return (lane >= head * HD) & (lane < (head + 1) * HD)


def allowed_rows(segments, rows):
    def kernel(seg_ref, out_ref):
        mine = lax.axis_index("dp")
        here = seg_ref[:, pl.ds(pl.multiple_of(mine * rows, rows), rows)].astype(f32)
        query_seg = jnp.broadcast_to(here, (rows, rows)).T
        query = lax.broadcasted_iota(jnp.int32, (rows, rows), 0)
        key = lax.broadcasted_iota(jnp.int32, (rows, rows), 1)
        for place in range(SPAN):
            behind = SPAN - 1 - place
            start = jnp.maximum(mine - behind, 0) * rows
            key_seg = seg_ref[:, pl.ds(pl.multiple_of(start, rows), rows)].astype(f32)
            same = (query_seg == key_seg) & (key <= query + behind * rows)
            seen = jnp.where(same, 1.0, 0.0) * jnp.where(mine >= behind, 1.0, 0.0)
            out_ref[:, place * rows : (place + 1) * rows] = seen

    row = segments[None, :]
    return call(kernel, [((rows, SPAN * rows), f32)], [row], 1e10, 1e8)[0]


def split_shapes(rows):
    return [((rows // 2, D), f32), ((rows // 2, D), bf16)]


def attend(q, kv_parts, mask, picked1, layer, params):
    rows, width = q.shape
    half = D // 2
    pad = -(half + width) % 128
    heads = width // HD

    def kernel(q_ref, *refs):
        kv_refs, refs = refs[:SPAN], refs[SPAN:]
        mask_ref, w_out, p1_ref, att_ref, lse_ref, sent_ref, keep_ref, give_ref = refs
        allowed = mask_ref[...] > 0.0
        kv_all = jnp.concatenate([r[...] for r in kv_refs], axis=0)
        keys, values = kv_all[:, :width], kv_all[:, width:]
        query = q_ref[...]
        mixed = jnp.zeros((rows, width), f32)
        logs = jnp.zeros((rows, 128), f32)
        lane = lax.broadcasted_iota(jnp.int32, (rows, 128), 1)
        for head in range(heads):
            inside = head_lanes((rows, width), head)
            scores = mm(jnp.where(inside, query, 0), keys, NT) * HD ** (-0.5)
            scores = jnp.where(allowed, scores, -1e30)
            top = jnp.max(scores, axis=-1, keepdims=True)
            log_total = top + jnp.log(jnp.sum(jnp.exp(scores - top), axis=-1, keepdims=True))
            weights = jnp.exp(scores - log_total).astype(bf16)
            mixed = jnp.where(inside, mm(weights, values), mixed)
            logs = jnp.where(lane == head, log_total, logs)
        att = mixed.astype(bf16)
        att_ref[...] = att
        sent_ref[:, :half] = p1_ref[:, half:]
        sent_ref[:, half : half + width] = att
        if pad:
            sent_ref[:, half + width :] = jnp.zeros((rows, pad), bf16)
        lse_ref[...] = logs
        split_halves(mm(att, w_out[layer]), keep_ref, give_ref)

    return call(
        kernel,
        [((rows, width), bf16), ((rows, 128), f32), ((rows, half + width + pad), bf16)]
        + split_shapes(rows),
        [q, *kv_parts, mask, params["w_out"], picked1],
    )


def feed_forward(hidden, pair, layer, params):
    rows = hidden.shape[0]
    half = D // 2
    inner = params["w_up"].shape[2]

    def kernel(h_ref, own_ref, other_ref, g_ref, b_ref, f_ref, q_ref, up, down,
               mid_ref, slope_ref, sent_ref, kept_ref, keep_ref, give_ref):
        small = (g_ref, b_ref, f_ref, q_ref)
        mid = h_ref[...] + joined(own_ref, other_ref) + bias(small, layer, 1)
        mid_ref[...] = mid
        hat, _ = normalize(mid)
        act2 = (hat * gain(small, layer, 1) + bias(small, layer, 2)).astype(bf16)
        pre = mm(act2, up[layer]) + ff_bias_row(small, layer)
        value, slope = gelu_pair(pre)
        act3 = value.astype(bf16)
        split_halves(mm(act3, down[layer]), keep_ref, give_ref)
        slope_ref[...] = slope
        kept_ref[...], sent_ref[:, :half] = picked_halves(act2)
        sent_ref[:, half:] = act3

    return call(
        kernel,
        [
            ((rows, D), f32),
            ((rows, inner), f32),
            ((rows, half + inner), bf16),
            ((rows, half), bf16),
        ]
        + split_shapes(rows),
        [hidden, *pair]
        + [*params["small"], params["w_up"], params["w_down"]],
    )


def last_rows(mid, pair, params, own_rows):
    def kernel(mid_ref, own_ref, other_ref, biases, out_ref, all_ref):
        own = mid_ref.shape[0] // 2
        total = mid_ref[...] + joined(own_ref.at[own:], other_ref.at[own:])
        all_ref[...] = total + biases[LAYERS - 1, 3:4]
        start = pl.multiple_of(lax.axis_index("tensor") * own_rows, own_rows)
        out_ref[...] = all_ref[pl.ds(start, own_rows), :].astype(bf16)

    args = [mid, *pair, params["small"][1]]
    return call(kernel, [((own_rows, D), bf16), (mid.shape, f32)], args)[0]


def norm1_grad(gmid_ref, own_ref, other_ref, h_ref, gains, layer):
    d_norm = joined(own_ref, other_ref)
    hat, rstd = normalize(h_ref[...])
    grad = gmid_ref[...] + norm_bwd(d_norm, hat, rstd, gains[layer, 0:1])
    return grad, column_sum(d_norm * hat), column_sum(d_norm)


def mlp_grad(grad, layer, refs, outs):
    slope_ref, up, down = refs
    sent_ref, small_ref, kept_ref, keep_ref, give_ref = outs
    half = D // 2
    grad_b = grad.astype(bf16)
    d_pre = mm(grad_b, down[layer], NT) * slope_ref[...]
    pre_b = d_pre.astype(bf16)
    split_halves(mm(pre_b, up[layer], NT), keep_ref, give_ref)
    kept_ref[...], sent_ref[:, :half] = picked_halves(grad_b)
    sent_ref[:, half:] = pre_b
    small_ref[0:1, :] = column_sum(d_pre)
    small_ref[1:2, :] = column_sum(grad)


def mlp_outs(rows, inner):
    assert inner == D
    return [
        ((rows, D), f32),
        ((rows, D // 2 + inner), bf16),
        ((8, D), f32),
        ((rows, D // 2), bf16),
    ] + split_shapes(rows)


def mlp_grad_last(pieces, slope, params):
    count = len(pieces)
    rows, inner = slope.shape

    def kernel(*refs):
        ins, outs = refs[: count + 3], refs[count + 3 :]
        place_pieces(ins[:count], outs[0])
        outs[2][...] = jnp.zeros((8, D), f32)
        mlp_grad(outs[0][...], LAYERS - 1, ins[count:], outs[1:])

    return call(
        kernel,
        mlp_outs(rows, inner),
        [*pieces, slope, params["w_up"], params["w_down"]],
    )


def mlp_grad_next(gmid, pair, hidden, slope, layer, params):
    rows, inner = slope.shape

    def kernel(gmid_ref, own_ref, other_ref, h_ref, gains, *refs):
        ins, outs = refs[:3], refs[3:]
        grad, g_gain, g_bias = norm1_grad(gmid_ref, own_ref, other_ref, h_ref, gains, layer + 1)
        outs[0][...] = grad
        outs[2][...] = jnp.zeros((8, D), f32)
        mlp_grad(grad, layer, ins, outs[1:])
        outs[2][2:3, :] = g_gain
        outs[2][3:4, :] = g_bias

    return call(
        kernel,
        mlp_outs(rows, inner),
        [gmid, *pair, hidden, params["small"][0], slope, params["w_up"], params["w_down"]],
    )


def attend_grad(grad, pair, mid, q, kv_parts, mask, att, lse, layer, params):
    rows, width = q.shape
    heads = width // HD
    back = SPAN - 1

    def kernel(g_ref, own_ref, other_ref, mid_ref, q_ref, *refs):
        kv_refs, refs = refs[:SPAN], refs[SPAN:]
        mask_ref, att_ref, lse_ref, gains, w_out = refs[:5]
        gmid_ref, picked_ref, dq_ref, dkv_ref, small_ref = refs[5:10]
        away_refs = refs[10:]
        d_norm = joined(own_ref, other_ref)
        hat, rstd = normalize(mid_ref[...])
        gmid = g_ref[...] + norm_bwd(d_norm, hat, rstd, gains[layer, 1:2])
        gmid_ref[...] = gmid
        mid_b = gmid.astype(bf16)
        d_att = mm(mid_b, w_out[layer], NT).astype(bf16)
        allowed = mask_ref[...] > 0.0
        kv_all = jnp.concatenate([r[...] for r in kv_refs], axis=0)
        keys, values = kv_all[:, :width], kv_all[:, width:]
        query, logs = q_ref[...], lse_ref[...]
        weighed = d_att.astype(f32) * att_ref[...].astype(f32)
        d_query = jnp.zeros((rows, width), f32)
        d_keys = jnp.zeros((SPAN * rows, width), f32)
        d_values = jnp.zeros((SPAN * rows, width), f32)
        for head in range(heads):
            inside = head_lanes((rows, width), head)
            query_h = jnp.where(inside, query, 0)
            d_att_h = jnp.where(inside, d_att, 0)
            scores = mm(query_h, keys, NT) * HD ** (-0.5)
            scores = jnp.where(allowed, scores, -1e30)
            probs = jnp.exp(scores - logs[:, head : head + 1])
            delta = jnp.sum(jnp.where(inside, weighed, 0.0), axis=-1, keepdims=True)
            d_prob = mm(d_att_h, values, NT)
            d_score = (probs * (d_prob - delta) * HD ** (-0.5)).astype(bf16)
            d_query = jnp.where(inside, mm(d_score, keys), d_query)
            d_keys = d_keys + mm(d_score, query_h, TN)
            d_values = d_values + mm(probs.astype(bf16), d_att_h, TN)
        d_kv = jnp.concatenate([d_keys, d_values], axis=1)
        dq_ref[...] = d_query
        dkv_ref[...] = d_kv[back * rows :]
        for distance in range(1, SPAN):
            block = back - distance
            away_refs[distance - 1][...] = d_kv[block * rows : (block + 1) * rows].astype(bf16)
        half = D // 2
        picked_ref[:, :half], picked_ref[:, half:] = picked_halves(mid_b)
        small_ref[...] = jnp.zeros((8, D), f32)
        small_ref[0:1, :] = column_sum(d_norm * hat)
        small_ref[1:2, :] = column_sum(d_norm)
        small_ref[2:3, :] = column_sum(gmid)

    return call(
        kernel,
        [
            ((rows, D), f32),
            ((rows, D), bf16),
            ((rows, width), f32),
            ((rows, 2 * width), f32),
            ((8, D), f32),
        ]
        + [((rows, 2 * width), bf16)] * back,
        [grad, *pair, mid, q, *kv_parts, mask, att, lse]
        + [params["small"][0], params["w_out"]],
    )


def project_grad(dq, dkv, arrived, picked, layer, params, more=()):
    rows, width = dq.shape
    half = D // 2
    pad = -(half + 3 * width) % 128

    def kernel(dq_ref, dkv_ref, *refs):
        near, refs = refs[: SPAN - 1], refs[SPAN - 1 :]
        picked_ref, w_qkv = refs[:2]
        sent_ref, small_ref, keep_ref, give_ref = refs[-4:]
        d_kv = dkv_ref[...]
        for ref in near:
            d_kv = d_kv + ref[...].astype(f32)
        d_query = dq_ref[...]
        query_b, kv_b = d_query.astype(bf16), d_kv.astype(bf16)
        part = mm(kv_b, w_qkv[layer, width:]) + mm(query_b, w_qkv[layer, :width])
        own = rows // 2
        split_halves(part, keep_ref.at[:own], give_ref.at[:own])
        for ref, source in zip((keep_ref, give_ref), refs[2:-4]):
            ref[own:, :] = source[...]
        sent_ref[:, :half] = picked_ref[:, half:]
        sent_ref[:, half : half + 2 * width] = kv_b
        sent_ref[:, half + 2 * width : half + 3 * width] = query_b
        if pad:
            sent_ref[:, half + 3 * width :] = jnp.zeros((rows, pad), bf16)
        small_ref[...] = jnp.zeros((8, D), f32)
        small_ref[0:1, :width] = column_sum(d_query)
        small_ref[1:2, :width] = column_sum(d_kv)[:, width:]

    return call(
        kernel,
        [((rows, half + 3 * width + pad), bf16), ((8, D), f32)]
        + split_shapes(rows * (2 if more else 1)),
        [dq, dkv, *arrived, picked, params["w_qkv"], *more],
    )


def small_rows(count):
    rows = 8 * LAYERS + LAYERS * count
    return rows + -rows % 8


def local_small(keep, give, hidden, mlp_small, att_small, qv_small, count, width):
    share = 1.0 / count

    def kernel(keep_ref, give_ref, h_ref, *refs):
        mlp, att, qv, out = refs[:LAYERS], refs[LAYERS : 2 * LAYERS], refs[2 * LAYERS : -1], refs[-1]
        mine = lax.axis_index("tensor")
        own = h_ref.shape[0] // 2
        part = joined(keep_ref.at[:own], give_ref.at[:own])
        hat, _ = normalize(h_ref[...])
        out[...] = jnp.zeros(out.shape, f32)
        for layer in range(LAYERS):
            gain1 = column_sum(part * hat) if layer == 0 else mlp[layer - 1][2:3, :] * share
            bias1 = column_sum(part) if layer == 0 else mlp[layer - 1][3:4, :] * share
            at = 2 * layer
            out[at : at + 1, :] = gain1
            out[at + 1 : at + 2, :] = att[layer][0:1, :] * share
            at = 2 * LAYERS + 4 * layer
            out[at : at + 1, :] = bias1
            out[at + 1 : at + 2, :] = att[layer][2:3, :] * share
            out[at + 2 : at + 3, :] = att[layer][1:2, :] * share
            out[at + 3 : at + 4, :] = mlp[layer][1:2, :] * share
            for target in range(count):
                here = mine == target
                at = 6 * LAYERS + 2 * layer
                lanes = slice(target * width, (target + 1) * width)
                out[at : at + 2, lanes] = jnp.where(here, qv[layer][0:2, :width], 0.0)
                at = 8 * LAYERS + layer * count + target
                out[at : at + 1, :] = jnp.where(here, mlp[layer][0:1, :], 0.0)

    args = [keep, give, hidden, *mlp_small, *att_small, *qv_small]
    return call(kernel, [((small_rows(count), D), f32)], args)[0]


def first_grad(gmid, pair, hidden, params, own_rows):
    def kernel(gmid_ref, own_ref, other_ref, h_ref, gains, in_ref, g_ref):
        own = h_ref.shape[0] // 2
        near, away = own_ref.at[:own], other_ref.at[:own]
        g_ref[...] = norm1_grad(gmid_ref, near, away, h_ref, gains, 0)[0]
        start = pl.multiple_of(lax.axis_index("tensor") * own_rows, own_rows)
        in_ref[...] = g_ref[pl.ds(start, own_rows), :].astype(bf16)

    args = [gmid, *pair, hidden, params["small"][0]]
    return call(kernel, [((own_rows, D), bf16), (gmid.shape, f32)], args)[0]


def small_outs(total, other, count):
    def kernel(total_ref, other_ref, gains, biases, qv, ffb):
        both = total_ref[...] + other_ref[...]
        for layer in range(LAYERS):
            gains[layer] = both[2 * layer : 2 * layer + 2]
            at = 2 * LAYERS + 4 * layer
            biases[layer] = both[at : at + 4]
            at = 6 * LAYERS + 2 * layer
            qv[layer] = both[at : at + 2]
            for target in range(count):
                at = 8 * LAYERS + layer * count + target
                ffb[layer : layer + 1, target * D : (target + 1) * D] = both[at : at + 1]

    return call(
        kernel,
        [
            ((LAYERS, 2, D), f32),
            ((LAYERS, 4, D), f32),
            ((LAYERS, 2, D), f32),
            ((LAYERS, count * D), f32),
        ],
        [total, other],
    )


def split_rows(total, bit, block, send_ref, keep_ref):
    mine = lax.axis_index("dp")
    high = jnp.where((mine & bit) != 0, 1, 0)
    pairs = total.shape[0] // (2 * block)
    for pair in range(pairs):
        for which in range(2):
            rows = total[(2 * pair + which) * block : (2 * pair + which + 1) * block]
            out = slice(pair * block, (pair + 1) * block)

            @pl.when(high == which)
            def _():
                keep_ref[out, :] = rows

            @pl.when(high != which)
            def _():
                send_ref[out, :] = rows.astype(bf16)


def split_plain(total, bit, block):
    pairs = total.shape[0] // (2 * block)
    split = total.reshape(pairs, 2, block, total.shape[1])
    high = jnp.where((lax.axis_index("dp") & bit) != 0, 1, 0)
    send = lax.dynamic_index_in_dim(split, 1 - high, 1, keepdims=False)
    keep = lax.dynamic_index_in_dim(split, high, 1, keepdims=False)
    return send.reshape(-1, total.shape[1]).astype(bf16), keep.reshape(-1, total.shape[1])


class Halving:
    def __init__(self, products, wide):
        self.products, self.wide = products, wide
        self.bits = [bit for bit in bits_of("dp") if bit != lax.axis_size("dp") // 4]
        self.block = D // lax.axis_size("dp")
        self.place = 0

    def begin(self, sources):
        half = D // 2
        flat = [array for source in sources for array in source]
        shape = (half // 2, self.wide)
        spots = self.products

        def products_of(refs):
            done = []
            for (la, kept_at, sent_at), (ra, r0, r1) in spots:
                kept = refs[3 * la + 2][:, kept_at : kept_at + half]
                given = refs[3 * la + 1][:, sent_at : sent_at + half]
                left = jnp.concatenate([kept, given], axis=0)
                right = [refs[3 * ra][:, r0:r1], refs[3 * ra + 1][:, r0:r1]]
                done.append(mm(left, jnp.concatenate(right, axis=0), TN))
            return jnp.concatenate(done, axis=1)

        bit, block, count = self.bits[0], self.block, len(flat)
        if block % 16:

            def kernel(*refs):
                refs[count][...] = products_of(refs)

            total = call(kernel, [((half, self.wide), f32)], flat)[0]
            self.send, self.keep = split_plain(total, bit, block)
        else:

            def kernel(*refs):
                split_rows(products_of(refs), bit, block, refs[count], refs[count + 1])

            self.send, self.keep = call(kernel, [(shape, bf16), (shape, f32)], flat)

    def launch(self, *gates):
        send = after(self.send, *gates) if gates else self.send
        self.arrived = swapped(send, "dp", self.bits[self.place])

    def absorb(self):
        self.place += 1
        bit, block = self.bits[self.place], self.block
        if block % 16:
            total = self.keep + self.arrived.astype(f32)
            self.send, self.keep = split_plain(total, bit, block)
            return

        def kernel(keep_ref, arrived_ref, send_ref, kept_ref):
            total = keep_ref[...] + arrived_ref[...].astype(f32)
            split_rows(total, bit, block, send_ref, kept_ref)

        shape = (self.keep.shape[0] // 2, self.wide)
        args = [self.keep, self.arrived]
        self.send, self.keep = call(kernel, [(shape, bf16), (shape, f32)], args)

    def finish(self):
        while self.place < len(self.bits) - 1:
            self.absorb()
            self.launch()
        return [self.keep, self.arrived]


def mlp_outputs(parts, block, inner):
    def kernel(*refs):
        up, down = refs[-2:]
        for layer in range(LAYERS):
            total = refs[2 * layer][...] + refs[2 * layer + 1][...].astype(f32)
            up[layer] = total[:, :inner]
            down[layer] = total[:, inner:]

    args = [a for pair in parts for a in pair]
    return call(kernel, [((LAYERS, block, inner), f32)] * 2, args)


def att_outputs(parts, block, width):
    def kernel(*refs):
        qkv, out = refs[-2:]
        for layer in range(LAYERS):
            total = refs[2 * layer][...] + refs[2 * layer + 1][...].astype(f32)
            qkv[layer, 0] = total[:, 2 * width : 3 * width]
            qkv[layer, 1] = total[:, :width]
            qkv[layer, 2] = total[:, width : 2 * width]
            out[layer] = total[:, 3 * width :].T

    args = [a for pair in parts for a in pair]
    return call(
        kernel,
        [((LAYERS, 3, block, width), f32), ((LAYERS, width, block), f32)],
        args,
    )


def shards(
    tokens, cotangent, segments, w_qkv, qv_bias, w_out, w_up, w_down, ff_bias, gains, biases
):
    tensor_count = lax.axis_size("tensor")
    dp_count = lax.axis_size("dp")
    own_rows = tokens.shape[0]
    rows = own_rows * tensor_count
    width = w_out.shape[1]
    inner = w_up.shape[2]
    half = D // 2
    block = D // dp_count
    joint = w_qkv.transpose(0, 2, 3, 1).reshape(LAYERS, 3 * width, D)
    params = {
        "small": [gains, biases, ff_bias, qv_bias],
        "w_qkv": joint,
        "w_out": w_out,
        "w_up": w_up,
        "w_down": w_down,
    }
    mask = allowed_rows(segments, rows)
    near = dp_count // 4

    def paired(sent, kept, gate):
        return [sent, swapped(after(sent, gate), "dp", near), kept]

    mlp_work = [
        Halving([((0, 0, 0), (1, half, half + inner)), ((1, 0, 0), (0, half, half + inner))], 2 * inner)
        for _ in range(LAYERS)
    ]
    att_work = [
        Halving([((0, 0, 0), (1, half, half + 3 * width)), ((1, 0, 0), (0, half, half + width))], 4 * width)
        for _ in range(LAYERS)
    ]
    token_pieces = gathered(tokens)
    token_pieces[-1] = after(token_pieces[-1], mask)
    saved, rows_a, rows_b = [], [None] * LAYERS, [None] * LAYERS
    cot_pieces = None
    mid = pair = None
    for layer in range(LAYERS):
        if layer == 0:
            hidden, picked1, q, kv = project_first(tokens, token_pieces[1:], params)
        else:
            hidden, picked1, q, kv = project_next(mid, pair, layer, params)
        kv_parts = [shifted(kv, "dp", distance) for distance in range(SPAN - 1, 0, -1)] + [kv]
        if layer:
            q = after(q, rows_a[layer - 1][1], rows_b[layer - 1][1])
        att, lse, sent_a, keep, give = attend(q, kv_parts, mask, picked1, layer, params)

        def launch_a(gate):
            nonlocal cot_pieces
            rows_a[layer] = paired(sent_a, picked1, gate)
            if layer == 0:
                cot_pieces = gathered(after(cotangent, gate))

        pair = exchanged(keep, give, launch_a)
        if layer == LAYERS - 1:
            pair[0] = after(pair[0], rows_a[layer][1])
        mid, slope, sent_b, kept_b, keep, give = feed_forward(hidden, pair, layer, params)
        saved.append((hidden, q, kv_parts, att, lse, mid, slope))
        if layer < LAYERS - 1:

            def launch_b(gate):
                rows_b[layer] = paired(sent_b, kept_b, gate)

            pair = exchanged(keep, give, launch_b)
            pair[0] = after(pair[0], cot_pieces[-1])
    last_keep, last_give = keep, give

    mlp_small, att_small, qv_small = ([None] * LAYERS for _ in range(3))
    gmid = last_pair = None
    for layer in range(LAYERS - 1, -1, -1):
        last = layer == LAYERS - 1
        later = layer + 1
        hidden, q, kv_parts, att, lse, mid, slope = saved[layer]
        if last:
            grad, sent1, mlp_small[layer], kept1, keep, give = mlp_grad_last(
                cot_pieces, slope, params
            )
        else:
            grad, sent1, mlp_small[layer], kept1, keep, give = mlp_grad_next(
                gmid, pair, saved[layer + 1][0], slope, layer, params
            )
        rows_1 = None

        def launch_1(gate):
            nonlocal rows_1
            if last:
                rows_b[layer] = paired(sent_b, kept_b, gate)
            else:
                rows_1 = paired(sent1, kept1, gate)

        pair = exchanged(keep, give, launch_1)
        gmid, picked, dq, dkv, att_small[layer], *away = attend_grad(
            grad, pair, mid, q, kv_parts, mask, att, lse, layer, params
        )
        arrived = [shifted(away[by - 1], "dp", -by) for by in range(SPAN - 1, 0, -1)]
        due = []
        if last:
            due.append(rows_b[layer][1])
        else:
            mlp_work[layer].begin([rows_b[layer], rows_1])
            mlp_work[later].absorb()
            due += [mlp_work[layer].send, mlp_work[later].send, att_work[later].send]
        sent2, qv_small[layer], keep, give = project_grad(
            dq,
            after(dkv, *due),
            arrived,
            picked,
            layer,
            params,
            () if last else (last_keep, last_give),
        )
        rows_2 = None

        def launch_2(gate):
            nonlocal rows_2
            rows_2 = paired(sent2, picked, gate)

        if last:

            def launch_late(gate):
                nonlocal rows_1
                rows_1 = paired(sent1, kept1, gate)
                launch_2(gate)

            pair = exchanged(keep, give, launch_late)
            mlp_work[layer].begin([rows_b[layer], rows_1])
            mlp_work[layer].launch()
            att_work[layer].begin([rows_a[layer], rows_2])
    small = local_small(
        keep, give, saved[0][0], mlp_small, att_small, qv_small, tensor_count, width
    )
    rows_2 = [sent2, swapped(sent2, "dp", near), picked]
    mlp_work[1].launch()
    mlp_work[0].launch()
    bits, dp_bits = bits_of("tensor"), bits_of("dp")
    total = keep
    for place, bit in enumerate(bits):
        rounded = give if place == 0 else total.astype(bf16)
        other = swapped(rounded, "tensor", bit)
        total = (total if place == 0 else rounded.astype(f32)) + other.astype(f32)
        small = small + swapped(small, "tensor", bit)
        total, small = lax.optimization_barrier((total, small))
    att_work[1].launch(total)
    small = small + swapped(small, "dp", dp_bits[-1])
    total = after(total, small, mlp_work[1].arrived, att_work[1].arrived)
    att_work[1].absorb()
    att_work[1].launch()
    rounded = total.astype(bf16)
    pair = [rounded, swapped(rounded, "tensor", bits[0])]
    input_grad = first_grad(gmid, pair, saved[0][0], params, own_rows)
    result = last_rows(saved[-1][5], pair, params, own_rows)
    rows_2[1] = after(rows_2[1], input_grad, result)
    att_work[0].begin([rows_a[0], rows_2])
    att_work[0].launch()
    mlp_work[0].arrived = after(mlp_work[0].arrived, att_work[0].send, att_work[1].arrived)
    mlp_work[0].absorb()
    mlp_work[0].launch()
    small = after(small, mlp_work[0].send)
    hops = dp_bits[:-1]
    for bit in hops[:-1]:
        small = small + swapped(small, "dp", bit)
    att_work[0].arrived = after(att_work[0].arrived, small)
    att_work[0].absorb()
    att_work[0].launch()
    small = after(small, att_work[0].send)
    small_grads = small_outs(small, swapped(small, "dp", hops[-1]), tensor_count)
    mlp_parts = [work.finish() for work in mlp_work]
    att_parts = [work.finish() for work in att_work]
    g_up, g_down = mlp_outputs(mlp_parts, block, inner)
    g_qkv, g_out = att_outputs(att_parts, block, width)
    return (
        result,
        input_grad,
        g_qkv.transpose(0, 2, 1, 3),
        g_out,
        g_up,
        g_down.transpose(0, 2, 1),
        *small_grads,
    )


def solution(mesh):
    return jax.shard_map(
        shards,
        mesh=mesh,
        in_specs=(
            P(("dp", "tensor"), None),
            P(("dp", "tensor"), None),
            P(),
            P(None, None, None, "tensor"),
            P(None, None, "tensor"),
            P(None, "tensor", None),
            P(None, None, "tensor"),
            P(None, "tensor", None),
            P(None, "tensor"),
            P(),
            P(),
        ),
        out_specs=(
            P(("dp", "tensor"), None),
            P(("dp", "tensor"), None),
            P(None, "dp", None, "tensor"),
            P(None, "tensor", "dp"),
            P(None, "dp", "tensor"),
            P(None, "tensor", "dp"),
            P(),
            P(),
            P(),
            P(),
        ),
        check_vma=False,
    )
```

```python
import jax
import jax.numpy as jnp
from jax import lax
from jax.experimental import pallas as pl
from jax.experimental.pallas import tpu as pltpu
from jax.sharding import PartitionSpec as P

D = 768
HD = 64
FF = 3072
LAYERS = 2
SPAN = 4

epsilon = 1e-05
gelu_c = 0.7978845608028654
f32 = jnp.float32
bf16 = jnp.bfloat16
VMEM_LIMIT = 28 * 1024 * 1024


def shifted(array, axis, by):
    length = lax.axis_size(axis)
    pairs = [(i, i + by) for i in range(length) if 0 <= i + by < length]
    return lax.ppermute(array, axis, pairs)


def swapped(array, axis, bit):
    length = lax.axis_size(axis)
    return lax.ppermute(array, axis, [(i, i ^ bit) for i in range(length)])


def bits_of(axis):
    length = lax.axis_size(axis)
    found, bit = [], 1
    while bit < length:
        found.append(bit)
        bit *= 2
    assert bit == length
    return found


def call(kernel, outs, args, flops=1, moved=1):
    spec = pl.BlockSpec(memory_space=pltpu.VMEM)
    shapes = [jax.ShapeDtypeStruct(shape, dtype) for shape, dtype in outs]
    return pl.pallas_call(
        kernel,
        out_shape=shapes,
        in_specs=[spec] * len(args),
        out_specs=[spec] * len(outs),
        compiler_params=pltpu.CompilerParams(vmem_limit_bytes=VMEM_LIMIT),
        cost_estimate=pl.CostEstimate(
            flops=int(flops), bytes_accessed=int(moved), transcendentals=0
        ),
    )(*args)


def picked_halves(rows):
    wide = rows.shape[1] // 4
    high = (lax.axis_index("dp") // (lax.axis_size("dp") // 4)) % 2 == 1
    quarters = [rows[:, k * wide : (k + 1) * wide] for k in range(4)]
    return tuple(
        jnp.concatenate(
            [jnp.where(high, quarters[k + one], quarters[k + zero]) for k in (0, 2)], axis=1
        )
        for zero, one in ((0, 1), (1, 0))
    )


def mm(left, right, contract=((1,), (0,))):
    return lax.dot_general(left, right, (contract, ((), ())), preferred_element_type=f32)


NT = ((1,), (1,))
TN = ((0,), (0,))


def normalize(values_in):
    mean_v = jnp.mean(values_in, axis=-1, keepdims=True)
    centred = values_in - mean_v
    var_v = jnp.mean(centred * centred, axis=-1, keepdims=True)
    rstd = lax.rsqrt(var_v + epsilon)
    return (centred * rstd, rstd)


def norm_bwd(grad_in, normed, rstd, gain):
    scaled = grad_in * gain
    inner = jnp.mean(scaled, axis=-1, keepdims=True)
    along = jnp.mean(scaled * normed, axis=-1, keepdims=True)
    return rstd * (scaled - inner - normed * along)


def gain(small, layer, which):
    return small[0][layer, which : which + 1]


def bias(small, layer, which):
    return small[1][layer, which : which + 1]


def ff_bias_row(small, layer):
    return small[2][layer : layer + 1]


def qv_bias(small, layer, which):
    return small[3][layer, which : which + 1]


def column_sum(values_in):
    return jnp.sum(values_in, axis=0, keepdims=True)


def gelu_pair(pre_act):
    inner = gelu_c * (pre_act + 0.044715 * pre_act * pre_act * pre_act)
    tanh_v = jnp.tanh(inner)
    value_out = 0.5 * pre_act * (1.0 + tanh_v)
    slope = 0.5 * (1.0 + tanh_v) + 0.5 * pre_act * (1.0 - tanh_v * tanh_v) * gelu_c * (
        1.0 + 3.0 * 0.044715 * pre_act * pre_act
    )
    return (value_out, slope)


def joined(own_ref, other_ref):
    high = (lax.axis_index("tensor") & 1) == 1
    own, other = own_ref[...].astype(f32), other_ref[...].astype(f32)
    return jnp.concatenate(
        [jnp.where(high, other, own), jnp.where(high, own, other)], axis=0
    )


def split_halves(total, keep_ref, give_ref):
    half = total.shape[0] // 2
    high = (lax.axis_index("tensor") & 1) == 1
    low_rows, high_rows = total[:half], total[half:]
    keep_ref[...] = jnp.where(high, high_rows, low_rows)
    give_ref[...] = jnp.where(high, low_rows, high_rows).astype(bf16)


def place_pieces(pieces, out_ref):
    mine = lax.axis_index("tensor")
    rows = pieces[0].shape[0]
    for number, piece in enumerate(pieces):
        start = pl.multiple_of((mine ^ number) * rows, rows)
        out_ref[pl.ds(start, rows), :] = piece[...].astype(out_ref.dtype)


def gathered(piece):
    pieces = {0: piece}
    for bit in bits_of("tensor")[::-1]:
        for number in list(pieces):
            pieces[number ^ bit] = swapped(pieces[number], "tensor", bit)
    return [pieces[number] for number in range(len(pieces))]


def after(value, *others):
    return lax.optimization_barrier((value, *others))[0]


def exchanged(keep, give, launch=None, due=()):
    bits = bits_of("tensor")
    total = keep + swapped(give, "tensor", bits[0]).astype(f32)
    for bit in bits[1:]:
        rounded = after(total.astype(bf16), *due)
        other = swapped(rounded, "tensor", bit)
        if launch is not None and bit == bits[-1]:
            launch(rounded)
        total = rounded.astype(f32) + other.astype(f32)
    rounded = total.astype(bf16)
    return [rounded, swapped(rounded, "tensor", bits[0])]


def project_rows(hidden, layer, refs, outs):
    small, w_qkv = refs[:4], refs[4]
    h_ref, picked_ref, q_ref, kv_ref = outs
    width = q_ref.shape[1]
    hat, _ = normalize(hidden)
    act = (hat * gain(small, layer, 0) + bias(small, layer, 0)).astype(bf16)
    kv = mm(act, w_qkv[layer, width:], NT)
    values = kv[:, width:] + qv_bias(small, layer, 1)
    kv_ref[...] = jnp.concatenate([kv[:, :width], values], axis=1).astype(bf16)
    query = mm(act, w_qkv[layer, :width], NT)
    q_ref[...] = (query + qv_bias(small, layer, 0)).astype(bf16)
    half = act.shape[1] // 2
    picked_ref[:, :half], picked_ref[:, half:] = picked_halves(act)


def project_first(tokens, pieces, params):
    count = len(pieces)
    own_rows = tokens.shape[0]
    rows = (count + 1) * own_rows
    width = params["w_out"].shape[1]
    gains, biases, _, qv = params["small"]
    far = [tokens, gains, biases, qv, params["w_qkv"]]
    many = len(far)

    def kernel(*refs):
        ins, near = refs[:count], refs[count : count + many]
        outs = refs[-4:]
        place_pieces([near[0], *ins], outs[0])
        small = (near[1], near[2], None, near[3])
        project_rows(outs[0][...], 0, [*small, near[4]], outs)

    def whole(array):
        zeros = (0,) * array.ndim
        return pl.BlockSpec(array.shape, lambda step: zeros)

    spec = pl.BlockSpec(memory_space=pltpu.VMEM)
    return pl.pallas_call(
        kernel,
        grid=(1,),
        out_shape=[
            jax.ShapeDtypeStruct((rows, D), f32),
            jax.ShapeDtypeStruct((rows, D), bf16),
            jax.ShapeDtypeStruct((rows, width), bf16),
            jax.ShapeDtypeStruct((rows, 2 * width), bf16),
        ],
        in_specs=[spec] * count
        + [whole(a) for a in far[:-1]]
        + [pl.BlockSpec((1,) + far[-1].shape[1:], lambda step: (0, 0, 0))],
        out_specs=[spec] * 4,
        compiler_params=pltpu.CompilerParams(vmem_limit_bytes=VMEM_LIMIT),
        cost_estimate=pl.CostEstimate(flops=1, bytes_accessed=1, transcendentals=0),
    )(*pieces, *far)


def project_next(mid, pair, layer, params):
    rows = mid.shape[0]
    width = params["w_out"].shape[1]

    def kernel(mid_ref, own_ref, other_ref, *refs):
        ins, outs = refs[:5], refs[5:]
        hidden = mid_ref[...] + joined(own_ref, other_ref) + bias(ins, layer - 1, 3)
        outs[0][...] = hidden
        project_rows(hidden, layer, ins, outs)

    return call(
        kernel,
        [((rows, D), f32), ((rows, D), bf16), ((rows, width), bf16), ((rows, 2 * width), bf16)],
        [mid, *pair, *params["small"], params["w_qkv"]],
    )


def head_lanes(shape, head):
    lane = lax.broadcasted_iota(jnp.int32, shape, 1)
    return (lane >= head * HD) & (lane < (head + 1) * HD)


def allowed_rows(segments, rows):
    def kernel(seg_ref, out_ref):
        mine = lax.axis_index("dp")
        here = seg_ref[:, pl.ds(pl.multiple_of(mine * rows, rows), rows)].astype(f32)
        query_seg = jnp.broadcast_to(here, (rows, rows)).T
        query = lax.broadcasted_iota(jnp.int32, (rows, rows), 0)
        key = lax.broadcasted_iota(jnp.int32, (rows, rows), 1)
        for place in range(SPAN):
            behind = SPAN - 1 - place
            start = jnp.maximum(mine - behind, 0) * rows
            key_seg = seg_ref[:, pl.ds(pl.multiple_of(start, rows), rows)].astype(f32)
            same = (query_seg == key_seg) & (key <= query + behind * rows)
            seen = jnp.where(same, 1.0, 0.0) * jnp.where(mine >= behind, 1.0, 0.0)
            out_ref[:, place * rows : (place + 1) * rows] = seen

    row = segments[None, :]
    return call(kernel, [((rows, SPAN * rows), f32)], [row], 1e10, 1e8)[0]


def split_shapes(rows):
    return [((rows // 2, D), f32), ((rows // 2, D), bf16)]


def attend(q, kv_parts, mask, picked1, layer, params):
    rows, width = q.shape
    half = D // 2
    pad = -(half + width) % 128
    heads = width // HD

    def kernel(q_ref, *refs):
        kv_refs, refs = refs[:SPAN], refs[SPAN:]
        mask_ref, w_out, p1_ref, att_ref, lse_ref, sent_ref, keep_ref, give_ref = refs
        allowed = mask_ref[...] > 0.0
        kv_all = jnp.concatenate([r[...] for r in kv_refs], axis=0)
        keys, values = kv_all[:, :width], kv_all[:, width:]
        query = q_ref[...]
        mixed = jnp.zeros((rows, width), f32)
        logs = jnp.zeros((rows, 128), f32)
        lane = lax.broadcasted_iota(jnp.int32, (rows, 128), 1)
        for head in range(heads):
            inside = head_lanes((rows, width), head)
            scores = mm(jnp.where(inside, query, 0), keys, NT) * HD ** (-0.5)
            scores = jnp.where(allowed, scores, -1e30)
            top = jnp.max(scores, axis=-1, keepdims=True)
            log_total = top + jnp.log(jnp.sum(jnp.exp(scores - top), axis=-1, keepdims=True))
            weights = jnp.exp(scores - log_total).astype(bf16)
            mixed = jnp.where(inside, mm(weights, values), mixed)
            logs = jnp.where(lane == head, log_total, logs)
        att = mixed.astype(bf16)
        att_ref[...] = att
        sent_ref[:, :half] = p1_ref[:, half:]
        sent_ref[:, half : half + width] = att
        if pad:
            sent_ref[:, half + width :] = jnp.zeros((rows, pad), bf16)
        lse_ref[...] = logs
        split_halves(mm(att, w_out[layer]), keep_ref, give_ref)

    return call(
        kernel,
        [((rows, width), bf16), ((rows, 128), f32), ((rows, half + width + pad), bf16)]
        + split_shapes(rows),
        [q, *kv_parts, mask, params["w_out"], picked1],
    )


def feed_forward(hidden, pair, layer, params):
    rows = hidden.shape[0]
    half = D // 2
    inner = params["w_up"].shape[2]

    def kernel(h_ref, own_ref, other_ref, g_ref, b_ref, f_ref, q_ref, up, down,
               mid_ref, slope_ref, sent_ref, kept_ref, keep_ref, give_ref):
        small = (g_ref, b_ref, f_ref, q_ref)
        mid = h_ref[...] + joined(own_ref, other_ref) + bias(small, layer, 1)
        mid_ref[...] = mid
        hat, _ = normalize(mid)
        act2 = (hat * gain(small, layer, 1) + bias(small, layer, 2)).astype(bf16)
        pre = mm(act2, up[layer]) + ff_bias_row(small, layer)
        value, slope = gelu_pair(pre)
        act3 = value.astype(bf16)
        split_halves(mm(act3, down[layer]), keep_ref, give_ref)
        slope_ref[...] = slope
        kept_ref[...], sent_ref[:, :half] = picked_halves(act2)
        sent_ref[:, half:] = act3

    return call(
        kernel,
        [
            ((rows, D), f32),
            ((rows, inner), f32),
            ((rows, half + inner), bf16),
            ((rows, half), bf16),
        ]
        + split_shapes(rows),
        [hidden, *pair]
        + [*params["small"], params["w_up"], params["w_down"]],
    )


def last_rows(mid, pair, params, own_rows):
    def kernel(mid_ref, own_ref, other_ref, biases, out_ref, all_ref):
        own = mid_ref.shape[0] // 2
        total = mid_ref[...] + joined(own_ref.at[own:], other_ref.at[own:])
        all_ref[...] = total + biases[LAYERS - 1, 3:4]
        start = pl.multiple_of(lax.axis_index("tensor") * own_rows, own_rows)
        out_ref[...] = all_ref[pl.ds(start, own_rows), :].astype(bf16)

    args = [mid, *pair, params["small"][1]]
    return call(kernel, [((own_rows, D), bf16), (mid.shape, f32)], args)[0]


def norm1_grad(gmid_ref, own_ref, other_ref, h_ref, gains, layer):
    d_norm = joined(own_ref, other_ref)
    hat, rstd = normalize(h_ref[...])
    grad = gmid_ref[...] + norm_bwd(d_norm, hat, rstd, gains[layer, 0:1])
    return grad, column_sum(d_norm * hat), column_sum(d_norm)


def mlp_grad(grad, layer, refs, outs):
    slope_ref, up, down = refs
    sent_ref, small_ref, kept_ref, keep_ref, give_ref = outs
    half = D // 2
    grad_b = grad.astype(bf16)
    d_pre = mm(grad_b, down[layer], NT) * slope_ref[...]
    pre_b = d_pre.astype(bf16)
    split_halves(mm(pre_b, up[layer], NT), keep_ref, give_ref)
    kept_ref[...], sent_ref[:, :half] = picked_halves(grad_b)
    sent_ref[:, half:] = pre_b
    small_ref[0:1, :] = column_sum(d_pre)
    small_ref[1:2, :] = column_sum(grad)


def mlp_outs(rows, inner):
    assert inner == D
    return [
        ((rows, D), f32),
        ((rows, D // 2 + inner), bf16),
        ((8, D), f32),
        ((rows, D // 2), bf16),
    ] + split_shapes(rows)


def mlp_grad_last(pieces, slope, params):
    count = len(pieces)
    rows, inner = slope.shape

    def kernel(*refs):
        ins, outs = refs[: count + 3], refs[count + 3 :]
        place_pieces(ins[:count], outs[0])
        outs[2][...] = jnp.zeros((8, D), f32)
        mlp_grad(outs[0][...], LAYERS - 1, ins[count:], outs[1:])

    return call(
        kernel,
        mlp_outs(rows, inner),
        [*pieces, slope, params["w_up"], params["w_down"]],
    )


def mlp_grad_next(gmid, pair, hidden, slope, layer, params):
    rows, inner = slope.shape

    def kernel(gmid_ref, own_ref, other_ref, h_ref, gains, *refs):
        ins, outs = refs[:3], refs[3:]
        grad, g_gain, g_bias = norm1_grad(gmid_ref, own_ref, other_ref, h_ref, gains, layer + 1)
        outs[0][...] = grad
        outs[2][...] = jnp.zeros((8, D), f32)
        mlp_grad(grad, layer, ins, outs[1:])
        outs[2][2:3, :] = g_gain
        outs[2][3:4, :] = g_bias

    return call(
        kernel,
        mlp_outs(rows, inner),
        [gmid, *pair, hidden, params["small"][0], slope, params["w_up"], params["w_down"]],
    )


def attend_grad(grad, pair, mid, q, kv_parts, mask, att, lse, layer, params):
    rows, width = q.shape
    heads = width // HD
    back = SPAN - 1

    def kernel(g_ref, own_ref, other_ref, mid_ref, q_ref, *refs):
        kv_refs, refs = refs[:SPAN], refs[SPAN:]
        mask_ref, att_ref, lse_ref, gains, w_out = refs[:5]
        gmid_ref, picked_ref, dq_ref, dkv_ref, small_ref = refs[5:10]
        away_refs = refs[10:]
        d_norm = joined(own_ref, other_ref)
        hat, rstd = normalize(mid_ref[...])
        gmid = g_ref[...] + norm_bwd(d_norm, hat, rstd, gains[layer, 1:2])
        gmid_ref[...] = gmid
        mid_b = gmid.astype(bf16)
        d_att = mm(mid_b, w_out[layer], NT).astype(bf16)
        allowed = mask_ref[...] > 0.0
        kv_all = jnp.concatenate([r[...] for r in kv_refs], axis=0)
        keys, values = kv_all[:, :width], kv_all[:, width:]
        query, logs = q_ref[...], lse_ref[...]
        weighed = d_att.astype(f32) * att_ref[...].astype(f32)
        d_query = jnp.zeros((rows, width), f32)
        d_keys = jnp.zeros((SPAN * rows, width), f32)
        d_values = jnp.zeros((SPAN * rows, width), f32)
        for head in range(heads):
            inside = head_lanes((rows, width), head)
            query_h = jnp.where(inside, query, 0)
            d_att_h = jnp.where(inside, d_att, 0)
            scores = mm(query_h, keys, NT) * HD ** (-0.5)
            scores = jnp.where(allowed, scores, -1e30)
            probs = jnp.exp(scores - logs[:, head : head + 1])
            delta = jnp.sum(jnp.where(inside, weighed, 0.0), axis=-1, keepdims=True)
            d_prob = mm(d_att_h, values, NT)
            d_score = (probs * (d_prob - delta) * HD ** (-0.5)).astype(bf16)
            d_query = jnp.where(inside, mm(d_score, keys), d_query)
            d_keys = d_keys + mm(d_score, query_h, TN)
            d_values = d_values + mm(probs.astype(bf16), d_att_h, TN)
        d_kv = jnp.concatenate([d_keys, d_values], axis=1)
        dq_ref[...] = d_query
        dkv_ref[...] = d_kv[back * rows :]
        for distance in range(1, SPAN):
            block = back - distance
            away_refs[distance - 1][...] = d_kv[block * rows : (block + 1) * rows].astype(bf16)
        half = D // 2
        picked_ref[:, :half], picked_ref[:, half:] = picked_halves(mid_b)
        small_ref[...] = jnp.zeros((8, D), f32)
        small_ref[0:1, :] = column_sum(d_norm * hat)
        small_ref[1:2, :] = column_sum(d_norm)
        small_ref[2:3, :] = column_sum(gmid)

    return call(
        kernel,
        [
            ((rows, D), f32),
            ((rows, D), bf16),
            ((rows, width), f32),
            ((rows, 2 * width), f32),
            ((8, D), f32),
        ]
        + [((rows, 2 * width), bf16)] * back,
        [grad, *pair, mid, q, *kv_parts, mask, att, lse]
        + [params["small"][0], params["w_out"]],
    )


def project_grad(dq, dkv, arrived, picked, layer, params, more=()):
    rows, width = dq.shape
    half = D // 2
    pad = -(half + 3 * width) % 128

    def kernel(dq_ref, dkv_ref, *refs):
        near, refs = refs[: SPAN - 1], refs[SPAN - 1 :]
        picked_ref, w_qkv = refs[:2]
        sent_ref, small_ref, keep_ref, give_ref = refs[-4:]
        d_kv = dkv_ref[...]
        for ref in near:
            d_kv = d_kv + ref[...].astype(f32)
        d_query = dq_ref[...]
        query_b, kv_b = d_query.astype(bf16), d_kv.astype(bf16)
        part = mm(kv_b, w_qkv[layer, width:]) + mm(query_b, w_qkv[layer, :width])
        own = rows // 2
        split_halves(part, keep_ref.at[:own], give_ref.at[:own])
        for ref, source in zip((keep_ref, give_ref), refs[2:-4]):
            ref[own:, :] = source[...]
        sent_ref[:, :half] = picked_ref[:, half:]
        sent_ref[:, half : half + 2 * width] = kv_b
        sent_ref[:, half + 2 * width : half + 3 * width] = query_b
        if pad:
            sent_ref[:, half + 3 * width :] = jnp.zeros((rows, pad), bf16)
        small_ref[...] = jnp.zeros((8, D), f32)
        small_ref[0:1, :width] = column_sum(d_query)
        small_ref[1:2, :width] = column_sum(d_kv)[:, width:]

    return call(
        kernel,
        [((rows, half + 3 * width + pad), bf16), ((8, D), f32)]
        + split_shapes(rows * (2 if more else 1)),
        [dq, dkv, *arrived, picked, params["w_qkv"], *more],
    )


def small_rows(count):
    rows = 8 * LAYERS + LAYERS * count
    return rows + -rows % 8


def local_small(keep, give, hidden, mlp_small, att_small, qv_small, count, width):
    share = 1.0 / count

    def kernel(keep_ref, give_ref, h_ref, *refs):
        mlp, att, qv, out = refs[:LAYERS], refs[LAYERS : 2 * LAYERS], refs[2 * LAYERS : -1], refs[-1]
        mine = lax.axis_index("tensor")
        own = h_ref.shape[0] // 2
        part = joined(keep_ref.at[:own], give_ref.at[:own])
        hat, _ = normalize(h_ref[...])
        out[...] = jnp.zeros(out.shape, f32)
        for layer in range(LAYERS):
            gain1 = column_sum(part * hat) if layer == 0 else mlp[layer - 1][2:3, :] * share
            bias1 = column_sum(part) if layer == 0 else mlp[layer - 1][3:4, :] * share
            at = 2 * layer
            out[at : at + 1, :] = gain1
            out[at + 1 : at + 2, :] = att[layer][0:1, :] * share
            at = 2 * LAYERS + 4 * layer
            out[at : at + 1, :] = bias1
            out[at + 1 : at + 2, :] = att[layer][2:3, :] * share
            out[at + 2 : at + 3, :] = att[layer][1:2, :] * share
            out[at + 3 : at + 4, :] = mlp[layer][1:2, :] * share
            for target in range(count):
                here = mine == target
                at = 6 * LAYERS + 2 * layer
                lanes = slice(target * width, (target + 1) * width)
                out[at : at + 2, lanes] = jnp.where(here, qv[layer][0:2, :width], 0.0)
                at = 8 * LAYERS + layer * count + target
                out[at : at + 1, :] = jnp.where(here, mlp[layer][0:1, :], 0.0)

    args = [keep, give, hidden, *mlp_small, *att_small, *qv_small]
    return call(kernel, [((small_rows(count), D), f32)], args)[0]


def first_grad(gmid, pair, hidden, params, own_rows):
    def kernel(gmid_ref, own_ref, other_ref, h_ref, gains, in_ref, g_ref):
        own = h_ref.shape[0] // 2
        near, away = own_ref.at[:own], other_ref.at[:own]
        g_ref[...] = norm1_grad(gmid_ref, near, away, h_ref, gains, 0)[0]
        start = pl.multiple_of(lax.axis_index("tensor") * own_rows, own_rows)
        in_ref[...] = g_ref[pl.ds(start, own_rows), :].astype(bf16)

    args = [gmid, *pair, hidden, params["small"][0]]
    return call(kernel, [((own_rows, D), bf16), (gmid.shape, f32)], args)[0]


def small_outs(total, other, count):
    def kernel(total_ref, other_ref, gains, biases, qv, ffb):
        both = total_ref[...] + other_ref[...]
        for layer in range(LAYERS):
            gains[layer] = both[2 * layer : 2 * layer + 2]
            at = 2 * LAYERS + 4 * layer
            biases[layer] = both[at : at + 4]
            at = 6 * LAYERS + 2 * layer
            qv[layer] = both[at : at + 2]
            for target in range(count):
                at = 8 * LAYERS + layer * count + target
                ffb[layer : layer + 1, target * D : (target + 1) * D] = both[at : at + 1]

    return call(
        kernel,
        [
            ((LAYERS, 2, D), f32),
            ((LAYERS, 4, D), f32),
            ((LAYERS, 2, D), f32),
            ((LAYERS, count * D), f32),
        ],
        [total, other],
    )


def split_rows(total, bit, block, send_ref, keep_ref):
    mine = lax.axis_index("dp")
    high = jnp.where((mine & bit) != 0, 1, 0)
    pairs = total.shape[0] // (2 * block)
    for pair in range(pairs):
        for which in range(2):
            rows = total[(2 * pair + which) * block : (2 * pair + which + 1) * block]
            out = slice(pair * block, (pair + 1) * block)

            @pl.when(high == which)
            def _():
                keep_ref[out, :] = rows

            @pl.when(high != which)
            def _():
                send_ref[out, :] = rows.astype(bf16)


def split_plain(total, bit, block):
    pairs = total.shape[0] // (2 * block)
    split = total.reshape(pairs, 2, block, total.shape[1])
    high = jnp.where((lax.axis_index("dp") & bit) != 0, 1, 0)
    send = lax.dynamic_index_in_dim(split, 1 - high, 1, keepdims=False)
    keep = lax.dynamic_index_in_dim(split, high, 1, keepdims=False)
    return send.reshape(-1, total.shape[1]).astype(bf16), keep.reshape(-1, total.shape[1])


class Halving:
    def __init__(self, products, wide):
        self.products, self.wide = products, wide
        self.bits = [bit for bit in bits_of("dp") if bit != lax.axis_size("dp") // 4]
        self.block = D // lax.axis_size("dp")
        self.place = 0

    def begin(self, sources):
        half = D // 2
        flat = [array for source in sources for array in source]
        shape = (half // 2, self.wide)
        spots = self.products

        def products_of(refs):
            done = []
            for (la, kept_at, sent_at), (ra, r0, r1) in spots:
                kept = refs[3 * la + 2][:, kept_at : kept_at + half]
                given = refs[3 * la + 1][:, sent_at : sent_at + half]
                left = jnp.concatenate([kept, given], axis=0)
                right = [refs[3 * ra][:, r0:r1], refs[3 * ra + 1][:, r0:r1]]
                done.append(mm(left, jnp.concatenate(right, axis=0), TN))
            return jnp.concatenate(done, axis=1)

        bit, block, count = self.bits[0], self.block, len(flat)
        if block % 16:

            def kernel(*refs):
                refs[count][...] = products_of(refs)

            total = call(kernel, [((half, self.wide), f32)], flat)[0]
            self.send, self.keep = split_plain(total, bit, block)
        else:

            def kernel(*refs):
                split_rows(products_of(refs), bit, block, refs[count], refs[count + 1])

            self.send, self.keep = call(kernel, [(shape, bf16), (shape, f32)], flat)

    def launch(self, *gates):
        send = after(self.send, *gates) if gates else self.send
        self.arrived = swapped(send, "dp", self.bits[self.place])

    def absorb(self):
        self.place += 1
        bit, block = self.bits[self.place], self.block
        if block % 16:
            total = self.keep + self.arrived.astype(f32)
            self.send, self.keep = split_plain(total, bit, block)
            return

        def kernel(keep_ref, arrived_ref, send_ref, kept_ref):
            total = keep_ref[...] + arrived_ref[...].astype(f32)
            split_rows(total, bit, block, send_ref, kept_ref)

        shape = (self.keep.shape[0] // 2, self.wide)
        args = [self.keep, self.arrived]
        self.send, self.keep = call(kernel, [(shape, bf16), (shape, f32)], args)

    def finish(self):
        while self.place < len(self.bits) - 1:
            self.absorb()
            self.launch()
        return [self.keep, self.arrived]


def mlp_outputs(parts, block, inner):
    def kernel(*refs):
        up, down = refs[-2:]
        for layer in range(LAYERS):
            total = refs[2 * layer][...] + refs[2 * layer + 1][...].astype(f32)
            up[layer] = total[:, :inner]
            down[layer] = total[:, inner:]

    args = [a for pair in parts for a in pair]
    return call(kernel, [((LAYERS, block, inner), f32)] * 2, args)


def att_outputs(parts, block, width):
    def kernel(*refs):
        qkv, out = refs[-2:]
        for layer in range(LAYERS):
            total = refs[2 * layer][...] + refs[2 * layer + 1][...].astype(f32)
            qkv[layer, 0] = total[:, 2 * width : 3 * width]
            qkv[layer, 1] = total[:, :width]
            qkv[layer, 2] = total[:, width : 2 * width]
            out[layer] = total[:, 3 * width :].T

    args = [a for pair in parts for a in pair]
    return call(
        kernel,
        [((LAYERS, 3, block, width), f32), ((LAYERS, width, block), f32)],
        args,
    )


def shards(
    tokens, cotangent, segments, w_qkv, qv_bias, w_out, w_up, w_down, ff_bias, gains, biases
):
    tensor_count = lax.axis_size("tensor")
    dp_count = lax.axis_size("dp")
    own_rows = tokens.shape[0]
    rows = own_rows * tensor_count
    width = w_out.shape[1]
    inner = w_up.shape[2]
    half = D // 2
    block = D // dp_count
    joint = w_qkv.transpose(0, 2, 3, 1).reshape(LAYERS, 3 * width, D)
    params = {
        "small": [gains, biases, ff_bias, qv_bias],
        "w_qkv": joint,
        "w_out": w_out,
        "w_up": w_up,
        "w_down": w_down,
    }
    mask = allowed_rows(segments, rows)
    near = dp_count // 4

    def paired(sent, kept, gate):
        return [sent, swapped(after(sent, gate), "dp", near), kept]

    mlp_work = [
        Halving([((0, 0, 0), (1, half, half + inner)), ((1, 0, 0), (0, half, half + inner))], 2 * inner)
        for _ in range(LAYERS)
    ]
    att_work = [
        Halving([((0, 0, 0), (1, half, half + 3 * width)), ((1, 0, 0), (0, half, half + width))], 4 * width)
        for _ in range(LAYERS)
    ]
    token_pieces = gathered(tokens)
    token_pieces[-1] = after(token_pieces[-1], mask)
    saved, rows_a, rows_b = [], [None] * LAYERS, [None] * LAYERS
    cot_pieces = None
    mid = pair = None
    for layer in range(LAYERS):
        if layer == 0:
            hidden, picked1, q, kv = project_first(tokens, token_pieces[1:], params)
        else:
            hidden, picked1, q, kv = project_next(mid, pair, layer, params)
        kv_parts = [shifted(kv, "dp", distance) for distance in range(SPAN - 1, 0, -1)] + [kv]
        if layer:
            q = after(q, rows_a[layer - 1][1], rows_b[layer - 1][1])
        att, lse, sent_a, keep, give = attend(q, kv_parts, mask, picked1, layer, params)

        def launch_a(gate):
            nonlocal cot_pieces
            rows_a[layer] = paired(sent_a, picked1, gate)
            if layer == 0:
                cot_pieces = gathered(after(cotangent, gate))

        pair = exchanged(keep, give, launch_a)
        if layer == LAYERS - 1:
            pair[0] = after(pair[0], rows_a[layer][1])
        mid, slope, sent_b, kept_b, keep, give = feed_forward(hidden, pair, layer, params)
        saved.append((hidden, q, kv_parts, att, lse, mid, slope))
        if layer < LAYERS - 1:

            def launch_b(gate):
                rows_b[layer] = paired(sent_b, kept_b, gate)

            pair = exchanged(keep, give, launch_b)
            pair[0] = after(pair[0], cot_pieces[-1])
    last_keep, last_give = keep, give

    mlp_small, att_small, qv_small = ([None] * LAYERS for _ in range(3))
    gmid = last_pair = None
    for layer in range(LAYERS - 1, -1, -1):
        last = layer == LAYERS - 1
        later = layer + 1
        hidden, q, kv_parts, att, lse, mid, slope = saved[layer]
        if last:
            grad, sent1, mlp_small[layer], kept1, keep, give = mlp_grad_last(
                cot_pieces, slope, params
            )
        else:
            grad, sent1, mlp_small[layer], kept1, keep, give = mlp_grad_next(
                gmid, pair, saved[layer + 1][0], slope, layer, params
            )
        rows_1 = None

        def launch_1(gate):
            nonlocal rows_1
            if last:
                rows_b[layer] = paired(sent_b, kept_b, gate)
            else:
                rows_1 = paired(sent1, kept1, gate)

        pair = exchanged(keep, give, launch_1)
        gmid, picked, dq, dkv, att_small[layer], *away = attend_grad(
            grad, pair, mid, q, kv_parts, mask, att, lse, layer, params
        )
        arrived = [shifted(away[by - 1], "dp", -by) for by in (SPAN - 1, *range(1, SPAN - 1))]
        due = []
        if last:
            due.append(rows_b[layer][1])
        else:
            mlp_work[layer].begin([rows_b[layer], rows_1])
            mlp_work[later].absorb()
            due += [mlp_work[layer].send, mlp_work[later].send, att_work[later].send]
        sent2, qv_small[layer], keep, give = project_grad(
            dq,
            after(dkv, *due),
            arrived,
            picked,
            layer,
            params,
            () if last else (last_keep, last_give),
        )
        rows_2 = None

        def launch_2(gate):
            nonlocal rows_2
            rows_2 = paired(sent2, picked, gate)

        if last:

            def launch_late(gate):
                nonlocal rows_1
                rows_1 = paired(sent1, kept1, gate)
                launch_2(gate)

            pair = exchanged(keep, give, launch_late)
            mlp_work[layer].begin([rows_b[layer], rows_1])
            mlp_work[layer].launch()
            att_work[layer].begin([rows_a[layer], rows_2])
    small = local_small(
        keep, give, saved[0][0], mlp_small, att_small, qv_small, tensor_count, width
    )
    rows_2 = [sent2, swapped(sent2, "dp", near), picked]
    mlp_work[1].launch()
    mlp_work[0].launch()
    bits, dp_bits = bits_of("tensor"), bits_of("dp")
    total = keep
    for place, bit in enumerate(bits):
        rounded = give if place == 0 else total.astype(bf16)
        other = swapped(rounded, "tensor", bit)
        total = (total if place == 0 else rounded.astype(f32)) + other.astype(f32)
        small = small + swapped(small, "tensor", bit)
        total, small = lax.optimization_barrier((total, small))
    att_work[1].launch(total)
    small = small + swapped(small, "dp", dp_bits[-1])
    total = after(total, small, mlp_work[1].arrived, att_work[1].arrived)
    att_work[1].absorb()
    att_work[1].launch()
    rounded = total.astype(bf16)
    pair = [rounded, swapped(rounded, "tensor", bits[0])]
    input_grad = first_grad(gmid, pair, saved[0][0], params, own_rows)
    result = last_rows(saved[-1][5], pair, params, own_rows)
    rows_2[1] = after(rows_2[1], input_grad, result)
    att_work[0].begin([rows_a[0], rows_2])
    att_work[0].launch()
    mlp_work[0].arrived = after(mlp_work[0].arrived, att_work[0].send, att_work[1].arrived)
    mlp_work[0].absorb()
    mlp_work[0].launch()
    small = after(small, mlp_work[0].send)
    hops = dp_bits[:-1]
    for bit in hops[:-1]:
        small = small + swapped(small, "dp", bit)
    att_work[0].arrived = after(att_work[0].arrived, small)
    att_work[0].absorb()
    att_work[0].launch()
    small = after(small, att_work[0].send)
    small_grads = small_outs(small, swapped(small, "dp", hops[-1]), tensor_count)
    mlp_parts = [work.finish() for work in mlp_work]
    att_parts = [work.finish() for work in att_work]
    g_up, g_down = mlp_outputs(mlp_parts, block, inner)
    g_qkv, g_out = att_outputs(att_parts, block, width)
    return (
        result,
        input_grad,
        g_qkv.transpose(0, 2, 1, 3),
        g_out,
        g_up,
        g_down.transpose(0, 2, 1),
        *small_grads,
    )


def solution(mesh):
    return jax.shard_map(
        shards,
        mesh=mesh,
        in_specs=(
            P(("dp", "tensor"), None),
            P(("dp", "tensor"), None),
            P(),
            P(None, None, None, "tensor"),
            P(None, None, "tensor"),
            P(None, "tensor", None),
            P(None, None, "tensor"),
            P(None, "tensor", None),
            P(None, "tensor"),
            P(),
            P(),
        ),
        out_specs=(
            P(("dp", "tensor"), None),
            P(("dp", "tensor"), None),
            P(None, "dp", None, "tensor"),
            P(None, "tensor", "dp"),
            P(None, "dp", "tensor"),
            P(None, "tensor", "dp"),
            P(),
            P(),
            P(),
            P(),
        ),
        check_vma=False,
    )
```
